512 devices in a mesh: slab: 8 (over z_lo, x), dev: 64 (over z_hi, y, core).
Axes of the slice: x: 4, y: 8, z: 8 (z_hi: 4, z_lo: 2; z = z_hi * 2 + z_lo), core: 2. Of those that a mesh axis runs over, the one named last changes fastest.
Arguments:
- fine_input: bfloat16 [131072, 768], P(('slab', 'dev')), may hold values from -6 to 6
- merge_weight: bfloat16 [768, 192], replicated, may hold values from -0.21875 to 0.21875
- conv_weight: bfloat16 [5184, 192], P('dev'), may hold values from -0.078125 to 0.078125
- pre_act: bfloat16 [2048, 16, 768], P(('slab', 'dev')), may hold values from -6 to 6
- norm_gain: float32 [192], replicated, may hold values from 0.5 to 2
- norm_bias: float32 [192], replicated, may hold values from -3 to 3
- cotangent: bfloat16 [2048, 16, 768], P(('slab', 'dev')), may hold values from -6 to 6
- counts: int32 [512], replicated, may hold values from 2 to 4, as said below
- neighbours: int32 [2048, 27], P(('slab', 'dev')), may hold values from -1 to 2047, as said below
Outputs:
- fine_grad: bfloat16 [131072, 768], P(('slab', 'dev'))
- merge_grad: float32 [768, 192], replicated
- conv_grad: float32 [5184, 192], P('dev', 'slab')
The draws below stay inside these ranges and needn't reach their ends.
Inputs may be any that keep to these rules, and one draw needn't show every extreme that they name: `counts`: the first and the last device hold 4 live bricks, the second holds the fewest allowed. `neighbours`: global slot = device * 4 + local slot. Entry 13 of a live slot's row is the slot itself; every other entry is -1 or a live slot on the same device, on the device one before along dev in the same slab (then among its last 1 live slots), on the device one after along dev (then among its first 1 slots), or on the device of the same dev index in an adjacent slab. Rows of slots that are not alive are all -1.
All inputs are finite; a program needn't handle non-finite values.
Results may differ from the reference program's by a relative error of at most 0.0057.
Values may be sent and summed in bfloat16 or wider, within the bound.
No kernel may reach another device: no remote copies, remote signals or barrier semaphores. Data moves between devices by JAX's collectives and lax.ppermute only.
A program may use at most 64 MiB of HBM per device.

```python
import math
import jax
import jax.numpy as jnp
from jax import lax

CF = 96
C = 192
BRICK_DEV = 4
BRICKS = 2048
N_SLAB = 8
N_DEV = 64


def brick_counts(key):
    shared_key = jax.random.fold_in(key, 11)
    devices = N_SLAB * N_DEV
    fewest = BRICK_DEV - BRICK_DEV // 2
    drawn = jax.random.randint(shared_key, (devices,), fewest, BRICK_DEV + 1)
    return drawn.at[0].set(BRICK_DEV).at[1].set(fewest).at[devices - 1].set(BRICK_DEV)


def draw_counts(key, part):
    return brick_counts(key)


def draw_neighbours(key, part):
    counts = brick_counts(key)
    key = jax.random.fold_in(key, 5)
    devices = N_SLAB * N_DEV
    slot_total = devices * BRICK_DEV
    edge_size = BRICK_DEV // 4
    brick_ids = jnp.arange(slot_total, dtype=jnp.int32)
    owner_index = brick_ids // BRICK_DEV
    local_slot = brick_ids % BRICK_DEV
    slab_place = owner_index // N_DEV
    dev_place = owner_index % N_DEV
    alive = local_slot < counts[owner_index]
    kind_key, pick_key = jax.random.split(key)
    kinds = jax.random.randint(kind_key, (slot_total, 27), 0, 7)
    picks = jax.random.randint(pick_key, (slot_total, 27), 0, 1 << 20)
    owner_col = owner_index[:, None]
    shift_table = jnp.array([0, 0, 0, -1, 1, -N_DEV, N_DEV], dtype=jnp.int32)
    target_owner = owner_col + shift_table[kinds]
    valid = kinds > 0
    valid = valid & ((kinds != 3) | (dev_place[:, None] > 0))
    valid = valid & ((kinds != 4) | (dev_place[:, None] < N_DEV - 1))
    valid = valid & ((kinds != 5) | (slab_place[:, None] > 0))
    valid = valid & ((kinds != 6) | (slab_place[:, None] < N_SLAB - 1))
    safe_owner = jnp.clip(target_owner, 0, devices - 1)
    their_count = counts[safe_owner]
    chosen = jnp.where(kinds == 3, their_count - 1 - picks % edge_size, jnp.where(kinds == 4, picks % edge_size, picks % their_count))
    target = safe_owner * BRICK_DEV + chosen
    table = jnp.where(valid & alive[:, None], target, -1)
    centre = jnp.where(alive, brick_ids, -1)
    return table.at[:, 13].set(centre).astype(jnp.int32)


def steps_of(own_key, dims, cuts, least, top_value):
    gain = 1.0
    for dim, parts in cuts:
        draws = jax.random.uniform(jax.random.fold_in(jax.random.fold_in(own_key, 6), dim), (parts,), jnp.float32, least / len(cuts), top_value / len(cuts))
        gain = gain * jnp.repeat(jnp.exp(draws), dims[dim] // parts).reshape((-1,) + (1,) * (len(dims) - 1 - dim))
    return gain


def noise(stream_key, extent, spread, bound, shards=(), kind=jnp.bfloat16):
    level = steps_of(stream_key, extent, shards, -0.22, 0.18) if shards else 1.0
    result = jax.random.normal(stream_key, extent, jnp.float32) * spread * level
    return jnp.minimum(jnp.maximum(result, -bound), bound).astype(kind)


def setup_inputs(seed: int = 0) -> dict:
    arg_keys = jax.random.split(jax.random.key(seed), 10)
    fine_input = noise(arg_keys[0], (BRICKS * 64, 8 * CF), 1.0, 6.0, ((0, 512),))
    merge_weight = noise(arg_keys[1], (8 * CF, C), (8 * CF) ** -0.5, 0.21875)
    conv_weight = noise(arg_keys[2], (27 * C, C), (27 * C) ** -0.5, 0.078125, ((0, 64),))
    pre_act = noise(arg_keys[3], (BRICKS, 16, 4 * C), 1.0, 6.0, ((0, 512),))
    norm_gain = jnp.clip(jnp.exp(jax.random.uniform(arg_keys[4], (C,), jnp.float32, math.log(0.5), math.log(2.0))), 0.5, 2.0)
    norm_bias = noise(arg_keys[5], (C,), 0.7, 3.0, (), jnp.float32)
    cotangent = noise(arg_keys[6], (BRICKS, 16, 4 * C), 1.0, 6.0, ((0, 512),))
    counts = draw_counts(jax.random.fold_in(arg_keys[9], 71), 0)
    neighbours = draw_neighbours(jax.random.fold_in(arg_keys[9], 71), 0)
    return dict(fine_input=fine_input, merge_weight=merge_weight, conv_weight=conv_weight, pre_act=pre_act, norm_gain=norm_gain, norm_bias=norm_bias, cotangent=cotangent, counts=counts, neighbours=neighbours)


def unfold_taps(gathered, channels):
    bricks_here = gathered.shape[0]
    field = gathered.reshape(bricks_here, 3, 3, 3, 4, 4, 4, channels)
    field = jnp.transpose(field, (0, 1, 4, 2, 5, 3, 6, 7)).reshape(bricks_here, 12, 12, 12, channels)
    padded = field[:, 3:9, 3:9, 3:9, :]
    columns = []
    for tap_index in range(27):
        start_x = 2 - tap_index // 9
        start_y = 2 - (tap_index // 3) % 3
        start_z = 2 - tap_index % 3
        window = padded[:, start_x:start_x + 4, start_y:start_y + 4, start_z:start_z + 4, :]
        columns.append(window.reshape(bricks_here * 64, channels))
    return jnp.concatenate(columns, axis=1)


def reference(fine_input, merge_weight, conv_weight, pre_act, norm_gain, norm_bias, cotangent, counts, neighbours):
    channels = merge_weight.shape[1]
    devices = N_SLAB * N_DEV
    slot_ids = jnp.arange(BRICKS, dtype=jnp.int32)
    alive = (slot_ids % BRICK_DEV < counts[slot_ids // BRICK_DEV]).astype(jnp.float32)
    alive_rows = jnp.repeat(alive, 64)
    merged = jnp.dot(fine_input, merge_weight, preferred_element_type=jnp.float32)
    merged = (merged * alive_rows[:, None]).astype(jnp.bfloat16)
    saved_pre = pre_act.astype(jnp.float32).reshape(BRICKS, 64, channels)
    upstream = cotangent.astype(jnp.float32).reshape(BRICKS, 64, channels)
    open_gate = (norm_gain * saved_pre + norm_bias > 0).astype(jnp.float32)
    grad_pre = (upstream * norm_gain * open_gate * alive[:, None, None]).astype(jnp.bfloat16)
    grad_pre = grad_pre.reshape(BRICKS, 16, 4 * channels)
    with_zero = jnp.concatenate([grad_pre, jnp.zeros((1, 16, 4 * channels), grad_pre.dtype)], axis=0)
    table = jnp.where(neighbours < 0, BRICKS, neighbours).astype(jnp.int32)
    table_blocks = table.reshape(devices, BRICK_DEV, 27)
    merged_blocks = merged.reshape(devices, BRICK_DEV * 64, channels)

    def one_block(carry, inputs):
        block_table, block_merged = inputs
        gathered = jnp.take(with_zero, block_table.reshape(-1), axis=0).reshape(BRICK_DEV, 27, 16, 4 * channels)
        tap_matrix = unfold_taps(gathered, channels)
        backward = jnp.dot(tap_matrix, conv_weight, preferred_element_type=jnp.float32)
        carry = carry + lax.dot_general(tap_matrix, block_merged, (((0,), (0,)), ((), ())), preferred_element_type=jnp.float32)
        return carry, backward

    conv_grad, backward = lax.scan(one_block, jnp.zeros((27 * channels, channels), jnp.float32), (table_blocks, merged_blocks))
    backward = backward.reshape(BRICKS * 64, channels)
    grad_merged = (backward * alive_rows[:, None]).astype(jnp.bfloat16)
    fine_grad = lax.dot_general(grad_merged, merge_weight, (((1,), (1,)), ((), ())), preferred_element_type=jnp.float32).astype(jnp.bfloat16)
    merge_grad = lax.dot_general(fine_input, grad_merged, (((0,), (0,)), ((), ())), preferred_element_type=jnp.float32)
    return fine_grad, merge_grad, conv_grad
```

```python
import functools

import numpy as np
import jax
import jax.numpy as jnp
from jax import lax
from jax.experimental import pallas as pl
from jax.experimental.pallas import tpu as pltpu
from jax.sharding import Mesh, PartitionSpec as P

F32 = jnp.float32
BF16 = jnp.bfloat16

AXES = ("zl", "x", "zh", "y", "c")
SIZES = (2, 4, 4, 8, 2)
SLAB = ("zl", "x")
DEV = ("zh", "y", "c")
SLABS = 8
DEVS = 64
B = 4
C = 192
ROWS = 81
FRAME = 96
HALF = 32 * ROWS
COLS = C // SLABS

SMEM = pl.BlockSpec(memory_space=pltpu.SMEM)
VMEM = pl.BlockSpec(memory_space=pltpu.VMEM)


def dot(a, b):
    return jnp.dot(a, b, preferred_element_type=F32)


def my_place():
    place = lax.axis_index(AXES[0])
    for axis, size in zip(AXES[1:], SIZES[1:]):
        place = place * size + lax.axis_index(axis)
    return place


def window_matrix():
    out = np.zeros((144, 144), np.float32)
    where = [(0, 3), (1, 0), (1, 1), (1, 2), (1, 3), (2, 0)]
    for sx in range(3):
        for sy in range(3):
            for vx in range(4):
                for vy in range(4):
                    kx, x = where[sx + vx]
                    ky, y = where[sy + vy]
                    out[(sx * 3 + sy) * 16 + vx * 4 + vy, (kx * 3 + ky) * 16 + x * 4 + y] = 1
    return out


def row_order():
    out = np.zeros((256, 256), np.float32)
    for z in range(4):
        for b in range(B):
            for xy in range(16):
                out[(z * B + b) * 16 + xy, (b * 16 + xy) * 4 + z] = 1
    return out


def tap_rows(tap):
    window = (2 - tap // 9) * 3 + 2 - tap // 3 % 3
    return (window * 6 + 2 - tap % 3) * 64


def prepare_kernel(counts, pre, cot, gain, bias, weight, grad, first, last, frames):
    place = my_place()
    count = counts[place]
    g = gain[...]
    for b in range(B):
        p = pre[b].astype(F32)
        u = cot[b].astype(F32)
        for z in range(4):
            pz = p[:, z * C : (z + 1) * C]
            uz = u[:, z * C : (z + 1) * C]
            gate = (g * pz + bias[...] > 0) & (b < count)
            grad[b, z] = jnp.where(gate, uz * g, 0.0).astype(BF16)
    first[0] = grad[0]
    last[0] = grad[count - 1]
    shift = lax.rem(place, 16)
    rows = lax.broadcasted_iota(jnp.int32, (FRAME, ROWS), 0)
    cols = lax.broadcasted_iota(jnp.int32, (FRAME, ROWS), 1)
    spread = jnp.where(rows == cols + shift, 1.0, 0.0).astype(BF16)
    frame = dot(spread, weight[...])
    main = frame[:, :128].astype(BF16)
    low = frame[:48, 128:].astype(BF16)
    high = frame[48:, 128:].astype(BF16)
    tail = jnp.concatenate([low, high], axis=1)
    for y in range(8):
        frames[y, :FRAME] = main
        frames[y, FRAME:] = tail


def conv_kernel(
    counts, near, grad, slab_low, slab_high, dev_low, dev_high, fine, weight, windows, order,
    conv, taps, bricks, block, total,
):
    place = my_place()
    count = counts[place]
    bricks[0:4] = grad[...]
    bricks[4:8] = slab_low[...]
    bricks[8:12] = slab_high[...]
    bricks[12:13] = dev_low[...]
    bricks[13:14] = dev_high[...]
    bricks[14:15] = jnp.zeros((1, 4, 16, C), BF16)
    window = windows[...]
    for b in range(B):
        slots = []
        for k in range(27):
            brick = near[b, k]
            away = lax.shift_right_arithmetic(brick, 2) - place
            slot = jnp.bitwise_and(brick, 3)
            at = jnp.where(away == 0, slot, 14)
            at = jnp.where(away == -DEVS, 4 + slot, at)
            at = jnp.where(away == DEVS, 8 + slot, at)
            at = jnp.where(away == -1, 12, at)
            at = jnp.where(away == 1, 13, at)
            slots.append(jnp.where(brick < 0, 14, at))
        for plane in range(6):
            kz, z = ((0, 3), (1, 0), (1, 1), (1, 2), (1, 3), (2, 0))[plane]
            for q in range(9):
                block[plane, q * 16 : (q + 1) * 16] = bricks[slots[q * 3 + kz], z]
        for plane in range(6):
            moved = dot(window, block[plane]).astype(BF16)
            for s in range(9):
                row = ((s * 6 + plane) * B + b) * 16
                taps[row : row + 16] = moved[s * 16 : (s + 1) * 16]
    merged = dot(fine[...], weight[...])
    brick_of = lax.broadcasted_iota(jnp.int32, (256, C), 0) // 64
    merged = jnp.where(brick_of < count, merged, 0.0).astype(BF16)
    merged = jnp.transpose(dot(order[...], merged)).astype(BF16)
    for tap in range(27):
        row = tap_rows(tap)
        term = dot(merged, taps[row : row + 256])
        at = tap * C
        end = at + C
        while at < end:
            owner = at // ROWS
            stop = min(end, (owner + 1) * ROWS)
            to = (owner // 2) * ROWS + at % ROWS
            total[owner % 2, :, to : to + stop - at] = term[:, at - tap * C : stop - tap * C]
            at = stop
    for half in range(2):
        conv[half] = total[half].astype(BF16)


def back_kernel(counts, frames, taps, fine, weight, order, back_order, fine_grad, term, whole):
    place = my_place()
    count = counts[place]
    for owner in range(DEVS):
        tile = ROWS * owner // 16
        frame = frames.at[owner % 2, owner // 16, owner // 2 % 8]
        main = frame[:FRAME]
        low = frame[FRAME:, :64]
        high = frame[FRAME:, 64:]
        row = tile * 16
        if owner % 16:
            whole[row : row + 16, :128] = whole[row : row + 16, :128] + main[:16]
            whole[row : row + 16, 128:] = whole[row : row + 16, 128:] + low[:16]
            whole[row + 16 : row + FRAME, :128] = main[16:]
            whole[row + 16 : row + 48, 128:] = low[16:]
        else:
            whole[row : row + FRAME, :128] = main
            whole[row : row + 48, 128:] = low
        whole[row + 48 : row + FRAME, 128:] = high
    back = jnp.zeros((256, C), F32)
    for tap in range(27):
        row = tap_rows(tap)
        back = back + dot(taps[row : row + 256], whole[tap * C : (tap + 1) * C])
    brick_of = lax.broadcasted_iota(jnp.int32, (256, C), 0) // 16 % B
    back = jnp.where(brick_of < count, back, 0.0).astype(BF16)
    back = dot(back_order[...], back)
    gm = back.astype(BF16)
    fine_grad[...] = lax.dot_general(
        gm, weight[...], (((1,), (1,)), ((), ())), preferred_element_type=F32
    ).astype(BF16)
    result = dot(jnp.transpose(back).astype(BF16), fine[...]).astype(BF16)
    for half in range(2):
        for part in range(6):
            term[half, part * 96 : (part + 1) * 96] = result[
                half * 96 : (half + 1) * 96, part * 128 : (part + 1) * 128
            ]


def cut_kernel(parts, out):
    total = parts[0].astype(F32)
    for i in range(1, SLABS):
        total = total + parts[i].astype(F32)
    for i in range(32):
        out[i] = total[:, i * ROWS : (i + 1) * ROWS].astype(BF16)


def merge_kernel(parts, out):
    for part in range(6):
        block = [parts[half, part * 96 : (part + 1) * 96].astype(F32) for half in range(2)]
        out[part * 128 : (part + 1) * 128] = jnp.transpose(jnp.concatenate(block, axis=0))


def call(kernel, outs, specs, scratch=(), flops=0, moved=0):
    return pl.pallas_call(
        kernel,
        out_shape=outs,
        in_specs=specs,
        out_specs=jax.tree.map(lambda _: VMEM, outs),
        scratch_shapes=scratch,
        cost_estimate=pl.CostEstimate(flops=flops, bytes_accessed=moved, transcendentals=0),
        compiler_params=pltpu.CompilerParams(vmem_limit_bytes=40 << 20),
    )


def shape(*dims, dtype=BF16):
    return jax.ShapeDtypeStruct(dims, dtype)


def swap(x, axes):
    return lax.all_to_all(x, axes, 0, 0, tiled=True)


def summed(x):
    return jnp.sum(x.astype(F32), axis=0)


def spread_sum(x, axes, count):
    return summed(swap(jnp.broadcast_to(x[None], (count,) + x.shape), axes))


def local(
    fine_input, merge_weight, conv_weight, pre_act, norm_gain, norm_bias, cotangent, counts, neighbours
):
    grad, first, last, frames = call(
        prepare_kernel,
        (shape(B, 4, 16, C), shape(1, 4, 16, C), shape(1, 4, 16, C), shape(8, 144, 128)),
        [SMEM] + [VMEM] * 5,
    )(counts, pre_act, cotangent, norm_gain.reshape(1, C), norm_bias.reshape(1, C), conv_weight)

    frames = swap(frames, "y")
    frames = lax.all_gather(frames, "zh", axis=0, tiled=False)
    frames = swap(jnp.broadcast_to(frames[None], (2, 4, 8, 144, 128)), "c")

    def shifted(x, axes, count, step):
        pairs = [(i, i + step) for i in range(count) if 0 <= i + step < count]
        return lax.ppermute(x, axes, pairs)

    slab_low = shifted(grad, SLAB, SLABS, 1)
    slab_high = shifted(grad, SLAB, SLABS, -1)
    dev_low = shifted(last, DEV, DEVS, 1)
    dev_high = shifted(first, DEV, DEVS, -1)

    windows = jnp.asarray(window_matrix(), BF16)
    order = jnp.asarray(row_order(), BF16)
    back_order = jnp.asarray(row_order().T, BF16)
    conv, taps = call(
        conv_kernel,
        (shape(2, C, HALF), shape(3456, C)),
        [SMEM, SMEM] + [VMEM] * 9,
        [
            pltpu.VMEM((15, 4, 16, C), BF16),
            pltpu.VMEM((6, 144, C), BF16),
            pltpu.VMEM((2, C, HALF), F32),
        ],
    )(
        counts, neighbours, grad, slab_low, slab_high, dev_low, dev_high, fine_input, merge_weight,
        windows, order,
    )

    conv = summed(swap(conv, "c")).astype(BF16)
    conv = swap(conv.reshape(SLABS, COLS, HALF), SLAB)
    conv = call(cut_kernel, shape(32, COLS, ROWS), [VMEM])(conv)
    conv = summed(swap(conv, ("zh", "y")))
    conv_grad = conv.T

    fine_grad, term = call(
        back_kernel,
        (shape(256, 768), shape(2, 576, 128)),
        [SMEM] + [VMEM] * 6,
        [pltpu.VMEM((27 * C, C), BF16)],
    )(counts, frames, taps, fine_input, merge_weight, order, back_order)

    term = summed(swap(term, "c")).astype(BF16)
    term = summed(swap(term.reshape(8, 72, 128), "y")).astype(BF16)
    term = spread_sum(term, ("zh", "zl"), 8).astype(BF16)
    term = spread_sum(term, "x", 4).astype(BF16)
    term = swap(jnp.broadcast_to(term[None], (8, 72, 128)), "y")
    term = lax.all_gather(term, "c", axis=0, tiled=False)
    merge_grad = call(merge_kernel, shape(768, C, dtype=F32), [VMEM])(term.reshape(2, 576, 128))
    return fine_grad, merge_grad, conv_grad


def solution(mesh):
    fine_mesh = Mesh(mesh.devices.reshape(SIZES), AXES)
    every = SLAB + DEV
    in_specs = (
        P(every, None),
        P(),
        P(DEV, None),
        P(every, None, None),
        P(),
        P(),
        P(every, None, None),
        P(),
        P(every, None),
    )
    out_specs = (P(every, None), P(), P(DEV, SLAB))
    return jax.shard_map(
        local, mesh=fine_mesh, in_specs=in_specs, out_specs=out_specs, check_vma=False
    )
```

```python
import jax
import jax.numpy as jnp
from jax import lax
from jax.experimental import pallas as pl
from jax.experimental.pallas import tpu as pltpu
from jax.sharding import Mesh, PartitionSpec as P

F32 = jnp.float32
BF16 = jnp.bfloat16

AXES = ("zl", "x", "zh", "y", "c")
SIZES = (2, 4, 4, 8, 2)
SLAB = ("zl", "x")
DEV = ("zh", "y", "c")
SLABS = 8
DEVS = 64
B = 4
C = 192
ROWS = 81
FRAME = 96
HALF = 32 * ROWS
COLS = C // SLABS

VMEM = pl.BlockSpec(memory_space=pltpu.VMEM)
ANY = pl.BlockSpec(memory_space=pl.ANY)


def dot(a, b):
    return jnp.dot(a, b, preferred_element_type=F32)


def my_place():
    place = lax.axis_index(AXES[0])
    for axis, size in zip(AXES[1:], SIZES[1:]):
        place = place * size + lax.axis_index(axis)
    return place


def iota(rows, cols, dim):
    return lax.broadcasted_iota(jnp.int32, (rows, cols), dim)


def ones_where(condition):
    return jnp.where(condition, 1.0, 0.0).astype(BF16)


def place_in_nine(start, v):
    p = start + v
    brick = jnp.where(p == 0, 0, jnp.where(p == 5, 2, 1))
    return brick, jnp.where(p == 0, 3, jnp.where(p == 5, 0, p - 1))


def window_matrix():
    row, col = iota(144, 144, 0), iota(144, 144, 1)
    s = lax.shift_right_logical(row, 4)
    sx = jnp.where(s >= 6, 2, jnp.where(s >= 3, 1, 0))
    v = jnp.bitwise_and(row, 15)
    kx, x = place_in_nine(sx, lax.shift_right_logical(v, 2))
    ky, y = place_in_nine(s - 3 * sx, jnp.bitwise_and(v, 3))
    return ones_where(col == (kx * 3 + ky) * 16 + x * 4 + y)


def row_order(inverse):
    inner, outer = iota(256, 256, int(inverse)), iota(256, 256, int(not inverse))
    return ones_where(
        outer == jnp.bitwise_and(inner, 63) * 4 + lax.shift_right_logical(inner, 6)
    )


def fetch(sems, *pairs):
    copies = [pltpu.make_async_copy(src, dst, sems.at[i]) for i, (src, dst) in enumerate(pairs)]
    for copy in copies:
        copy.start()
    return copies


def tap_rows(tap):
    window = (2 - tap // 9) * 3 + 2 - tap // 3 % 3
    return (window * 6 + 2 - tap % 3) * 64


def prepare_kernel(
    counts_in, pre_in, cot_in, gain_in, bias_in, weight_in, grad, first, last, frames,
    counts, pre, cot, gain, bias, weight, sems,
):
    copies = fetch(
        sems, (counts_in, counts), (pre_in, pre), (cot_in, cot), (gain_in, gain), (bias_in, bias),
        (weight_in, weight),
    )
    place = my_place()
    copies[5].wait()
    shift = jnp.bitwise_and(place, 15)
    spread = ones_where(iota(FRAME, ROWS, 0) == iota(FRAME, ROWS, 1) + shift)
    frame = dot(spread, weight[...])
    main = frame[:, :128].astype(BF16)
    low = frame[:48, 128:].astype(BF16)
    high = frame[48:, 128:].astype(BF16)
    tail = jnp.concatenate([low, high], axis=1)
    for i in range(32):
        frames[i, :FRAME] = main
        frames[i, FRAME:] = tail
    for copy in copies[:5]:
        copy.wait()
    count = counts[place]
    g = gain[...]
    for b in range(B):
        p = pre[b].astype(F32)
        u = cot[b].astype(F32)
        for z in range(4):
            pz = p[:, z * C : (z + 1) * C]
            uz = u[:, z * C : (z + 1) * C]
            gate = (g * pz + bias[...] > 0) & (b < count)
            grad[b, z] = jnp.where(gate, uz * g, 0.0).astype(BF16)
    first[0] = grad[0]
    last[0] = grad[count - 1]


def conv_kernel(
    counts_in, near_in, fine_in, weight_in, grad, slab_low, slab_high, dev_low, dev_high,
    conv, taps, counts, near, fine, weight, sems, bricks, block, total,
):
    copies = fetch(
        sems, (counts_in, counts), (near_in, near), (fine_in, fine), (weight_in, weight)
    )
    place = my_place()
    bricks[0:4] = grad[...]
    bricks[4:8] = slab_low[...]
    bricks[8:12] = slab_high[...]
    bricks[12:13] = dev_low[...]
    bricks[13:14] = dev_high[...]
    bricks[14:15] = jnp.zeros((1, 4, 16, C), BF16)
    window = window_matrix()
    copies[1].wait()
    for b in range(B):
        slots = []
        for k in range(27):
            brick = near[b, k]
            away = lax.shift_right_arithmetic(brick, 2) - place
            slot = jnp.bitwise_and(brick, 3)
            at = jnp.where(away == 0, slot, 14)
            at = jnp.where(away == -DEVS, 4 + slot, at)
            at = jnp.where(away == DEVS, 8 + slot, at)
            at = jnp.where(away == -1, 12, at)
            at = jnp.where(away == 1, 13, at)
            slots.append(jnp.where(brick < 0, 14, at))
        for plane in range(6):
            kz, z = ((0, 3), (1, 0), (1, 1), (1, 2), (1, 3), (2, 0))[plane]
            for q in range(9):
                block[plane, q * 16 : (q + 1) * 16] = bricks[slots[q * 3 + kz], z]
        for plane in range(6):
            moved = dot(window, block[plane]).astype(BF16)
            for s in range(9):
                row = ((s * 6 + plane) * B + b) * 16
                taps[row : row + 16] = moved[s * 16 : (s + 1) * 16]
    for copy in (copies[0], copies[2], copies[3]):
        copy.wait()
    count = counts[place]
    merged = dot(fine[...], weight[...])
    brick_of = lax.broadcasted_iota(jnp.int32, (256, C), 0) // 64
    merged = jnp.where(brick_of < count, merged, 0.0).astype(BF16)
    merged = jnp.transpose(dot(row_order(False), merged)).astype(BF16)
    for tap in range(27):
        row = tap_rows(tap)
        term = dot(merged, taps[row : row + 256])
        at = tap * C
        end = at + C
        while at < end:
            owner = at // ROWS
            stop = min(end, (owner + 1) * ROWS)
            to = (owner // 2) * ROWS + at % ROWS
            total[owner % 2, :, to : to + stop - at] = term[:, at - tap * C : stop - tap * C]
            at = stop
    for half in range(2):
        conv[half] = total[half].astype(BF16)


def back_kernel(
    counts_in, fine_in, weight_in, mine, other, taps, fine_grad, term,
    counts, fine, weight, sems, both, whole,
):
    copies = fetch(sems, (counts_in, counts), (fine_in, fine), (weight_in, weight))
    place = my_place()
    core = jnp.bitwise_and(place, 1)
    both[core] = mine[...]
    both[1 - core] = other[...]
    for owner in range(DEVS):
        tile = ROWS * owner // 16
        frame = both.at[owner % 2, owner // 2]
        main = frame[:FRAME]
        low = frame[FRAME:, :64]
        high = frame[FRAME:, 64:]
        row = tile * 16
        if owner % 16:
            whole[row : row + 16, :128] = whole[row : row + 16, :128] + main[:16]
            whole[row : row + 16, 128:] = whole[row : row + 16, 128:] + low[:16]
            whole[row + 16 : row + FRAME, :128] = main[16:]
            whole[row + 16 : row + 48, 128:] = low[16:]
        else:
            whole[row : row + FRAME, :128] = main
            whole[row : row + 48, 128:] = low
        whole[row + 48 : row + FRAME, 128:] = high
    back = jnp.zeros((256, C), F32)
    for tap in range(27):
        row = tap_rows(tap)
        back = back + dot(taps[row : row + 256], whole[tap * C : (tap + 1) * C])
    brick_of = lax.broadcasted_iota(jnp.int32, (256, C), 0) // 16 % B
    for copy in copies:
        copy.wait()
    count = counts[place]
    back = jnp.where(brick_of < count, back, 0.0).astype(BF16)
    back = dot(row_order(True), back)
    gm = back.astype(BF16)
    fine_grad[...] = lax.dot_general(
        gm, weight[...], (((1,), (1,)), ((), ())), preferred_element_type=F32
    ).astype(BF16)
    result = dot(jnp.transpose(back).astype(BF16), fine[...]).astype(BF16)
    for part in range(6):
        term[part * C : (part + 1) * C] = result[:, part * 128 : (part + 1) * 128]
    term[6 * C :] = jnp.zeros((8 * C - 6 * C, 128), BF16)


def cut_kernel(parts, out):
    total = parts[0].astype(F32)
    for i in range(1, SLABS):
        total = total + parts[i].astype(F32)
    for i in range(32):
        out[i] = total[:, i * ROWS : (i + 1) * ROWS].astype(BF16)


def spread_kernel(parts, out):
    total = parts[0].astype(F32)
    for i in range(1, parts.shape[0]):
        total = total + parts[i].astype(F32)
    for i in range(out.shape[0]):
        out[i] = total.astype(BF16)


def merge_kernel(parts, out):
    for part in range(6):
        block = parts[part * C : (part + 1) * C].astype(F32)
        out[part * 128 : (part + 1) * 128] = jnp.transpose(block)


def call(kernel, outs, specs, scratch=()):
    return pl.pallas_call(
        kernel,
        out_shape=outs,
        in_specs=specs,
        out_specs=jax.tree.map(lambda _: VMEM, outs),
        scratch_shapes=scratch,
        compiler_params=pltpu.CompilerParams(vmem_limit_bytes=40 << 20),
    )


def shape(*dims, dtype=BF16):
    return jax.ShapeDtypeStruct(dims, dtype)


def swap(x, axes):
    return lax.all_to_all(x, axes, 0, 0, tiled=True)


def summed(x):
    return jnp.sum(x.astype(F32), axis=0)


def local(
    fine_input, merge_weight, conv_weight, pre_act, norm_gain, norm_bias, cotangent, counts, neighbours
):
    counts_scratch = pltpu.SMEM((SLABS * DEVS,), jnp.int32)
    grad, first, last, frames = call(
        prepare_kernel,
        (shape(B, 4, 16, C), shape(1, 4, 16, C), shape(1, 4, 16, C), shape(32, 144, 128)),
        [ANY] * 6,
        [
            counts_scratch,
            pltpu.VMEM((B, 16, 4 * C), BF16),
            pltpu.VMEM((B, 16, 4 * C), BF16),
            pltpu.VMEM((1, C), F32),
            pltpu.VMEM((1, C), F32),
            pltpu.VMEM((ROWS, C), BF16),
            pltpu.SemaphoreType.DMA((6,)),
        ],
    )(counts, pre_act, cotangent, norm_gain.reshape(1, C), norm_bias.reshape(1, C), conv_weight)

    frames = swap(frames, ("zh", "y"))

    def shifted(x, axes, count, step):
        pairs = [(i, i + step) for i in range(count) if 0 <= i + step < count]
        return lax.ppermute(x, axes, pairs)

    slab_low = shifted(grad, SLAB, SLABS, 1)
    slab_high = shifted(grad, SLAB, SLABS, -1)
    dev_low = shifted(last, DEV, DEVS, 1)
    dev_high = shifted(first, DEV, DEVS, -1)

    fine_scratch = pltpu.VMEM((256, 768), BF16)
    weight_scratch = pltpu.VMEM((768, C), BF16)
    conv, taps = call(
        conv_kernel,
        (shape(2, C, HALF), shape(3456, C)),
        [ANY] * 4 + [VMEM] * 5,
        [
            counts_scratch,
            pltpu.SMEM((B, 27), jnp.int32),
            fine_scratch,
            weight_scratch,
            pltpu.SemaphoreType.DMA((4,)),
            pltpu.VMEM((15, 4, 16, C), BF16),
            pltpu.VMEM((6, 144, C), BF16),
            pltpu.VMEM((2, C, HALF), F32),
        ],
    )(
        counts, neighbours, fine_input, merge_weight, grad, slab_low, slab_high, dev_low, dev_high
    )

    conv = summed(swap(conv, "c")).astype(BF16)
    conv = swap(conv.reshape(SLABS, COLS, HALF), SLAB)
    frames, conv = lax.optimization_barrier((frames, conv))

    other = lax.ppermute(frames, "c", [(0, 1), (1, 0)])
    fine_grad, term = call(
        back_kernel,
        (shape(256, 768), shape(DEVS * 24, 128)),
        [ANY] * 3 + [VMEM] * 3,
        [
            counts_scratch,
            fine_scratch,
            weight_scratch,
            pltpu.SemaphoreType.DMA((3,)),
            pltpu.VMEM((2, 32, 144, 128), BF16),
            pltpu.VMEM((27 * C, C), BF16),
        ],
    )(counts, fine_input, merge_weight, frames, other, taps)

    conv = call(cut_kernel, shape(32, COLS, ROWS), [VMEM])(conv)
    conv_grad = summed(swap(conv, ("zh", "y"))).T

    term = swap(term.reshape(DEVS, 24, 128), DEV)
    term = call(spread_kernel, shape(SLABS, 24, 128), [VMEM])(term)
    term = swap(term, SLAB)
    term = call(spread_kernel, shape(DEVS, 24, 128), [VMEM])(term)
    term = swap(term, DEV)
    merge_grad = call(merge_kernel, shape(768, C, dtype=F32), [VMEM])(term.reshape(DEVS * 24, 128))
    return fine_grad, merge_grad, conv_grad


def solution(mesh):
    fine_mesh = Mesh(mesh.devices.reshape(SIZES), AXES)
    every = SLAB + DEV
    in_specs = (
        P(every, None),
        P(),
        P(DEV, None),
        P(every, None, None),
        P(),
        P(),
        P(every, None, None),
        P(),
        P(every, None),
    )
    out_specs = (P(every, None), P(), P(DEV, SLAB))
    return jax.shard_map(
        local, mesh=fine_mesh, in_specs=in_specs, out_specs=out_specs, check_vma=False
    )
```

```python
import jax
import jax.numpy as jnp
from jax import lax
from jax.experimental import pallas as pl
from jax.experimental.pallas import tpu as pltpu
from jax.sharding import Mesh, PartitionSpec as P

F32 = jnp.float32
BF16 = jnp.bfloat16

AXES = ("zl", "x", "zh", "y", "c")
SIZES = (2, 4, 4, 8, 2)
SLAB = ("zl", "x")
DEV = ("zh", "y", "c")
SLABS = 8
DEVS = 64
B = 4
C = 192
ROWS = 81
FRAME = 96
HALF = 32 * ROWS
COLS = C // SLABS

VMEM = pl.BlockSpec(memory_space=pltpu.VMEM)
HBM = pl.BlockSpec(memory_space=pltpu.HBM)


def dot(a, b):
    return jnp.dot(a, b, preferred_element_type=F32)


def my_place():
    place = lax.axis_index(AXES[0])
    for axis, size in zip(AXES[1:], SIZES[1:]):
        place = place * size + lax.axis_index(axis)
    return place


def iota(rows, cols, dim):
    return lax.broadcasted_iota(jnp.int32, (rows, cols), dim)


def ones_where(condition):
    return jnp.where(condition, 1.0, 0.0).astype(BF16)


def place_in_nine(start, v):
    p = start + v
    brick = jnp.where(p == 0, 0, jnp.where(p == 5, 2, 1))
    return brick, jnp.where(p == 0, 3, jnp.where(p == 5, 0, p - 1))


def window_matrix():
    row, col = iota(144, 144, 0), iota(144, 144, 1)
    s = lax.shift_right_logical(row, 4)
    sx = jnp.where(s >= 6, 2, jnp.where(s >= 3, 1, 0))
    v = jnp.bitwise_and(row, 15)
    kx, x = place_in_nine(sx, lax.shift_right_logical(v, 2))
    ky, y = place_in_nine(s - 3 * sx, jnp.bitwise_and(v, 3))
    return ones_where(col == (kx * 3 + ky) * 16 + x * 4 + y)


def row_order(inverse):
    inner, outer = iota(256, 256, int(inverse)), iota(256, 256, int(not inverse))
    return ones_where(
        outer == jnp.bitwise_and(inner, 63) * 4 + lax.shift_right_logical(inner, 6)
    )


def fetch(sems, *pairs):
    copies = [pltpu.make_async_copy(src, dst, sems.at[i]) for i, (src, dst) in enumerate(pairs)]
    for copy in copies:
        copy.start()
    return copies


def tap_rows(tap):
    window = (2 - tap // 9) * 3 + 2 - tap // 3 % 3
    return (window * 6 + 2 - tap % 3) * 64


def prepare_kernel(
    counts_in, pre_in, cot_in, gain_in, bias_in, weight_in, grad, first, last, frames,
    counts, pre, cot, gain, bias, weight, sems,
):
    copies = fetch(
        sems, (counts_in, counts), (pre_in, pre), (cot_in, cot), (gain_in, gain), (bias_in, bias),
        (weight_in, weight),
    )
    place = my_place()
    copies[5].wait()
    shift = jnp.bitwise_and(place, 15)
    spread = ones_where(iota(FRAME, ROWS, 0) == iota(FRAME, ROWS, 1) + shift)
    frame = dot(spread, weight[...])
    main = frame[:, :128].astype(BF16)
    low = frame[:48, 128:].astype(BF16)
    high = frame[48:, 128:].astype(BF16)
    tail = jnp.concatenate([low, high], axis=1)
    for i in range(32):
        frames[i, :FRAME] = main
        frames[i, FRAME:] = tail
    for copy in copies[:5]:
        copy.wait()
    count = counts[place]
    g = gain[...]
    for b in range(B):
        p = pre[b].astype(F32)
        u = cot[b].astype(F32)
        for z in range(4):
            pz = p[:, z * C : (z + 1) * C]
            uz = u[:, z * C : (z + 1) * C]
            gate = (g * pz + bias[...] > 0) & (b < count)
            grad[b, z] = jnp.where(gate, uz * g, 0.0).astype(BF16)
    first[0] = grad[0]
    last[0] = grad[count - 1]


def conv_kernel(
    counts_in, near_in, fine_in, weight_in, grad, slab_low, slab_high, dev_low, dev_high,
    keep, send, taps, counts, near, fine, weight, sems, bricks, block, total,
):
    copies = fetch(
        sems, (counts_in, counts), (near_in, near), (fine_in, fine), (weight_in, weight)
    )
    place = my_place()
    bricks[0:4] = grad[...]
    bricks[4:8] = slab_low[...]
    bricks[8:12] = slab_high[...]
    bricks[12:13] = dev_low[...]
    bricks[13:14] = dev_high[...]
    bricks[14:15] = jnp.zeros((1, 4, 16, C), BF16)
    window = window_matrix()
    copies[1].wait()
    for b in range(B):
        slots = []
        for k in range(27):
            brick = near[b, k]
            away = lax.shift_right_arithmetic(brick, 2) - place
            slot = jnp.bitwise_and(brick, 3)
            at = jnp.where(away == 0, slot, 14)
            at = jnp.where(away == -DEVS, 4 + slot, at)
            at = jnp.where(away == DEVS, 8 + slot, at)
            at = jnp.where(away == -1, 12, at)
            at = jnp.where(away == 1, 13, at)
            slots.append(jnp.where(brick < 0, 14, at))
        for plane in range(6):
            kz, z = ((0, 3), (1, 0), (1, 1), (1, 2), (1, 3), (2, 0))[plane]
            for q in range(9):
                block[plane, q * 16 : (q + 1) * 16] = bricks[slots[q * 3 + kz], z]
        for plane in range(6):
            moved = dot(window, block[plane]).astype(BF16)
            for s in range(9):
                row = ((s * 6 + plane) * B + b) * 16
                taps[row : row + 16] = moved[s * 16 : (s + 1) * 16]
    for copy in (copies[0], copies[2], copies[3]):
        copy.wait()
    count = counts[place]
    merged = lax.dot_general(
        fine[...], weight[...], (((1,), (1,)), ((), ())), preferred_element_type=F32
    )
    brick_of = lax.broadcasted_iota(jnp.int32, (256, C), 0) // 64
    merged = jnp.where(brick_of < count, merged, 0.0).astype(BF16)
    merged = jnp.transpose(dot(row_order(False), merged)).astype(BF16)
    for tap in range(27):
        row = tap_rows(tap)
        term = dot(merged, taps[row : row + 256])
        at = tap * C
        end = at + C
        while at < end:
            owner = at // ROWS
            stop = min(end, (owner + 1) * ROWS)
            to = (owner // 2) * ROWS + at % ROWS
            total[owner % 2, :, to : to + stop - at] = term[:, at - tap * C : stop - tap * C]
            at = stop
    core = jnp.bitwise_and(place, 1)
    for out, half in ((keep, core), (send, 1 - core)):
        for slab in range(SLABS):
            out[slab] = total[half, slab * COLS : (slab + 1) * COLS].astype(BF16)


def slab_partners():
    return [(dz, dx) for dz in range(2) for dx in range(4) if dz or dx]


def split_kernel(keep, received, *outs):
    zl, x = lax.axis_index("zl"), lax.axis_index("x")
    for out, (dz, dx) in zip(outs, [(0, 0)] + slab_partners()):
        slab = jnp.bitwise_xor(zl, dz) * 4 + jnp.bitwise_and(x + dx, 3)
        out[...] = (keep[slab].astype(F32) + received[slab].astype(F32)).astype(BF16)


def back_kernel(
    counts_in, fine_in, weight_in, mine, other, taps, fine_grad, keep, send,
    counts, fine, weight, sems, both, whole, term,
):
    copies = fetch(sems, (counts_in, counts), (fine_in, fine), (weight_in, weight))
    place = my_place()
    core = jnp.bitwise_and(place, 1)
    both[core] = mine[...]
    both[1 - core] = other[...]
    for owner in range(DEVS):
        tile = ROWS * owner // 16
        frame = both.at[owner % 2, owner // 2]
        main = frame[:FRAME]
        low = frame[FRAME:, :64]
        high = frame[FRAME:, 64:]
        row = tile * 16
        if owner % 16:
            whole[row : row + 16, :128] = whole[row : row + 16, :128] + main[:16]
            whole[row : row + 16, 128:] = whole[row : row + 16, 128:] + low[:16]
            whole[row + 16 : row + FRAME, :128] = main[16:]
            whole[row + 16 : row + 48, 128:] = low[16:]
        else:
            whole[row : row + FRAME, :128] = main
            whole[row : row + 48, 128:] = low
        whole[row + 48 : row + FRAME, 128:] = high
    back = jnp.zeros((256, C), F32)
    for tap in range(27):
        row = tap_rows(tap)
        back = back + dot(taps[row : row + 256], whole[tap * C : (tap + 1) * C])
    brick_of = lax.broadcasted_iota(jnp.int32, (256, C), 0) // 16 % B
    for copy in copies:
        copy.wait()
    count = counts[place]
    back = jnp.where(brick_of < count, back, 0.0).astype(BF16)
    back = dot(row_order(True), back)
    gm = back.astype(BF16)
    fine_grad[...] = dot(gm, weight[...]).astype(BF16)
    result = dot(jnp.transpose(back).astype(BF16), fine[...]).astype(BF16)
    for part in range(6):
        row = part % 3 * C
        term[part // 3, row : row + C] = result[:, part * 128 : (part + 1) * 128]
    keep[...] = term[core]
    send[...] = term[1 - core]


def join_kernel(keep, received, *refs):
    parts, out = refs[:-1], refs[-1]
    total = parts[0][...].astype(F32)
    for part in parts[1:]:
        total = total + part[...].astype(F32)
    pad = jnp.zeros((COLS, 128 - ROWS), BF16)
    for i in range(32):
        piece = total[:, i * ROWS : (i + 1) * ROWS].astype(BF16)
        out[i, 0] = jnp.concatenate([piece, pad], axis=1)
    for i in range(24):
        out[i, 1] = (keep[i].astype(F32) + received[i].astype(F32)).astype(BF16)
    for i in range(24, 32):
        out[i, 1] = jnp.zeros((24, 128), BF16)


def part_kernel(parts, conv_grad, out):
    total = [parts[0, kind].astype(F32) for kind in range(2)]
    for i in range(1, 32):
        total = [total[kind] + parts[i, kind].astype(F32) for kind in range(2)]
    conv_grad[...] = jnp.transpose(total[0])[:ROWS]
    for i in range(SLABS):
        out[i] = total[1].astype(BF16)


def spread_kernel(parts, out):
    total = parts[0].astype(F32)
    for i in range(1, parts.shape[0]):
        total = total + parts[i].astype(F32)
    for i in range(out.shape[0]):
        out[i] = total.astype(BF16)


def merge_kernel(parts, out, held, sems):
    for part in range(6):
        row = part % 3 * C
        block = parts[part // 3, row : row + C]
        held[:, part * 128 : (part + 1) * 128] = block.astype(F32)
    copy = pltpu.make_async_copy(held, out, sems.at[0])
    copy.start()
    copy.wait()


def call(kernel, outs, specs, scratch=(), flops=0, out_spec=VMEM, vmem=40):
    return pl.pallas_call(
        kernel,
        out_shape=outs,
        in_specs=specs,
        out_specs=jax.tree.map(lambda _: out_spec, outs),
        scratch_shapes=scratch,
        cost_estimate=pl.CostEstimate(flops=flops, bytes_accessed=0, transcendentals=0),
        compiler_params=pltpu.CompilerParams(vmem_limit_bytes=vmem << 20),
    )


def shape(*dims, dtype=BF16):
    return jax.ShapeDtypeStruct(dims, dtype)


def swap(x, axes):
    return lax.all_to_all(x, axes, 0, 0, tiled=True)


def local(
    fine_input, merge_weight, conv_weight, pre_act, norm_gain, norm_bias, cotangent, counts, neighbours
):
    counts_scratch = pltpu.SMEM((SLABS * DEVS,), jnp.int32)
    grad, first, last, frames = call(
        prepare_kernel,
        (shape(B, 4, 16, C), shape(1, 4, 16, C), shape(1, 4, 16, C), shape(32, 144, 128)),
        [HBM] * 6,
        [
            counts_scratch,
            pltpu.VMEM((B, 16, 4 * C), BF16),
            pltpu.VMEM((B, 16, 4 * C), BF16),
            pltpu.VMEM((1, C), F32),
            pltpu.VMEM((1, C), F32),
            pltpu.VMEM((ROWS, C), BF16),
            pltpu.SemaphoreType.DMA((6,)),
        ],
        vmem=60,
    )(counts, pre_act, cotangent, norm_gain.reshape(1, C), norm_bias.reshape(1, C), conv_weight)

    frames = swap(frames, ("zh", "y"))

    def shifted(x, axes, count, step):
        pairs = [(i, i + step) for i in range(count) if 0 <= i + step < count]
        return lax.ppermute(x, axes, pairs)

    def flipped(x):
        return lax.ppermute(x, "c", [(0, 1), (1, 0)])

    slab_low = shifted(grad, SLAB, SLABS, 1)
    slab_high = shifted(grad, SLAB, SLABS, -1)
    dev_low = shifted(last, DEV, DEVS, 1)
    dev_high = shifted(first, DEV, DEVS, -1)

    fine_scratch = pltpu.VMEM((256, 768), BF16)
    weight_scratch = pltpu.VMEM((C, 768), BF16)
    merge_weight = merge_weight.T
    keep, send, taps = call(
        conv_kernel,
        (shape(SLABS, COLS, HALF), shape(SLABS, COLS, HALF), shape(3456, C)),
        [HBM] * 4 + [VMEM] * 5,
        [
            counts_scratch,
            pltpu.SMEM((B, 27), jnp.int32),
            fine_scratch,
            weight_scratch,
            pltpu.SemaphoreType.DMA((4,)),
            pltpu.VMEM((15, 4, 16, C), BF16),
            pltpu.VMEM((6, 144, C), BF16),
            pltpu.VMEM((2, C, HALF), F32),
        ],
        flops=6 * 10**9,
    )(
        counts, neighbours, fine_input, merge_weight, grad, slab_low, slab_high, dev_low, dev_high
    )

    conv = call(split_kernel, (shape(COLS, HALF),) * SLABS, [VMEM] * 2)(keep, flipped(send))
    moved = [conv[0]]
    for block, (dz, dx) in zip(conv[1:], slab_partners()):
        pairs = [(i, (i // 4 ^ dz) * 4 + (i + dx) % 4) for i in range(SLABS)]
        moved.append(lax.ppermute(block, SLAB, pairs))
    frames, moved = lax.optimization_barrier((frames, moved))

    other = flipped(frames)
    fine_grad, keep, send = call(
        back_kernel,
        (shape(256, 768), shape(576, 128), shape(576, 128)),
        [HBM] * 3 + [VMEM] * 3,
        [
            counts_scratch,
            fine_scratch,
            weight_scratch,
            pltpu.SemaphoreType.DMA((3,)),
            pltpu.VMEM((2, 32, 144, 128), BF16),
            pltpu.VMEM((27 * C, C), BF16),
            pltpu.VMEM((2, 576, 128), BF16),
        ],
        flops=4 * 10**9,
        vmem=48,
    )(counts, fine_input, merge_weight, frames, other, taps)

    joined = call(join_kernel, shape(32, 2, 24, 128), [VMEM] * (2 + SLABS))(
        keep.reshape(24, 24, 128), flipped(send).reshape(24, 24, 128), *moved
    )
    joined = swap(joined, ("zh", "y"))
    conv_grad, term = call(
        part_kernel, (shape(ROWS, COLS, dtype=F32), shape(SLABS, 24, 128)), [VMEM]
    )(joined)
    term = swap(term, SLAB)
    term = call(spread_kernel, shape(32, 24, 128), [VMEM])(term)
    term = swap(term, ("zh", "y"))
    term = lax.all_gather(term, "c", axis=0, tiled=False)
    merge_grad = call(
        merge_kernel,
        shape(C, 768, dtype=F32),
        [VMEM],
        [pltpu.VMEM((C, 768), F32), pltpu.SemaphoreType.DMA((1,))],
        out_spec=HBM,
    )(term.reshape(2, 768, 128)).T
    return fine_grad, merge_grad, conv_grad


def solution(mesh):
    fine_mesh = Mesh(mesh.devices.reshape(SIZES), AXES)
    every = SLAB + DEV
    in_specs = (
        P(every, None),
        P(),
        P(DEV, None),
        P(every, None, None),
        P(),
        P(),
        P(every, None, None),
        P(),
        P(every, None),
    )
    out_specs = (P(every, None), P(), P(DEV, SLAB))
    return jax.shard_map(
        local, mesh=fine_mesh, in_specs=in_specs, out_specs=out_specs, check_vma=False
    )
```

```python
import jax
import jax.numpy as jnp
from jax import lax
from jax.experimental import pallas as pl
from jax.experimental.pallas import tpu as pltpu
from jax.sharding import Mesh, PartitionSpec as P

F32 = jnp.float32
BF16 = jnp.bfloat16

AXES = ("zl", "x", "zh", "y", "c")
SIZES = (2, 4, 4, 8, 2)
SLAB = ("zl", "x")
DEV = ("zh", "y", "c")
SLABS = 8
DEVS = 64
B = 4
C = 192
ROWS = 81
FRAME = 96
HALF = 32 * ROWS
COLS = C // SLABS

VMEM = pl.BlockSpec(memory_space=pltpu.VMEM)
HBM = pl.BlockSpec(memory_space=pltpu.HBM)


def dot(a, b):
    return jnp.dot(a, b, preferred_element_type=F32)


def my_place():
    place = lax.axis_index(AXES[0])
    for axis, size in zip(AXES[1:], SIZES[1:]):
        place = place * size + lax.axis_index(axis)
    return place


def iota(rows, cols, dim):
    return lax.broadcasted_iota(jnp.int32, (rows, cols), dim)


def ones_where(condition):
    return jnp.where(condition, 1.0, 0.0).astype(BF16)


def place_in_nine(start, v):
    p = start + v
    brick = jnp.where(p == 0, 0, jnp.where(p == 5, 2, 1))
    return brick, jnp.where(p == 0, 3, jnp.where(p == 5, 0, p - 1))


def window_matrix():
    row, col = iota(144, 144, 0), iota(144, 144, 1)
    s = lax.shift_right_logical(row, 4)
    sx = jnp.where(s >= 6, 2, jnp.where(s >= 3, 1, 0))
    v = jnp.bitwise_and(row, 15)
    kx, x = place_in_nine(sx, lax.shift_right_logical(v, 2))
    ky, y = place_in_nine(s - 3 * sx, jnp.bitwise_and(v, 3))
    return ones_where(col == (kx * 3 + ky) * 16 + x * 4 + y)


def row_order(inverse):
    inner, outer = iota(256, 256, int(inverse)), iota(256, 256, int(not inverse))
    return ones_where(
        outer == jnp.bitwise_and(inner, 63) * 4 + lax.shift_right_logical(inner, 6)
    )


def fetch(sems, *pairs):
    copies = [pltpu.make_async_copy(src, dst, sems.at[i]) for i, (src, dst) in enumerate(pairs)]
    for copy in copies:
        copy.start()
    return copies


def tap_rows(tap):
    window = (2 - tap // 9) * 3 + 2 - tap // 3 % 3
    return (window * 6 + 2 - tap % 3) * 64


def prepare_kernel(
    counts_in, pre_in, cot_in, gain_in, bias_in, weight_in, grad, first, last, frames,
    counts, pre, cot, gain, bias, weight, sems,
):
    copies = fetch(
        sems, (counts_in, counts), (pre_in, pre), (cot_in, cot), (gain_in, gain), (bias_in, bias),
        (weight_in, weight),
    )
    place = my_place()
    copies[5].wait()
    shift = jnp.bitwise_and(place, 15)
    spread = ones_where(iota(FRAME, ROWS, 0) == iota(FRAME, ROWS, 1) + shift)
    frame = dot(spread, weight[...])
    main = frame[:, :128].astype(BF16)
    low = frame[:48, 128:].astype(BF16)
    high = frame[48:, 128:].astype(BF16)
    tail = jnp.concatenate([low, high], axis=1)
    for i in range(32):
        frames[i, :FRAME] = main
        frames[i, FRAME:] = tail
    for copy in copies[:5]:
        copy.wait()
    count = counts[place]
    g = gain[...]
    for b in range(B):
        p = pre[b].astype(F32)
        u = cot[b].astype(F32)
        for z in range(4):
            pz = p[:, z * C : (z + 1) * C]
            uz = u[:, z * C : (z + 1) * C]
            gate = (g * pz + bias[...] > 0) & (b < count)
            grad[b, z] = jnp.where(gate, uz * g, 0.0).astype(BF16)
    first[0] = grad[0]
    last[0] = grad[count - 1]


def conv_kernel(
    counts_in, near_in, fine_in, weight_in, grad, slab_low, slab_high, dev_low, dev_high,
    keep, send, taps_out, counts, near, fine, weight, sems, bricks, block, total, taps,
):
    copies = fetch(
        sems, (counts_in, counts), (near_in, near), (fine_in, fine), (weight_in, weight)
    )
    place = my_place()
    bricks[0:4] = grad[...]
    bricks[4:8] = slab_low[...]
    bricks[8:12] = slab_high[...]
    bricks[12:13] = dev_low[...]
    bricks[13:14] = dev_high[...]
    bricks[14:15] = jnp.zeros((1, 4, 16, C), BF16)
    window = window_matrix()
    copies[1].wait()
    for b in range(B):
        slots = []
        for k in range(27):
            brick = near[b, k]
            away = lax.shift_right_arithmetic(brick, 2) - place
            slot = jnp.bitwise_and(brick, 3)
            at = jnp.where(away == 0, slot, 14)
            at = jnp.where(away == -DEVS, 4 + slot, at)
            at = jnp.where(away == DEVS, 8 + slot, at)
            at = jnp.where(away == -1, 12, at)
            at = jnp.where(away == 1, 13, at)
            slots.append(jnp.where(brick < 0, 14, at))
        for plane in range(6):
            kz, z = ((0, 3), (1, 0), (1, 1), (1, 2), (1, 3), (2, 0))[plane]
            for q in range(9):
                block[plane, q * 16 : (q + 1) * 16] = bricks[slots[q * 3 + kz], z]
        for plane in range(6):
            moved = dot(window, block[plane]).astype(BF16)
            for s in range(9):
                row = ((s * 6 + plane) * B + b) * 16
                taps[row : row + 16] = moved[s * 16 : (s + 1) * 16]
    leave = pltpu.make_async_copy(taps, taps_out, sems.at[4])
    leave.start()
    for copy in (copies[0], copies[2], copies[3]):
        copy.wait()
    count = counts[place]
    merged = lax.dot_general(
        fine[...], weight[...], (((1,), (1,)), ((), ())), preferred_element_type=F32
    )
    brick_of = lax.broadcasted_iota(jnp.int32, (256, C), 0) // 64
    merged = jnp.where(brick_of < count, merged, 0.0).astype(BF16)
    merged = jnp.transpose(dot(row_order(False), merged)).astype(BF16)
    for tap in range(27):
        row = tap_rows(tap)
        term = dot(merged, taps[row : row + 256])
        at = tap * C
        end = at + C
        while at < end:
            owner = at // ROWS
            stop = min(end, (owner + 1) * ROWS)
            to = (owner // 2) * ROWS + at % ROWS
            total[owner % 2, :, to : to + stop - at] = term[:, at - tap * C : stop - tap * C]
            at = stop
    core = jnp.bitwise_and(place, 1)
    for out, half in ((keep, core), (send, 1 - core)):
        for slab in range(SLABS):
            out[slab] = total[half, slab * COLS : (slab + 1) * COLS].astype(BF16)
    leave.wait()


def split_kernel(keep, received, *outs):
    x = lax.axis_index("x")
    for dx, out in enumerate(outs):
        for zl in range(2):
            slab = zl * 4 + jnp.bitwise_and(x + dx, 3)
            out[zl] = (keep[slab].astype(F32) + received[slab].astype(F32)).astype(BF16)


def halve_kernel(a, b, c, d, keep, send):
    zl = lax.axis_index("zl")
    for out, half in ((keep, zl), (send, 1 - zl)):
        total = a[half].astype(F32) + b[half].astype(F32) + c[half].astype(F32)
        out[...] = (total + d[half].astype(F32)).astype(BF16)


def back_kernel(
    counts_in, fine_in, weight_in, taps_in, mine, other, fine_grad, keep, send,
    counts, fine, weight, taps, sems, both, whole, term,
):
    copies = fetch(
        sems, (counts_in, counts), (fine_in, fine), (weight_in, weight), (taps_in, taps)
    )
    place = my_place()
    core = jnp.bitwise_and(place, 1)
    both[core] = mine[...]
    both[1 - core] = other[...]
    for owner in range(DEVS):
        tile = ROWS * owner // 16
        frame = both.at[owner % 2, owner // 2]
        main = frame[:FRAME]
        low = frame[FRAME:, :64]
        high = frame[FRAME:, 64:]
        row = tile * 16
        if owner % 16:
            whole[row : row + 16, :128] = whole[row : row + 16, :128] + main[:16]
            whole[row : row + 16, 128:] = whole[row : row + 16, 128:] + low[:16]
            whole[row + 16 : row + FRAME, :128] = main[16:]
            whole[row + 16 : row + 48, 128:] = low[16:]
        else:
            whole[row : row + FRAME, :128] = main
            whole[row : row + 48, 128:] = low
        whole[row + 48 : row + FRAME, 128:] = high
    copies[3].wait()
    back = jnp.zeros((256, C), F32)
    for tap in range(27):
        row = tap_rows(tap)
        back = back + dot(taps[row : row + 256], whole[tap * C : (tap + 1) * C])
    brick_of = lax.broadcasted_iota(jnp.int32, (256, C), 0) // 16 % B
    for copy in copies[:3]:
        copy.wait()
    count = counts[place]
    back = jnp.where(brick_of < count, back, 0.0).astype(BF16)
    back = dot(row_order(True), back)
    gm = back.astype(BF16)
    fine_grad[...] = dot(gm, weight[...]).astype(BF16)
    result = dot(jnp.transpose(back).astype(BF16), fine[...]).astype(BF16)
    for part in range(6):
        row = part % 3 * C
        term[part // 3, row : row + C] = result[:, part * 128 : (part + 1) * 128]
    keep[...] = term[core]
    send[...] = term[1 - core]


def join_kernel(keep, received, conv_keep, conv_received, out):
    total = conv_keep[...].astype(F32) + conv_received[...].astype(F32)
    pad = jnp.zeros((COLS, 128 - ROWS), BF16)
    for i in range(32):
        piece = total[:, i * ROWS : (i + 1) * ROWS].astype(BF16)
        out[i, 0] = jnp.concatenate([piece, pad], axis=1)
    for i in range(24):
        out[i, 1] = (keep[i].astype(F32) + received[i].astype(F32)).astype(BF16)
    for i in range(24, 32):
        out[i, 1] = jnp.zeros((24, 128), BF16)


def part_kernel(parts, conv_grad, out):
    total = [parts[0, kind].astype(F32) for kind in range(2)]
    for i in range(1, 32):
        total = [total[kind] + parts[i, kind].astype(F32) for kind in range(2)]
    conv_grad[...] = jnp.transpose(total[0])[:ROWS]
    for i in range(SLABS):
        out[i] = total[1].astype(BF16)


def spread_kernel(parts, out):
    total = parts[0].astype(F32)
    for i in range(1, parts.shape[0]):
        total = total + parts[i].astype(F32)
    for i in range(out.shape[0]):
        out[i] = total.astype(BF16)


def merge_kernel(parts, out, held, sems):
    for part in range(6):
        row = part % 3 * C
        block = parts[part // 3, row : row + C]
        held[:, part * 128 : (part + 1) * 128] = block.astype(F32)
    copy = pltpu.make_async_copy(held, out, sems.at[0])
    copy.start()
    copy.wait()


def call(kernel, outs, specs, scratch=(), flops=0, out_spec=None, vmem=40):
    return pl.pallas_call(
        kernel,
        out_shape=outs,
        in_specs=specs,
        out_specs=out_spec or jax.tree.map(lambda _: VMEM, outs),
        scratch_shapes=scratch,
        cost_estimate=pl.CostEstimate(flops=flops, bytes_accessed=0, transcendentals=0),
        compiler_params=pltpu.CompilerParams(vmem_limit_bytes=vmem << 20),
    )


def shape(*dims, dtype=BF16):
    return jax.ShapeDtypeStruct(dims, dtype)


def swap(x, axes):
    return lax.all_to_all(x, axes, 0, 0, tiled=True)


def local(
    fine_input, merge_weight, conv_weight, pre_act, norm_gain, norm_bias, cotangent, counts, neighbours
):
    counts_scratch = pltpu.SMEM((SLABS * DEVS,), jnp.int32)
    grad, first, last, frames = call(
        prepare_kernel,
        (shape(B, 4, 16, C), shape(1, 4, 16, C), shape(1, 4, 16, C), shape(32, 144, 128)),
        [HBM] * 6,
        [
            counts_scratch,
            pltpu.VMEM((B, 16, 4 * C), BF16),
            pltpu.VMEM((B, 16, 4 * C), BF16),
            pltpu.VMEM((1, C), F32),
            pltpu.VMEM((1, C), F32),
            pltpu.VMEM((ROWS, C), BF16),
            pltpu.SemaphoreType.DMA((6,)),
        ],
        vmem=60,
    )(counts, pre_act, cotangent, norm_gain.reshape(1, C), norm_bias.reshape(1, C), conv_weight)

    def shifted(x, axes, count, step):
        pairs = [(i, i + step) for i in range(count) if 0 <= i + step < count]
        return lax.ppermute(x, axes, pairs)

    def flipped(x):
        return lax.ppermute(x, "c", [(0, 1), (1, 0)])

    slab_low = shifted(grad, SLAB, SLABS, 1)
    slab_high = shifted(grad, SLAB, SLABS, -1)
    dev_low = shifted(last, DEV, DEVS, 1)
    dev_high = shifted(first, DEV, DEVS, -1)

    frames, slab_low, slab_high, dev_low, dev_high = lax.optimization_barrier(
        (frames, slab_low, slab_high, dev_low, dev_high)
    )
    frames = swap(frames, ("zh", "y"))

    fine_scratch = pltpu.VMEM((256, 768), BF16)
    taps_scratch = pltpu.VMEM((3456, C), BF16)
    weight_scratch = pltpu.VMEM((C, 768), BF16)
    merge_weight = merge_weight.T
    keep, send, taps = call(
        conv_kernel,
        (shape(SLABS, COLS, HALF), shape(SLABS, COLS, HALF), shape(3456, C)),
        [HBM] * 4 + [VMEM] * 5,
        [
            counts_scratch,
            pltpu.SMEM((B, 27), jnp.int32),
            fine_scratch,
            weight_scratch,
            pltpu.SemaphoreType.DMA((5,)),
            pltpu.VMEM((15, 4, 16, C), BF16),
            pltpu.VMEM((6, 144, C), BF16),
            pltpu.VMEM((2, C, HALF), F32),
            taps_scratch,
        ],
        flops=6 * 10**9,
        out_spec=(VMEM, VMEM, HBM),
    )(
        counts, neighbours, fine_input, merge_weight, grad, slab_low, slab_high, dev_low, dev_high
    )

    conv = call(split_kernel, (shape(2, COLS, HALF),) * 4, [VMEM] * 2)(keep, flipped(send))
    conv = [conv[0]] + [
        lax.ppermute(conv[dx], "x", [(i, (i + dx) % 4) for i in range(4)]) for dx in (1, 2, 3)
    ]
    keep, send = call(halve_kernel, (shape(COLS, HALF),) * 2, [VMEM] * 4)(*conv)
    conv = (keep, lax.ppermute(send, "zl", [(0, 1), (1, 0)]))
    frames, conv = lax.optimization_barrier((frames, conv))

    other = flipped(frames)
    fine_grad, keep, send = call(
        back_kernel,
        (shape(256, 768), shape(576, 128), shape(576, 128)),
        [HBM] * 4 + [VMEM] * 2,
        [
            counts_scratch,
            fine_scratch,
            weight_scratch,
            taps_scratch,
            pltpu.SemaphoreType.DMA((4,)),
            pltpu.VMEM((2, 32, 144, 128), BF16),
            pltpu.VMEM((27 * C, C), BF16),
            pltpu.VMEM((2, 576, 128), BF16),
        ],
        flops=4 * 10**9,
        vmem=48,
    )(counts, fine_input, merge_weight, taps, frames, other)

    joined = call(join_kernel, shape(32, 2, 24, 128), [VMEM] * 4)(
        keep.reshape(24, 24, 128), flipped(send).reshape(24, 24, 128), *conv
    )
    joined = swap(joined, ("zh", "y"))
    conv_grad, term = call(
        part_kernel, (shape(ROWS, COLS, dtype=F32), shape(SLABS, 24, 128)), [VMEM]
    )(joined)
    term = swap(term, SLAB)
    term = call(spread_kernel, shape(32, 24, 128), [VMEM])(term)
    term = swap(term, ("zh", "y"))
    term = lax.all_gather(term, "c", axis=0, tiled=False)
    merge_grad = call(
        merge_kernel,
        shape(C, 768, dtype=F32),
        [VMEM],
        [pltpu.VMEM((C, 768), F32), pltpu.SemaphoreType.DMA((1,))],
        out_spec=HBM,
    )(term.reshape(2, 768, 128)).T
    return fine_grad, merge_grad, conv_grad


def solution(mesh):
    fine_mesh = Mesh(mesh.devices.reshape(SIZES), AXES)
    every = SLAB + DEV
    in_specs = (
        P(every, None),
        P(),
        P(DEV, None),
        P(every, None, None),
        P(),
        P(),
        P(every, None, None),
        P(),
        P(every, None),
    )
    out_specs = (P(every, None), P(), P(DEV, SLAB))
    return jax.shard_map(
        local, mesh=fine_mesh, in_specs=in_specs, out_specs=out_specs, check_vma=False
    )
```

```python
import jax
import jax.numpy as jnp
from jax import lax
from jax.experimental import pallas as pl
from jax.experimental.pallas import tpu as pltpu
from jax.sharding import Mesh, PartitionSpec as P

F32 = jnp.float32
BF16 = jnp.bfloat16

AXES = ("zl", "x", "zh", "y", "c")
SIZES = (2, 4, 4, 8, 2)
SLAB = ("zl", "x")
DEV = ("zh", "y", "c")
SLABS = 8
DEVS = 64
B = 4
C = 192
ROWS = 81
FRAME = 96
HALF = 32 * ROWS
COLS = C // SLABS

VMEM = pl.BlockSpec(memory_space=pltpu.VMEM)
HBM = pl.BlockSpec(memory_space=pltpu.HBM)


def dot(a, b):
    return jnp.dot(a, b, preferred_element_type=F32)


def my_place():
    place = lax.axis_index(AXES[0])
    for axis, size in zip(AXES[1:], SIZES[1:]):
        place = place * size + lax.axis_index(axis)
    return place


def iota(rows, cols, dim):
    return lax.broadcasted_iota(jnp.int32, (rows, cols), dim)


def ones_where(condition):
    return jnp.where(condition, 1.0, 0.0).astype(BF16)


def place_in_nine(start, v):
    p = start + v
    brick = jnp.where(p == 0, 0, jnp.where(p == 5, 2, 1))
    return brick, jnp.where(p == 0, 3, jnp.where(p == 5, 0, p - 1))


def window_matrix():
    row, col = iota(144, 144, 0), iota(144, 144, 1)
    s = lax.shift_right_logical(row, 4)
    sx = jnp.where(s >= 6, 2, jnp.where(s >= 3, 1, 0))
    v = jnp.bitwise_and(row, 15)
    kx, x = place_in_nine(sx, lax.shift_right_logical(v, 2))
    ky, y = place_in_nine(s - 3 * sx, jnp.bitwise_and(v, 3))
    return ones_where(col == (kx * 3 + ky) * 16 + x * 4 + y)


def row_order(inverse):
    inner, outer = iota(256, 256, int(inverse)), iota(256, 256, int(not inverse))
    return ones_where(
        outer == jnp.bitwise_and(inner, 63) * 4 + lax.shift_right_logical(inner, 6)
    )


def fetch(sems, *pairs):
    copies = [pltpu.make_async_copy(src, dst, sems.at[i]) for i, (src, dst) in enumerate(pairs)]
    for copy in copies:
        copy.start()
    return copies


def tap_rows(tap):
    window = (2 - tap // 9) * 3 + 2 - tap // 3 % 3
    return (window * 6 + 2 - tap % 3) * 64


def prepare_kernel(
    counts_in, pre_in, cot_in, gain_in, bias_in, weight_in, grad, first, last, frames,
    counts, pre, cot, gain, bias, weight, sems,
):
    copies = fetch(
        sems, (counts_in, counts), (pre_in, pre), (cot_in, cot), (gain_in, gain), (bias_in, bias),
        (weight_in, weight),
    )
    place = my_place()
    copies[5].wait()
    shift = jnp.bitwise_and(place, 15)
    spread = ones_where(iota(FRAME, ROWS, 0) == iota(FRAME, ROWS, 1) + shift)
    frame = dot(spread, weight[...])
    main = frame[:, :128].astype(BF16)
    low = frame[:48, 128:].astype(BF16)
    high = frame[48:, 128:].astype(BF16)
    tail = jnp.concatenate([low, high], axis=1)
    for i in range(32):
        frames[i, :FRAME] = main
        frames[i, FRAME:] = tail
    for copy in copies[:5]:
        copy.wait()
    count = counts[place]
    g = gain[...]
    for b in range(B):
        p = pre[b].astype(F32)
        u = cot[b].astype(F32)
        for z in range(4):
            pz = p[:, z * C : (z + 1) * C]
            uz = u[:, z * C : (z + 1) * C]
            gate = (g * pz + bias[...] > 0) & (b < count)
            grad[b, z] = jnp.where(gate, uz * g, 0.0).astype(BF16)
    first[0] = grad[0]
    last[0] = grad[count - 1]


def conv_kernel(
    counts_in, near_in, fine_in, weight_in, grad, slab_low, slab_high, dev_low, dev_high,
    keep, send, taps, counts, near, fine, weight, sems, bricks, block, total,
):
    copies = fetch(
        sems, (counts_in, counts), (near_in, near), (fine_in, fine), (weight_in, weight)
    )
    place = my_place()
    bricks[0:4] = grad[...]
    bricks[4:8] = slab_low[...]
    bricks[8:12] = slab_high[...]
    bricks[12:13] = dev_low[...]
    bricks[13:14] = dev_high[...]
    bricks[14:15] = jnp.zeros((1, 4, 16, C), BF16)
    window = window_matrix()
    copies[1].wait()
    for b in range(B):
        slots = []
        for k in range(27):
            brick = near[b, k]
            away = lax.shift_right_arithmetic(brick, 2) - place
            slot = jnp.bitwise_and(brick, 3)
            at = jnp.where(away == 0, slot, 14)
            at = jnp.where(away == -DEVS, 4 + slot, at)
            at = jnp.where(away == DEVS, 8 + slot, at)
            at = jnp.where(away == -1, 12, at)
            at = jnp.where(away == 1, 13, at)
            slots.append(jnp.where(brick < 0, 14, at))
        for plane in range(6):
            kz, z = ((0, 3), (1, 0), (1, 1), (1, 2), (1, 3), (2, 0))[plane]
            for q in range(9):
                block[plane, q * 16 : (q + 1) * 16] = bricks[slots[q * 3 + kz], z]
        for plane in range(6):
            moved = dot(window, block[plane]).astype(BF16)
            for s in range(9):
                row = ((s * 6 + plane) * B + b) * 16
                taps[row : row + 16] = moved[s * 16 : (s + 1) * 16]
    for copy in (copies[0], copies[2], copies[3]):
        copy.wait()
    count = counts[place]
    merged = lax.dot_general(
        fine[...], weight[...], (((1,), (1,)), ((), ())), preferred_element_type=F32
    )
    brick_of = lax.broadcasted_iota(jnp.int32, (256, C), 0) // 64
    merged = jnp.where(brick_of < count, merged, 0.0).astype(BF16)
    merged = jnp.transpose(dot(row_order(False), merged)).astype(BF16)
    for tap in range(27):
        row = tap_rows(tap)
        term = dot(merged, taps[row : row + 256])
        at = tap * C
        end = at + C
        while at < end:
            owner = at // ROWS
            stop = min(end, (owner + 1) * ROWS)
            to = (owner // 2) * ROWS + at % ROWS
            total[owner % 2, :, to : to + stop - at] = term[:, at - tap * C : stop - tap * C]
            at = stop
    core = jnp.bitwise_and(place, 1)
    for out, half in ((keep, core), (send, 1 - core)):
        for slab in range(SLABS):
            out[slab] = total[half, slab * COLS : (slab + 1) * COLS].astype(BF16)


def split_kernel(keep, received, *outs):
    x = lax.axis_index("x")
    for dx, out in enumerate(outs):
        for zl in range(2):
            slab = zl * 4 + jnp.bitwise_and(x + dx, 3)
            out[zl] = (keep[slab].astype(F32) + received[slab].astype(F32)).astype(BF16)


def halve_kernel(a, b, c, d, keep, send):
    zl = lax.axis_index("zl")
    for out, half in ((keep, zl), (send, 1 - zl)):
        total = a[half].astype(F32) + b[half].astype(F32) + c[half].astype(F32)
        out[...] = (total + d[half].astype(F32)).astype(BF16)


def back_kernel(
    counts_in, fine_in, weight_in, taps, mine, other, fine_grad, keep, send,
    counts, fine, weight, sems, both, whole, term,
):
    copies = fetch(sems, (counts_in, counts), (fine_in, fine), (weight_in, weight))
    place = my_place()
    core = jnp.bitwise_and(place, 1)
    both[core] = mine[...]
    both[1 - core] = other[...]
    for owner in range(DEVS):
        tile = ROWS * owner // 16
        frame = both.at[owner % 2, owner // 2]
        main = frame[:FRAME]
        low = frame[FRAME:, :64]
        high = frame[FRAME:, 64:]
        row = tile * 16
        if owner % 16:
            whole[row : row + 16, :128] = whole[row : row + 16, :128] + main[:16]
            whole[row : row + 16, 128:] = whole[row : row + 16, 128:] + low[:16]
            whole[row + 16 : row + FRAME, :128] = main[16:]
            whole[row + 16 : row + 48, 128:] = low[16:]
        else:
            whole[row : row + FRAME, :128] = main
            whole[row : row + 48, 128:] = low
        whole[row + 48 : row + FRAME, 128:] = high
    back = jnp.zeros((256, C), F32)
    for tap in range(27):
        row = tap_rows(tap)
        back = back + dot(taps[row : row + 256], whole[tap * C : (tap + 1) * C])
    brick_of = lax.broadcasted_iota(jnp.int32, (256, C), 0) // 16 % B
    for copy in copies:
        copy.wait()
    count = counts[place]
    back = jnp.where(brick_of < count, back, 0.0).astype(BF16)
    back = dot(row_order(True), back)
    gm = back.astype(BF16)
    fine_grad[...] = dot(gm, weight[...]).astype(BF16)
    result = dot(jnp.transpose(back).astype(BF16), fine[...]).astype(BF16)
    for part in range(6):
        row = part % 3 * C
        term[part // 3, row : row + C] = result[:, part * 128 : (part + 1) * 128]
    keep[...] = term[core]
    send[...] = term[1 - core]


def join_kernel(keep, received, out):
    for i in range(24):
        out[i] = (keep[i].astype(F32) + received[i].astype(F32)).astype(BF16)
    for i in range(24, 32):
        out[i] = jnp.zeros((24, 128), BF16)


def spread_kernel(parts, out):
    total = parts[0].astype(F32)
    for i in range(1, parts.shape[0]):
        total = total + parts[i].astype(F32)
    for i in range(out.shape[0]):
        out[i] = total.astype(BF16)


def both_kernel(parts, keep, received, out):
    merge = parts[0].astype(F32)
    for i in range(1, SLABS):
        merge = merge + parts[i].astype(F32)
    conv = keep[...].astype(F32) + received[...].astype(F32)
    pad = jnp.zeros((COLS, 128 - ROWS), BF16)
    for i in range(32):
        piece = conv[:, i * ROWS : (i + 1) * ROWS].astype(BF16)
        out[i, 0] = jnp.concatenate([piece, pad], axis=1)
        out[i, 1] = merge.astype(BF16)


def part_kernel(parts, conv_grad, merge):
    conv = parts[0, 0].astype(F32)
    for i in range(1, 32):
        conv = conv + parts[i, 0].astype(F32)
    conv_grad[...] = jnp.transpose(conv)[:ROWS]
    for i in range(32):
        merge[i] = parts[i, 1]


def merge_kernel(parts, out, held, sems):
    for part in range(6):
        row = part % 3 * C
        block = parts[part // 3, row : row + C]
        held[:, part * 128 : (part + 1) * 128] = block.astype(F32)
    copy = pltpu.make_async_copy(held, out, sems.at[0])
    copy.start()
    copy.wait()


def call(kernel, outs, specs, scratch=(), flops=0, out_spec=None, vmem=20):
    return pl.pallas_call(
        kernel,
        out_shape=outs,
        in_specs=specs,
        out_specs=out_spec or jax.tree.map(lambda _: VMEM, outs),
        scratch_shapes=scratch,
        cost_estimate=pl.CostEstimate(flops=flops, bytes_accessed=0, transcendentals=0),
        compiler_params=pltpu.CompilerParams(vmem_limit_bytes=vmem << 20),
    )


def shape(*dims, dtype=BF16):
    return jax.ShapeDtypeStruct(dims, dtype)


def swap(x, axes):
    return lax.all_to_all(x, axes, 0, 0, tiled=True)


def local(
    fine_input, merge_weight, conv_weight, pre_act, norm_gain, norm_bias, cotangent, counts, neighbours
):
    counts_scratch = pltpu.SMEM((SLABS * DEVS,), jnp.int32)
    grad, first, last, frames = call(
        prepare_kernel,
        (shape(B, 4, 16, C), shape(1, 4, 16, C), shape(1, 4, 16, C), shape(32, 144, 128)),
        [HBM] * 6,
        [
            counts_scratch,
            pltpu.VMEM((B, 16, 4 * C), BF16),
            pltpu.VMEM((B, 16, 4 * C), BF16),
            pltpu.VMEM((1, C), F32),
            pltpu.VMEM((1, C), F32),
            pltpu.VMEM((ROWS, C), BF16),
            pltpu.SemaphoreType.DMA((6,)),
        ],
        vmem=60,
    )(counts, pre_act, cotangent, norm_gain.reshape(1, C), norm_bias.reshape(1, C), conv_weight)

    def shifted(x, axes, count, step):
        pairs = [(i, i + step) for i in range(count) if 0 <= i + step < count]
        return lax.ppermute(x, axes, pairs)

    def flipped(x):
        return lax.ppermute(x, "c", [(0, 1), (1, 0)])

    slab_low = shifted(grad, SLAB, SLABS, 1)
    slab_high = shifted(grad, SLAB, SLABS, -1)
    dev_low = shifted(last, DEV, DEVS, 1)
    dev_high = shifted(first, DEV, DEVS, -1)

    frames, dev_low, dev_high = lax.optimization_barrier((frames, dev_low, dev_high))
    frames = swap(frames, ("zh", "y"))

    fine_scratch = pltpu.VMEM((256, 768), BF16)
    weight_scratch = pltpu.VMEM((C, 768), BF16)
    merge_weight = merge_weight.T
    keep, send, taps = call(
        conv_kernel,
        (shape(SLABS, COLS, HALF), shape(SLABS, COLS, HALF), shape(3456, C)),
        [HBM] * 4 + [VMEM] * 5,
        [
            counts_scratch,
            pltpu.SMEM((B, 27), jnp.int32),
            fine_scratch,
            weight_scratch,
            pltpu.SemaphoreType.DMA((4,)),
            pltpu.VMEM((15, 4, 16, C), BF16),
            pltpu.VMEM((6, 144, C), BF16),
            pltpu.VMEM((2, C, HALF), F32),
        ],
        flops=6 * 10**9,
        vmem=20,
    )(
        counts, neighbours, fine_input, merge_weight, grad, slab_low, slab_high, dev_low, dev_high
    )

    frames, received = lax.optimization_barrier((frames, flipped(send)))
    conv = call(split_kernel, (shape(2, COLS, HALF),) * 4, [VMEM] * 2)(keep, received)
    conv = [conv[0]] + [
        lax.ppermute(conv[dx], "x", [(i, (i + dx) % 4) for i in range(4)]) for dx in (1, 2, 3)
    ]
    keep, send = call(halve_kernel, (shape(COLS, HALF),) * 2, [VMEM] * 4)(*conv)
    conv = (keep, lax.ppermute(send, "zl", [(0, 1), (1, 0)]))
    other = flipped(frames)
    fine_grad, keep, send = call(
        back_kernel,
        (shape(256, 768), shape(576, 128), shape(576, 128)),
        [HBM] * 3 + [VMEM] * 3,
        [
            counts_scratch,
            fine_scratch,
            weight_scratch,
            pltpu.SemaphoreType.DMA((3,)),
            pltpu.VMEM((2, 32, 144, 128), BF16),
            pltpu.VMEM((27 * C, C), BF16),
            pltpu.VMEM((2, 576, 128), BF16),
        ],
        flops=4 * 10**9,
        vmem=20,
    )(counts, fine_input, merge_weight, taps, frames, other)

    term = call(join_kernel, shape(32, 24, 128), [VMEM] * 2)(
        keep.reshape(24, 24, 128), flipped(send).reshape(24, 24, 128)
    )
    term = swap(term, ("zh", "y"))
    term = call(spread_kernel, shape(SLABS, 24, 128), [VMEM])(term)
    term = swap(term, SLAB)
    joined = call(both_kernel, shape(32, 2, 24, 128), [VMEM] * 3)(term, *conv)
    joined = swap(joined, ("zh", "y"))
    conv_grad, term = call(
        part_kernel, (shape(ROWS, COLS, dtype=F32), shape(32, 24, 128)), [VMEM]
    )(joined)
    term = lax.all_gather(term, "c", axis=0, tiled=False)
    merge_grad = call(
        merge_kernel,
        shape(C, 768, dtype=F32),
        [VMEM],
        [pltpu.VMEM((C, 768), F32), pltpu.SemaphoreType.DMA((1,))],
        out_spec=HBM,
    )(term.reshape(2, 768, 128)).T
    return fine_grad, merge_grad, conv_grad


def solution(mesh):
    fine_mesh = Mesh(mesh.devices.reshape(SIZES), AXES)
    every = SLAB + DEV
    in_specs = (
        P(every, None),
        P(),
        P(DEV, None),
        P(every, None, None),
        P(),
        P(),
        P(every, None, None),
        P(),
        P(every, None),
    )
    out_specs = (P(every, None), P(), P(DEV, SLAB))
    return jax.shard_map(
        local, mesh=fine_mesh, in_specs=in_specs, out_specs=out_specs, check_vma=False
    )
```

```python
import jax
import jax.numpy as jnp
from jax import lax
from jax.experimental import pallas as pl
from jax.experimental.pallas import tpu as pltpu
from jax.sharding import Mesh, PartitionSpec as P

F32 = jnp.float32
BF16 = jnp.bfloat16

AXES = ("zl", "x", "zh", "y", "c")
SIZES = (2, 4, 4, 8, 2)
SLAB = ("zl", "x")
DEV = ("zh", "y", "c")
SLABS = 8
DEVS = 64
B = 4
C = 192
ROWS = 81
FRAME = 80
HALF = 32 * ROWS
COLS = C // SLABS

VMEM = pl.BlockSpec(memory_space=pltpu.VMEM)
HBM = pl.BlockSpec(memory_space=pltpu.HBM)


def dot(a, b):
    return jnp.dot(a, b, preferred_element_type=F32)


def my_place():
    place = lax.axis_index(AXES[0])
    for axis, size in zip(AXES[1:], SIZES[1:]):
        place = place * size + lax.axis_index(axis)
    return place


def repeat_kernel(block, out):
    for i in range(out.shape[0]):
        out[i] = block[...]


def iota(rows, cols, dim):
    return lax.broadcasted_iota(jnp.int32, (rows, cols), dim)


def ones_where(condition):
    return jnp.where(condition, 1.0, 0.0).astype(BF16)


def place_in_nine(start, v):
    p = start + v
    brick = jnp.where(p == 0, 0, jnp.where(p == 5, 2, 1))
    return brick, jnp.where(p == 0, 3, jnp.where(p == 5, 0, p - 1))


def window_matrix():
    row, col = iota(144, 144, 0), iota(144, 144, 1)
    s = lax.shift_right_logical(row, 4)
    sx = jnp.where(s >= 6, 2, jnp.where(s >= 3, 1, 0))
    v = jnp.bitwise_and(row, 15)
    kx, x = place_in_nine(sx, lax.shift_right_logical(v, 2))
    ky, y = place_in_nine(s - 3 * sx, jnp.bitwise_and(v, 3))
    return ones_where(col == (kx * 3 + ky) * 16 + x * 4 + y)


def row_order(inverse):
    inner, outer = iota(256, 256, int(inverse)), iota(256, 256, int(not inverse))
    return ones_where(
        outer == jnp.bitwise_and(inner, 63) * 4 + lax.shift_right_logical(inner, 6)
    )


def fetch(sems, *pairs):
    copies = [pltpu.make_async_copy(src, dst, sems.at[i]) for i, (src, dst) in enumerate(pairs)]
    for copy in copies:
        copy.start()
    return copies


def tap_rows(tap):
    window = (2 - tap // 9) * 3 + 2 - tap // 3 % 3
    return (window * 6 + 2 - tap % 3) * 64


def prepare_kernel(
    counts_in, pre_in, cot_in, gain_in, bias_in, weight_in, grad, first, last, frames,
    counts, pre, cot, gain, bias, weight, tiles, sems,
):
    copies = fetch(
        sems, (counts_in, counts), (pre_in, pre), (cot_in, cot), (gain_in, gain), (bias_in, bias),
        (weight_in, weight),
    )
    place = my_place()
    copies[5].wait()
    shift = jnp.bitwise_and(place, 15)
    at = iota(FRAME, ROWS, 1) + shift
    turned = jnp.where(at >= FRAME, at - FRAME, at)
    spread = ones_where((iota(FRAME, ROWS, 0) == turned) & (iota(FRAME, ROWS, 1) < FRAME))
    turned = dot(spread, weight[...])
    for i in range(5):
        tiles[i] = turned[i * 16 : (i + 1) * 16, :128].astype(BF16)
    extra = dot(ones_where(iota(16, ROWS, 1) == ROWS - 1), weight[...])
    row = iota(16, 64, 0)
    extra = jnp.where(
        row == 0, extra[:, :64], jnp.where(row == 1, extra[:, 64:128], extra[:, 128:])
    )
    tails = [turned[i * 16 : (i + 1) * 16, 128:] for i in range(5)] + [extra]
    for i in range(3):
        pair = jnp.concatenate([tails[2 * i], tails[2 * i + 1]], axis=1)
        tiles[5 + i] = pair.astype(BF16)
    mine = tiles[lax.shift_right_logical(place, 6)]
    for i in range(32):
        frames[i] = mine
    for copy in copies[:5]:
        copy.wait()
    count = counts[place]
    g = gain[...]
    for b in range(B):
        p = pre[b].astype(F32)
        u = cot[b].astype(F32)
        for z in range(4):
            pz = p[:, z * C : (z + 1) * C]
            uz = u[:, z * C : (z + 1) * C]
            gate = (g * pz + bias[...] > 0) & (b < count)
            grad[b, z] = jnp.where(gate, uz * g, 0.0).astype(BF16)
    first[0] = grad[0]
    last[0] = grad[count - 1]


def conv_kernel(
    counts_in, near_in, fine_in, weight_in, grad, slab_low, slab_high, dev_low, dev_high,
    keep, send, taps, counts, near, fine, weight, sems, bricks, block, total,
):
    copies = fetch(
        sems, (counts_in, counts), (near_in, near), (fine_in, fine), (weight_in, weight)
    )
    place = my_place()
    bricks[0:4] = grad[...]
    bricks[4:8] = slab_low[...]
    bricks[8:12] = slab_high[...]
    bricks[12:13] = dev_low[...]
    bricks[13:14] = dev_high[...]
    bricks[14:15] = jnp.zeros((1, 4, 16, C), BF16)
    window = window_matrix()
    copies[1].wait()
    for b in range(B):
        slots = []
        for k in range(27):
            brick = near[b, k]
            away = lax.shift_right_arithmetic(brick, 2) - place
            slot = jnp.bitwise_and(brick, 3)
            at = jnp.where(away == 0, slot, 14)
            at = jnp.where(away == -DEVS, 4 + slot, at)
            at = jnp.where(away == DEVS, 8 + slot, at)
            at = jnp.where(away == -1, 12, at)
            at = jnp.where(away == 1, 13, at)
            slots.append(jnp.where(brick < 0, 14, at))
        for plane in range(6):
            kz, z = ((0, 3), (1, 0), (1, 1), (1, 2), (1, 3), (2, 0))[plane]
            for q in range(9):
                block[plane, q * 16 : (q + 1) * 16] = bricks[slots[q * 3 + kz], z]
        for plane in range(6):
            moved = dot(window, block[plane]).astype(BF16)
            for s in range(9):
                row = ((s * 6 + plane) * B + b) * 16
                taps[row : row + 16] = moved[s * 16 : (s + 1) * 16]
    for copy in (copies[0], copies[2], copies[3]):
        copy.wait()
    count = counts[place]
    merged = lax.dot_general(
        fine[...], weight[...], (((1,), (1,)), ((), ())), preferred_element_type=F32
    )
    brick_of = lax.broadcasted_iota(jnp.int32, (256, C), 0) // 64
    merged = jnp.where(brick_of < count, merged, 0.0).astype(BF16)
    merged = jnp.transpose(dot(row_order(False), merged)).astype(BF16)
    for tap in range(27):
        row = tap_rows(tap)
        term = dot(merged, taps[row : row + 256])
        at = tap * C
        end = at + C
        while at < end:
            owner = at // ROWS
            stop = min(end, (owner + 1) * ROWS)
            to = (owner // 2) * ROWS + at % ROWS
            total[owner % 2, :, to : to + stop - at] = term[:, at - tap * C : stop - tap * C]
            at = stop
    core = jnp.bitwise_and(place, 1)
    for out, half in ((keep, core), (send, 1 - core)):
        for slab in range(SLABS):
            out[slab] = total[half, slab * COLS : (slab + 1) * COLS].astype(BF16)


def split_kernel(keep, received, *outs):
    x = lax.axis_index("x")
    for dx, out in enumerate(outs):
        for zl in range(2):
            slab = zl * 4 + jnp.bitwise_and(x + dx, 3)
            out[zl] = (keep[slab].astype(F32) + received[slab].astype(F32)).astype(BF16)


def halve_kernel(a, b, c, d, keep, send):
    zl = lax.axis_index("zl")
    for out, half in ((keep, zl), (send, 1 - zl)):
        total = a[half].astype(F32) + b[half].astype(F32) + c[half].astype(F32)
        out[...] = (total + d[half].astype(F32)).astype(BF16)


def back_kernel(
    counts_in, fine_in, weight_in, taps, mine, other, fine_grad, keep, send,
    counts, fine, weight, sems, both, whole, term,
):
    copies = fetch(sems, (counts_in, counts), (fine_in, fine), (weight_in, weight))
    place = my_place()
    core = jnp.bitwise_and(place, 1)
    both[core] = mine[...]
    both[1 - core] = other[...]
    row = iota(16, 128, 0)
    held = None
    for owner in range(DEVS):
        first = ROWS * owner // 16 * 16
        shift = owner % 16
        tiles = [both[owner % 2, i, owner // 2] for i in range(SLABS)]
        for i in range(1, 5):
            whole[first + i * 16 : first + (i + 1) * 16, :128] = tiles[i]
            half = i % 2 * 64
            whole[first + i * 16 : first + (i + 1) * 16, 128:] = tiles[5 + i // 2][
                :, half : half + 64
            ]
        main, tail = tiles[0].astype(F32), tiles[5][:, :64].astype(F32)
        extra = tiles[7][:, 64:].astype(F32)
        long = jnp.concatenate([extra[0:1], extra[1:2]], axis=1)
        ends = [jnp.where(row < shift, main, jnp.where(row == shift, long, 0.0))]
        short = row[:, :64]
        ends.append(jnp.where(short < shift, tail, jnp.where(short == shift, extra[2:3], 0.0)))
        if shift:
            main = jnp.where(row >= shift, main, held[0])
            tail = jnp.where(short >= shift, tail, held[1])
        whole[first : first + 16, :128] = main.astype(BF16)
        whole[first : first + 16, 128:] = tail.astype(BF16)
        if shift == 15:
            whole[first + 80 : first + 96, :128] = ends[0].astype(BF16)
            whole[first + 80 : first + 96, 128:] = ends[1].astype(BF16)
        held = ends
    back = jnp.zeros((256, C), F32)
    for tap in range(27):
        row = tap_rows(tap)
        back = back + dot(taps[row : row + 256], whole[tap * C : (tap + 1) * C])
    brick_of = lax.broadcasted_iota(jnp.int32, (256, C), 0) // 16 % B
    for copy in copies:
        copy.wait()
    count = counts[place]
    back = jnp.where(brick_of < count, back, 0.0).astype(BF16)
    back = dot(row_order(True), back)
    gm = back.astype(BF16)
    fine_grad[...] = dot(gm, weight[...]).astype(BF16)
    result = dot(jnp.transpose(back).astype(BF16), fine[...]).astype(BF16)
    for part in range(6):
        row = part % 3 * C
        term[part // 3, row : row + C] = result[:, part * 128 : (part + 1) * 128]
    keep[...] = term[core]
    send[...] = term[1 - core]


def join_kernel(keep, received, out):
    for i in range(24):
        out[i] = (keep[i].astype(F32) + received[i].astype(F32)).astype(BF16)
    for i in range(24, 32):
        out[i] = jnp.zeros((24, 128), BF16)


def spread_kernel(parts, out):
    total = parts[0].astype(F32)
    for i in range(1, parts.shape[0]):
        total = total + parts[i].astype(F32)
    for i in range(out.shape[0]):
        out[i] = total.astype(BF16)


def both_kernel(parts, keep, received, out):
    merge = parts[0].astype(F32)
    for i in range(1, SLABS):
        merge = merge + parts[i].astype(F32)
    conv = keep[...].astype(F32) + received[...].astype(F32)
    pad = jnp.zeros((COLS, 128 - ROWS), BF16)
    for i in range(32):
        piece = conv[:, i * ROWS : (i + 1) * ROWS].astype(BF16)
        out[i, 0] = jnp.concatenate([piece, pad], axis=1)
        out[i, 1] = merge.astype(BF16)


def part_kernel(parts, conv_grad, merge):
    conv = parts[0, 0].astype(F32)
    for i in range(1, 32):
        conv = conv + parts[i, 0].astype(F32)
    conv_grad[...] = jnp.transpose(conv)[:ROWS]
    for i in range(32):
        merge[i] = parts[i, 1]


def merge_kernel(parts, out, held, sems):
    for part in range(6):
        row = part % 3 * C
        block = parts[part // 3, row : row + C]
        held[:, part * 128 : (part + 1) * 128] = block.astype(F32)
    copy = pltpu.make_async_copy(held, out, sems.at[0])
    copy.start()
    copy.wait()


def call(kernel, outs, specs, scratch=(), flops=0, out_spec=None, vmem=20):
    return pl.pallas_call(
        kernel,
        out_shape=outs,
        in_specs=specs,
        out_specs=out_spec or jax.tree.map(lambda _: VMEM, outs),
        scratch_shapes=scratch,
        cost_estimate=pl.CostEstimate(flops=flops, bytes_accessed=0, transcendentals=0),
        compiler_params=pltpu.CompilerParams(vmem_limit_bytes=vmem << 20),
    )


def shape(*dims, dtype=BF16):
    return jax.ShapeDtypeStruct(dims, dtype)


def swap(x, axes):
    return lax.all_to_all(x, axes, 0, 0, tiled=True)


def local(
    fine_input, merge_weight, conv_weight, pre_act, norm_gain, norm_bias, cotangent, counts, neighbours
):
    counts_scratch = pltpu.SMEM((SLABS * DEVS,), jnp.int32)
    grad, first, last, frames = call(
        prepare_kernel,
        (shape(B, 4, 16, C), shape(1, 4, 16, C), shape(1, 4, 16, C), shape(32, 16, 128)),
        [HBM] * 6,
        [
            counts_scratch,
            pltpu.VMEM((B, 16, 4 * C), BF16),
            pltpu.VMEM((B, 16, 4 * C), BF16),
            pltpu.VMEM((1, C), F32),
            pltpu.VMEM((1, C), F32),
            pltpu.VMEM((ROWS, C), BF16),
            pltpu.VMEM((SLABS, 16, 128), BF16),
            pltpu.SemaphoreType.DMA((6,)),
        ],
        vmem=60,
    )(counts, pre_act, cotangent, norm_gain.reshape(1, C), norm_bias.reshape(1, C), conv_weight)

    def shifted(x, axes, count, step):
        pairs = [(i, i + step) for i in range(count) if 0 <= i + step < count]
        return lax.ppermute(x, axes, pairs)

    def flipped(x):
        return lax.ppermute(x, "c", [(0, 1), (1, 0)])

    slab_low = shifted(grad, SLAB, SLABS, 1)
    slab_high = shifted(grad, SLAB, SLABS, -1)
    dev_low = shifted(last, DEV, DEVS, 1)
    dev_high = shifted(first, DEV, DEVS, -1)

    frames = swap(frames, ("zh", "y"))
    frames, slab_low, slab_high, dev_low, dev_high = lax.optimization_barrier(
        (frames, slab_low, slab_high, dev_low, dev_high)
    )
    frames = call(repeat_kernel, shape(SLABS, 32, 16, 128), [VMEM])(frames)
    frames = swap(frames, SLAB)

    fine_scratch = pltpu.VMEM((256, 768), BF16)
    weight_scratch = pltpu.VMEM((C, 768), BF16)
    merge_weight = merge_weight.T
    keep, send, taps = call(
        conv_kernel,
        (shape(SLABS, COLS, HALF), shape(SLABS, COLS, HALF), shape(3456, C)),
        [HBM] * 4 + [VMEM] * 5,
        [
            counts_scratch,
            pltpu.SMEM((B, 27), jnp.int32),
            fine_scratch,
            weight_scratch,
            pltpu.SemaphoreType.DMA((4,)),
            pltpu.VMEM((15, 4, 16, C), BF16),
            pltpu.VMEM((6, 144, C), BF16),
            pltpu.VMEM((2, C, HALF), F32),
        ],
        flops=6 * 10**9,
        vmem=20,
    )(
        counts, neighbours, fine_input, merge_weight, grad, slab_low, slab_high, dev_low, dev_high
    )

    frames, received = lax.optimization_barrier((frames, flipped(send)))
    conv = call(split_kernel, (shape(2, COLS, HALF),) * 4, [VMEM] * 2)(keep, received)
    conv = [conv[0]] + [
        lax.ppermute(conv[dx], "x", [(i, (i + dx) % 4) for i in range(4)]) for dx in (1, 2, 3)
    ]
    keep, send = call(halve_kernel, (shape(COLS, HALF),) * 2, [VMEM] * 4)(*conv)
    conv = (keep, lax.ppermute(send, "zl", [(0, 1), (1, 0)]))
    other = flipped(frames)
    fine_grad, keep, send = call(
        back_kernel,
        (shape(256, 768), shape(576, 128), shape(576, 128)),
        [HBM] * 3 + [VMEM] * 3,
        [
            counts_scratch,
            fine_scratch,
            weight_scratch,
            pltpu.SemaphoreType.DMA((3,)),
            pltpu.VMEM((2, SLABS, 32, 16, 128), BF16),
            pltpu.VMEM((27 * C, C), BF16),
            pltpu.VMEM((2, 576, 128), BF16),
        ],
        flops=4 * 10**9,
        vmem=20,
    )(counts, fine_input, merge_weight, taps, frames, other)

    term = call(join_kernel, shape(32, 24, 128), [VMEM] * 2)(
        keep.reshape(24, 24, 128), flipped(send).reshape(24, 24, 128)
    )
    term = swap(term, ("zh", "y"))
    term = call(spread_kernel, shape(SLABS, 24, 128), [VMEM])(term)
    term = swap(term, SLAB)
    joined = call(both_kernel, shape(32, 2, 24, 128), [VMEM] * 3)(term, *conv)
    joined = swap(joined, ("zh", "y"))
    conv_grad, term = call(
        part_kernel, (shape(ROWS, COLS, dtype=F32), shape(32, 24, 128)), [VMEM]
    )(joined)
    term = lax.all_gather(term, "c", axis=0, tiled=False)
    merge_grad = call(
        merge_kernel,
        shape(C, 768, dtype=F32),
        [VMEM],
        [pltpu.VMEM((C, 768), F32), pltpu.SemaphoreType.DMA((1,))],
        out_spec=HBM,
    )(term.reshape(2, 768, 128)).T
    return fine_grad, merge_grad, conv_grad


def solution(mesh):
    fine_mesh = Mesh(mesh.devices.reshape(SIZES), AXES)
    every = SLAB + DEV
    in_specs = (
        P(every, None),
        P(),
        P(DEV, None),
        P(every, None, None),
        P(),
        P(),
        P(every, None, None),
        P(),
        P(every, None),
    )
    out_specs = (P(every, None), P(), P(DEV, SLAB))
    return jax.shard_map(
        local, mesh=fine_mesh, in_specs=in_specs, out_specs=out_specs, check_vma=False
    )
```

```python
import jax
import jax.numpy as jnp
from jax import lax
from jax.experimental import pallas as pl
from jax.experimental.pallas import tpu as pltpu
from jax.sharding import Mesh, PartitionSpec as P

F32 = jnp.float32
BF16 = jnp.bfloat16

AXES = ("zl", "x", "zh", "y", "c")
SIZES = (2, 4, 4, 8, 2)
SLAB = ("zl", "x")
DEV = ("zh", "y", "c")
SLABS = 8
DEVS = 64
B = 4
C = 192
ROWS = 81
FRAME = 80
HALF = 32 * ROWS
COLS = C // SLABS
WIDE = 2688

VMEM = pl.BlockSpec(memory_space=pltpu.VMEM)
HBM = pl.BlockSpec(memory_space=pltpu.HBM)


def dot(a, b):
    return jnp.dot(a, b, preferred_element_type=F32)


def my_place():
    place = lax.axis_index(AXES[0])
    for axis, size in zip(AXES[1:], SIZES[1:]):
        place = place * size + lax.axis_index(axis)
    return place


def repeat_kernel(block, out):
    for i in range(out.shape[0]):
        out[i] = block[...]


def iota(rows, cols, dim):
    return lax.broadcasted_iota(jnp.int32, (rows, cols), dim)


def ones_where(condition):
    return jnp.where(condition, 1.0, 0.0).astype(BF16)


def place_in_nine(start, v):
    p = start + v
    brick = jnp.where(p == 0, 0, jnp.where(p == 5, 2, 1))
    return brick, jnp.where(p == 0, 3, jnp.where(p == 5, 0, p - 1))


def window_matrix():
    row, col = iota(144, 144, 0), iota(144, 144, 1)
    s = lax.shift_right_logical(row, 4)
    sx = jnp.where(s >= 6, 2, jnp.where(s >= 3, 1, 0))
    v = jnp.bitwise_and(row, 15)
    kx, x = place_in_nine(sx, lax.shift_right_logical(v, 2))
    ky, y = place_in_nine(s - 3 * sx, jnp.bitwise_and(v, 3))
    return ones_where(col == (kx * 3 + ky) * 16 + x * 4 + y)


def row_order(inverse):
    inner, outer = iota(256, 256, int(inverse)), iota(256, 256, int(not inverse))
    return ones_where(
        outer == jnp.bitwise_and(inner, 63) * 4 + lax.shift_right_logical(inner, 6)
    )


def fetch(sems, *pairs):
    copies = [pltpu.make_async_copy(src, dst, sems.at[i]) for i, (src, dst) in enumerate(pairs)]
    for copy in copies:
        copy.start()
    return copies


def tap_rows(tap):
    window = (2 - tap // 9) * 3 + 2 - tap // 3 % 3
    return (window * 6 + 2 - tap % 3) * 64


def prepare_kernel(
    counts_in, pre_in, cot_in, gain_in, bias_in, weight_in, grad, first, last, frames,
    counts, pre, cot, gain, bias, weight, tiles, sems,
):
    copies = fetch(
        sems, (counts_in, counts), (pre_in, pre), (cot_in, cot), (gain_in, gain), (bias_in, bias),
        (weight_in, weight),
    )
    place = my_place()
    copies[5].wait()
    shift = jnp.bitwise_and(place, 15)
    at = iota(FRAME, ROWS, 1) + shift
    turned = jnp.where(at >= FRAME, at - FRAME, at)
    spread = ones_where((iota(FRAME, ROWS, 0) == turned) & (iota(FRAME, ROWS, 1) < FRAME))
    turned = dot(spread, weight[...])
    for i in range(5):
        tiles[i] = turned[i * 16 : (i + 1) * 16, :128].astype(BF16)
    extra = dot(ones_where(iota(16, ROWS, 1) == ROWS - 1), weight[...])
    row = iota(16, 64, 0)
    extra = jnp.where(
        row == 0, extra[:, :64], jnp.where(row == 1, extra[:, 64:128], extra[:, 128:])
    )
    tails = [turned[i * 16 : (i + 1) * 16, 128:] for i in range(5)] + [extra]
    for i in range(3):
        pair = jnp.concatenate([tails[2 * i], tails[2 * i + 1]], axis=1)
        tiles[5 + i] = pair.astype(BF16)
    mine = tiles[lax.shift_right_logical(place, 6)]
    for i in range(32):
        frames[i] = mine
    for copy in copies[:5]:
        copy.wait()
    count = counts[place]
    g = gain[...]
    for b in range(B):
        p = pre[b].astype(F32)
        u = cot[b].astype(F32)
        for z in range(4):
            pz = p[:, z * C : (z + 1) * C]
            uz = u[:, z * C : (z + 1) * C]
            gate = (g * pz + bias[...] > 0) & (b < count)
            grad[b, z] = jnp.where(gate, uz * g, 0.0).astype(BF16)
    first[0] = grad[0]
    last[0] = grad[count - 1]


def conv_kernel(
    counts_in, near_in, fine_in, weight_in, grad, slab_low, slab_high, dev_low, dev_high,
    keep_out, send_out, taps_out, counts, near, fine, weight, sems, bricks, block, total, taps,
    keep, send,
):
    copies = fetch(
        sems, (near_in, near), (grad, bricks.at[0:4]), (slab_low, bricks.at[4:8]),
        (slab_high, bricks.at[8:12]), (dev_low, bricks.at[12:13]), (dev_high, bricks.at[13:14]),
        (counts_in, counts), (fine_in, fine), (weight_in, weight),
    )
    place = my_place()
    bricks[14:15] = jnp.zeros((1, 4, 16, C), BF16)
    window = window_matrix()
    for copy in copies[:6]:
        copy.wait()
    for b in range(B):
        slots = []
        for k in range(27):
            brick = near[b, k]
            away = lax.shift_right_arithmetic(brick, 2) - place
            slot = jnp.bitwise_and(brick, 3)
            at = jnp.where(away == 0, slot, 14)
            at = jnp.where(away == -DEVS, 4 + slot, at)
            at = jnp.where(away == DEVS, 8 + slot, at)
            at = jnp.where(away == -1, 12, at)
            at = jnp.where(away == 1, 13, at)
            slots.append(jnp.where(brick < 0, 14, at))
        for plane in range(6):
            kz, z = ((0, 3), (1, 0), (1, 1), (1, 2), (1, 3), (2, 0))[plane]
            for q in range(9):
                block[plane, q * 16 : (q + 1) * 16] = bricks[slots[q * 3 + kz], z]
        for plane in range(6):
            moved = dot(window, block[plane]).astype(BF16)
            for s in range(9):
                row = ((s * 6 + plane) * B + b) * 16
                taps[row : row + 16] = moved[s * 16 : (s + 1) * 16]
    leave = [pltpu.make_async_copy(taps, taps_out, sems.at[9])]
    leave[0].start()
    for copy in copies[6:]:
        copy.wait()
    count = counts[place]
    merged = lax.dot_general(
        fine[...], weight[...], (((1,), (1,)), ((), ())), preferred_element_type=F32
    )
    brick_of = lax.broadcasted_iota(jnp.int32, (256, C), 0) // 64
    merged = jnp.where(brick_of < count, merged, 0.0).astype(BF16)
    merged = jnp.transpose(dot(row_order(False), merged)).astype(BF16)
    for tap in range(27):
        row = tap_rows(tap)
        term = dot(merged, taps[row : row + 256])
        at = tap * C
        end = at + C
        while at < end:
            owner = at // ROWS
            stop = min(end, (owner + 1) * ROWS)
            to = (owner // 2) * ROWS + at % ROWS
            total[owner % 2, :, to : to + stop - at] = term[:, at - tap * C : stop - tap * C]
            at = stop
    core = jnp.bitwise_and(place, 1)
    for i, (held, out, half) in enumerate(((send, send_out, 1 - core), (keep, keep_out, core))):
        for slab in range(SLABS):
            held[slab] = total[half, slab * COLS : (slab + 1) * COLS].astype(BF16)
        leave.append(pltpu.make_async_copy(held, out, sems.at[10 + i]))
        leave[-1].start()
    for copy in leave:
        copy.wait()


def back_kernel(
    counts_in, fine_in, weight_in, taps_in, mine, other, fine_grad, keep, send,
    counts, fine, weight, taps, sems, both, whole, term,
):
    place = my_place()
    core = jnp.bitwise_and(place, 1)
    copies = fetch(
        sems, (mine, both.at[core]), (other, both.at[1 - core]), (taps_in, taps),
        (fine_in, fine), (weight_in, weight), (counts_in, counts),
    )
    for copy in copies[:2]:
        copy.wait()
    row = iota(16, 128, 0)
    held = None
    for owner in range(DEVS):
        first = ROWS * owner // 16 * 16
        shift = owner % 16
        tiles = [both[owner % 2, i, owner // 2] for i in range(SLABS)]
        for i in range(1, 5):
            whole[first + i * 16 : first + (i + 1) * 16, :128] = tiles[i]
            half = i % 2 * 64
            whole[first + i * 16 : first + (i + 1) * 16, 128:] = tiles[5 + i // 2][
                :, half : half + 64
            ]
        main, tail = tiles[0].astype(F32), tiles[5][:, :64].astype(F32)
        extra = tiles[7][:, 64:].astype(F32)
        long = jnp.concatenate([extra[0:1], extra[1:2]], axis=1)
        ends = [jnp.where(row < shift, main, jnp.where(row == shift, long, 0.0))]
        short = row[:, :64]
        ends.append(jnp.where(short < shift, tail, jnp.where(short == shift, extra[2:3], 0.0)))
        if shift:
            main = jnp.where(row >= shift, main, held[0])
            tail = jnp.where(short >= shift, tail, held[1])
        whole[first : first + 16, :128] = main.astype(BF16)
        whole[first : first + 16, 128:] = tail.astype(BF16)
        if shift == 15:
            whole[first + 80 : first + 96, :128] = ends[0].astype(BF16)
            whole[first + 80 : first + 96, 128:] = ends[1].astype(BF16)
        held = ends
    for copy in copies[2:]:
        copy.wait()
    back = jnp.zeros((256, C), F32)
    for tap in range(27):
        row = tap_rows(tap)
        back = back + dot(taps[row : row + 256], whole[tap * C : (tap + 1) * C])
    brick_of = lax.broadcasted_iota(jnp.int32, (256, C), 0) // 16 % B
    count = counts[place]
    back = jnp.where(brick_of < count, back, 0.0).astype(BF16)
    back = dot(row_order(True), back)
    gm = back.astype(BF16)
    fine_grad[...] = dot(gm, weight[...]).astype(BF16)
    result = dot(jnp.transpose(back).astype(BF16), fine[...]).astype(BF16)
    for part in range(6):
        row = part % 3 * C
        term[part // 3, row : row + C] = result[:, part * 128 : (part + 1) * 128]
    keep[...] = term[core]
    send[...] = term[1 - core]


def join_kernel(keep, received, out):
    for i in range(24):
        out[i] = (keep[i].astype(F32) + received[i].astype(F32)).astype(BF16)
    for i in range(24, 32):
        out[i] = jnp.zeros((24, 128), BF16)


def spread_kernel(parts, keep, received, out):
    merge = parts[0].astype(F32)
    for i in range(1, 32):
        merge = merge + parts[i].astype(F32)
    for i in range(SLABS):
        out[i, :, :HALF] = (keep[i].astype(F32) + received[i].astype(F32)).astype(BF16)
        out[i, :, HALF:WIDE] = jnp.zeros((COLS, WIDE - HALF), BF16)
        out[i, :, WIDE:] = merge.astype(BF16)


def both_kernel(parts, out):
    total = parts[0].astype(F32)
    for i in range(1, SLABS):
        total = total + parts[i].astype(F32)
    merge = total[:, WIDE:].astype(BF16)
    pad = jnp.zeros((COLS, 128 - ROWS), BF16)
    for i in range(32):
        piece = total[:, i * ROWS : (i + 1) * ROWS].astype(BF16)
        out[i, 0] = jnp.concatenate([piece, pad], axis=1)
        out[i, 1] = merge


def part_kernel(parts, conv_grad, merge):
    conv = parts[0, 0].astype(F32)
    for i in range(1, 32):
        conv = conv + parts[i, 0].astype(F32)
    conv_grad[...] = jnp.transpose(conv)[:ROWS]
    for i in range(32):
        merge[i] = parts[i, 1]


def merge_kernel(parts, out, held, sems):
    for part in range(6):
        row = part % 3 * C
        block = parts[part // 3, row : row + C]
        held[:, part * 128 : (part + 1) * 128] = block.astype(F32)
    copy = pltpu.make_async_copy(held, out, sems.at[0])
    copy.start()
    copy.wait()


def call(kernel, outs, specs, scratch=(), flops=0, out_spec=None, vmem=20):
    return pl.pallas_call(
        kernel,
        out_shape=outs,
        in_specs=specs,
        out_specs=out_spec or jax.tree.map(lambda _: VMEM, outs),
        scratch_shapes=scratch,
        cost_estimate=pl.CostEstimate(flops=flops, bytes_accessed=0, transcendentals=0),
        compiler_params=pltpu.CompilerParams(vmem_limit_bytes=vmem << 20),
    )


def shape(*dims, dtype=BF16):
    return jax.ShapeDtypeStruct(dims, dtype)


def swap(x, axes):
    return lax.all_to_all(x, axes, 0, 0, tiled=True)


def local(
    fine_input, merge_weight, conv_weight, pre_act, norm_gain, norm_bias, cotangent, counts, neighbours
):
    counts_scratch = pltpu.SMEM((SLABS * DEVS,), jnp.int32)
    grad, first, last, frames = call(
        prepare_kernel,
        (shape(B, 4, 16, C), shape(1, 4, 16, C), shape(1, 4, 16, C), shape(32, 16, 128)),
        [HBM] * 6,
        [
            counts_scratch,
            pltpu.VMEM((B, 16, 4 * C), BF16),
            pltpu.VMEM((B, 16, 4 * C), BF16),
            pltpu.VMEM((1, C), F32),
            pltpu.VMEM((1, C), F32),
            pltpu.VMEM((ROWS, C), BF16),
            pltpu.VMEM((SLABS, 16, 128), BF16),
            pltpu.SemaphoreType.DMA((6,)),
        ],
        vmem=60,
    )(counts, pre_act, cotangent, norm_gain.reshape(1, C), norm_bias.reshape(1, C), conv_weight)

    def shifted(x, axes, count, step):
        pairs = [(i, i + step) for i in range(count) if 0 <= i + step < count]
        return lax.ppermute(x, axes, pairs)

    def flipped(x):
        return lax.ppermute(x, "c", [(0, 1), (1, 0)])

    slab_low = shifted(grad, SLAB, SLABS, 1)
    slab_high = shifted(grad, SLAB, SLABS, -1)
    frames = swap(frames, ("zh", "y"))
    frames, slab_low, slab_high, first, last = lax.optimization_barrier(
        (frames, slab_low, slab_high, first, last)
    )
    dev_low = shifted(last, DEV, DEVS, 1)
    dev_high = shifted(first, DEV, DEVS, -1)
    frames = call(repeat_kernel, shape(SLABS, 32, 16, 128), [VMEM])(frames)
    frames = swap(frames, SLAB)

    fine_scratch = pltpu.VMEM((256, 768), BF16)
    weight_scratch = pltpu.VMEM((C, 768), BF16)
    merge_weight = merge_weight.T
    keep, send, taps = call(
        conv_kernel,
        (shape(SLABS, COLS, HALF), shape(SLABS, COLS, HALF), shape(3456, C)),
        [HBM] * 9,
        [
            counts_scratch,
            pltpu.SMEM((B, 27), jnp.int32),
            fine_scratch,
            weight_scratch,
            pltpu.SemaphoreType.DMA((12,)),
            pltpu.VMEM((15, 4, 16, C), BF16),
            pltpu.VMEM((6, 144, C), BF16),
            pltpu.VMEM((2, C, HALF), F32),
            pltpu.VMEM((3456, C), BF16),
            pltpu.VMEM((SLABS, COLS, HALF), BF16),
            pltpu.VMEM((SLABS, COLS, HALF), BF16),
        ],
        flops=6 * 10**9,
        out_spec=(HBM, HBM, HBM),
        vmem=60,
    )(
        counts, neighbours, fine_input, merge_weight, grad, slab_low, slab_high, dev_low, dev_high
    )

    frames, taps = lax.optimization_barrier((frames, taps))
    conv_keep, conv_send = keep, send

    other = flipped(frames)
    fine_grad, keep, send = call(
        back_kernel,
        (shape(256, 768), shape(576, 128), shape(576, 128)),
        [HBM] * 6,
        [
            counts_scratch,
            fine_scratch,
            weight_scratch,
            pltpu.VMEM((3456, C), BF16),
            pltpu.SemaphoreType.DMA((6,)),
            pltpu.VMEM((2, SLABS, 32, 16, 128), BF16),
            pltpu.VMEM((27 * C, C), BF16),
            pltpu.VMEM((2, 576, 128), BF16),
        ],
        flops=4 * 10**9,
        vmem=60,
    )(counts, fine_input, merge_weight, taps, frames, other)

    term = call(join_kernel, shape(32, 24, 128), [VMEM] * 2)(
        keep.reshape(24, 24, 128), flipped(send).reshape(24, 24, 128)
    )
    term = swap(term, ("zh", "y"))
    term = call(spread_kernel, shape(SLABS, COLS, WIDE + 128), [VMEM] * 3)(
        term, conv_keep, flipped(conv_send)
    )
    term = swap(term, SLAB)
    joined = call(both_kernel, shape(32, 2, 24, 128), [VMEM])(term)
    joined = swap(joined, ("zh", "y"))
    conv_grad, term = call(
        part_kernel, (shape(ROWS, COLS, dtype=F32), shape(32, 24, 128)), [VMEM]
    )(joined)
    term = lax.all_gather(term, "c", axis=0, tiled=False)
    merge_grad = call(
        merge_kernel,
        shape(C, 768, dtype=F32),
        [VMEM],
        [pltpu.VMEM((C, 768), F32), pltpu.SemaphoreType.DMA((1,))],
        out_spec=HBM,
    )(term.reshape(2, 768, 128)).T
    return fine_grad, merge_grad, conv_grad


def solution(mesh):
    fine_mesh = Mesh(mesh.devices.reshape(SIZES), AXES)
    every = SLAB + DEV
    in_specs = (
        P(every, None),
        P(),
        P(DEV, None),
        P(every, None, None),
        P(),
        P(),
        P(every, None, None),
        P(),
        P(every, None),
    )
    out_specs = (P(every, None), P(), P(DEV, SLAB))
    return jax.shard_map(
        local, mesh=fine_mesh, in_specs=in_specs, out_specs=out_specs, check_vma=False
    )
```

```python
import jax
import jax.numpy as jnp
from jax import lax
from jax.experimental import pallas as pl
from jax.experimental.pallas import tpu as pltpu
from jax.sharding import Mesh, PartitionSpec as P

F32 = jnp.float32
BF16 = jnp.bfloat16

AXES = ("zl", "x", "zh", "y", "c")
SIZES = (2, 4, 4, 8, 2)
SLAB = ("zl", "x")
DEV = ("zh", "y", "c")
SLABS = 8
DEVS = 64
B = 4
C = 192
ROWS = 81
FRAME = 80
HALF = 32 * ROWS
COLS = C // SLABS
PIECES = 48
WIDE = 2688

VMEM = pl.BlockSpec(memory_space=pltpu.VMEM)
HBM = pl.BlockSpec(memory_space=pltpu.HBM)


def dot(a, b):
    return jnp.dot(a, b, preferred_element_type=F32)


def my_place():
    place = lax.axis_index(AXES[0])
    for axis, size in zip(AXES[1:], SIZES[1:]):
        place = place * size + lax.axis_index(axis)
    return place


def repeat_kernel(block, out):
    for i in range(out.shape[0]):
        out[i] = block[...]


def iota(rows, cols, dim):
    return lax.broadcasted_iota(jnp.int32, (rows, cols), dim)


def ones_where(condition):
    return jnp.where(condition, 1.0, 0.0).astype(BF16)


def place_in_nine(start, v):
    p = start + v
    brick = jnp.where(p == 0, 0, jnp.where(p == 5, 2, 1))
    return brick, jnp.where(p == 0, 3, jnp.where(p == 5, 0, p - 1))


def window_matrix():
    row, col = iota(144, 144, 0), iota(144, 144, 1)
    s = lax.shift_right_logical(row, 4)
    sx = jnp.where(s >= 6, 2, jnp.where(s >= 3, 1, 0))
    v = jnp.bitwise_and(row, 15)
    kx, x = place_in_nine(sx, lax.shift_right_logical(v, 2))
    ky, y = place_in_nine(s - 3 * sx, jnp.bitwise_and(v, 3))
    return ones_where(col == (kx * 3 + ky) * 16 + x * 4 + y)


def row_order(inverse):
    inner, outer = iota(256, 256, int(inverse)), iota(256, 256, int(not inverse))
    return ones_where(
        outer == jnp.bitwise_and(inner, 63) * 4 + lax.shift_right_logical(inner, 6)
    )


def fetch(sems, *pairs):
    copies = [pltpu.make_async_copy(src, dst, sems.at[i]) for i, (src, dst) in enumerate(pairs)]
    for copy in copies:
        copy.start()
    return copies


def tap_rows(tap):
    window = (2 - tap // 9) * 3 + 2 - tap // 3 % 3
    return (window * 6 + 2 - tap % 3) * 64


def prepare_kernel(
    counts_in, pre_in, cot_in, gain_in, bias_in, weight_in, grad, near, far, frames,
    counts, pre, cot, gain, bias, weight, tiles, sems,
):
    copies = fetch(
        sems, (counts_in, counts), (pre_in, pre), (cot_in, cot), (gain_in, gain), (bias_in, bias),
        (weight_in, weight),
    )
    place = my_place()
    copies[5].wait()
    shift = jnp.bitwise_and(place, 15)
    at = iota(FRAME, ROWS, 1) + shift
    turned = jnp.where(at >= FRAME, at - FRAME, at)
    spread = ones_where((iota(FRAME, ROWS, 0) == turned) & (iota(FRAME, ROWS, 1) < FRAME))
    turned = dot(spread, weight[...])
    for i in range(5):
        tiles[i] = turned[i * 16 : (i + 1) * 16, :128].astype(BF16)
    extra = dot(ones_where(iota(16, ROWS, 1) == ROWS - 1), weight[...])
    row = iota(16, 64, 0)
    extra = jnp.where(
        row == 0, extra[:, :64], jnp.where(row == 1, extra[:, 64:128], extra[:, 128:])
    )
    tails = [turned[i * 16 : (i + 1) * 16, 128:] for i in range(5)] + [extra]
    for i in range(3):
        pair = jnp.concatenate([tails[2 * i], tails[2 * i + 1]], axis=1)
        tiles[5 + i] = pair.astype(BF16)
    mine = tiles[lax.shift_right_logical(place, 6)]
    for i in range(32):
        frames[i] = mine
    for copy in copies[:5]:
        copy.wait()
    count = counts[place]
    g = gain[...]
    for b in range(B):
        p = pre[b].astype(F32)
        u = cot[b].astype(F32)
        for z in range(4):
            pz = p[:, z * C : (z + 1) * C]
            uz = u[:, z * C : (z + 1) * C]
            gate = (g * pz + bias[...] > 0) & (b < count)
            grad[b, z] = jnp.where(gate, uz * g, 0.0).astype(BF16)
    core = jnp.bitwise_and(place, 1)
    near[0] = grad[jnp.where(core == 0, count - 1, 0)]
    far[0] = grad[jnp.where(core == 0, 0, count - 1)]


def conv_kernel(
    counts_in, near_in, fine_in, weight_in, grad, slab_low, slab_high, dev_near, dev_far,
    keep_out, send_out, taps_out, counts, near, fine, weight, sems, bricks, block, total, taps,
    keep, send,
):
    place = my_place()
    core = jnp.bitwise_and(place, 1)
    copies = fetch(
        sems, (near_in, near), (grad, bricks.at[0:4]), (slab_low, bricks.at[4:8]),
        (slab_high, bricks.at[8:12]), (dev_near, bricks.at[pl.ds(13 - core, 1)]),
        (dev_far, bricks.at[pl.ds(12 + core, 1)]),
        (counts_in, counts), (fine_in, fine), (weight_in, weight),
    )
    bricks[14:15] = jnp.zeros((1, 4, 16, C), BF16)
    window = window_matrix()
    for copy in copies[:6]:
        copy.wait()
    for b in range(B):
        slots = []
        for k in range(27):
            brick = near[b, k]
            away = lax.shift_right_arithmetic(brick, 2) - place
            slot = jnp.bitwise_and(brick, 3)
            at = jnp.where(away == 0, slot, 14)
            at = jnp.where(away == -DEVS, 4 + slot, at)
            at = jnp.where(away == DEVS, 8 + slot, at)
            at = jnp.where(away == -1, 12, at)
            at = jnp.where(away == 1, 13, at)
            slots.append(jnp.where(brick < 0, 14, at))
        for plane in range(6):
            kz, z = ((0, 3), (1, 0), (1, 1), (1, 2), (1, 3), (2, 0))[plane]
            for q in range(9):
                block[plane, q * 16 : (q + 1) * 16] = bricks[slots[q * 3 + kz], z]
        for plane in range(6):
            moved = dot(window, block[plane]).astype(BF16)
            for s in range(9):
                row = ((s * 6 + plane) * B + b) * 16
                taps[row : row + 16] = moved[s * 16 : (s + 1) * 16]
    leave = [pltpu.make_async_copy(taps, taps_out, sems.at[9])]
    leave[0].start()
    for copy in copies[6:]:
        copy.wait()
    count = counts[place]
    merged = lax.dot_general(
        fine[...], weight[...], (((1,), (1,)), ((), ())), preferred_element_type=F32
    )
    brick_of = lax.broadcasted_iota(jnp.int32, (256, C), 0) // 64
    merged = jnp.where(brick_of < count, merged, 0.0).astype(BF16)
    merged = jnp.transpose(dot(row_order(False), merged)).astype(BF16)
    for tap in range(27):
        row = tap_rows(tap)
        term = dot(merged, taps[row : row + 256])
        at = tap * C
        end = at + C
        while at < end:
            owner = at // ROWS
            stop = min(end, (owner + 1) * ROWS)
            to = (owner // 2) * ROWS + at % ROWS
            total[owner % 2, :, to : to + stop - at] = term[:, at - tap * C : stop - tap * C]
            at = stop
    for i, (held, out, half) in enumerate(((send, send_out, 1 - core), (keep, keep_out, core))):
        for slab in range(SLABS):
            held[slab] = total[half, slab * COLS : (slab + 1) * COLS].astype(BF16)
        leave.append(pltpu.make_async_copy(held, out, sems.at[10 + i]))
        leave[-1].start()
    for copy in leave:
        copy.wait()


def back_kernel(
    counts_in, fine_in, weight_in, taps_in, mine, other, fine_grad, term,
    counts, fine, weight, taps, sems, both, whole,
):
    place = my_place()
    core = jnp.bitwise_and(place, 1)
    copies = fetch(
        sems, (mine, both.at[core]), (other, both.at[1 - core]), (taps_in, taps),
        (fine_in, fine), (weight_in, weight), (counts_in, counts),
    )
    for copy in copies[:2]:
        copy.wait()
    row = iota(16, 128, 0)
    held = None
    for owner in range(DEVS):
        first = ROWS * owner // 16 * 16
        shift = owner % 16
        tiles = [both[owner % 2, i, owner // 2] for i in range(SLABS)]
        for i in range(1, 5):
            whole[first + i * 16 : first + (i + 1) * 16, :128] = tiles[i]
            half = i % 2 * 64
            whole[first + i * 16 : first + (i + 1) * 16, 128:] = tiles[5 + i // 2][
                :, half : half + 64
            ]
        main, tail = tiles[0].astype(F32), tiles[5][:, :64].astype(F32)
        extra = tiles[7][:, 64:].astype(F32)
        long = jnp.concatenate([extra[0:1], extra[1:2]], axis=1)
        ends = [jnp.where(row < shift, main, jnp.where(row == shift, long, 0.0))]
        short = row[:, :64]
        ends.append(jnp.where(short < shift, tail, jnp.where(short == shift, extra[2:3], 0.0)))
        if shift:
            main = jnp.where(row >= shift, main, held[0])
            tail = jnp.where(short >= shift, tail, held[1])
        whole[first : first + 16, :128] = main.astype(BF16)
        whole[first : first + 16, 128:] = tail.astype(BF16)
        if shift == 15:
            whole[first + 80 : first + 96, :128] = ends[0].astype(BF16)
            whole[first + 80 : first + 96, 128:] = ends[1].astype(BF16)
        held = ends
    for copy in copies[2:]:
        copy.wait()
    back = jnp.zeros((256, C), F32)
    for tap in range(27):
        row = tap_rows(tap)
        back = back + dot(taps[row : row + 256], whole[tap * C : (tap + 1) * C])
    brick_of = lax.broadcasted_iota(jnp.int32, (256, C), 0) // 16 % B
    count = counts[place]
    back = jnp.where(brick_of < count, back, 0.0).astype(BF16)
    back = dot(row_order(True), back)
    gm = back.astype(BF16)
    fine_grad[...] = dot(gm, weight[...]).astype(BF16)
    result = dot(jnp.transpose(back).astype(BF16), fine[...])
    for i in range(DEVS):
        if i < PIECES:
            piece = result[i % 8 * 24 : i % 8 * 24 + 24, i // 8 * 128 : i // 8 * 128 + 128]
            term[i] = piece.astype(BF16)
        else:
            term[i] = jnp.zeros((24, 128), BF16)


def spread_kernel(parts, keep, received, out):
    merge = parts[0].astype(F32)
    for i in range(1, DEVS):
        merge = merge + parts[i].astype(F32)
    for i in range(SLABS):
        out[i, :, :HALF] = (keep[i].astype(F32) + received[i].astype(F32)).astype(BF16)
        out[i, :, HALF:WIDE] = jnp.zeros((COLS, WIDE - HALF), BF16)
        out[i, :, WIDE:] = merge.astype(BF16)


def both_kernel(parts, out):
    total = parts[0].astype(F32)
    for i in range(1, SLABS):
        total = total + parts[i].astype(F32)
    merge = total[:, WIDE:].astype(BF16)
    pad = jnp.zeros((COLS, 128 - ROWS), BF16)
    for i in range(32):
        piece = total[:, i * ROWS : (i + 1) * ROWS].astype(BF16)
        out[i, 0] = jnp.concatenate([piece, pad], axis=1)
        out[i, 1] = merge


def last_kernel(parts, merge_out, conv_out, merge, conv, sems):
    core = jnp.bitwise_and(my_place(), 1)
    for i in range(PIECES):
        row, col = i % 8 * 24, i // 8 * 128
        merge[row : row + 24, col : col + 128] = parts[i % 2, i // 2, 1].astype(F32)
    copies = fetch(sems, (merge, merge_out))
    total = parts[core, 0, 0].astype(F32)
    for i in range(1, 32):
        total = total + parts[core, i, 0].astype(F32)
    conv[...] = total[:, :ROWS]
    copies += fetch(sems.at[1:], (conv, conv_out))
    for copy in copies:
        copy.wait()


def call(kernel, outs, specs, scratch=(), flops=0, out_spec=None, vmem=20):
    return pl.pallas_call(
        kernel,
        out_shape=outs,
        in_specs=specs,
        out_specs=out_spec or jax.tree.map(lambda _: VMEM, outs),
        scratch_shapes=scratch,
        cost_estimate=pl.CostEstimate(flops=flops, bytes_accessed=0, transcendentals=0),
        compiler_params=pltpu.CompilerParams(vmem_limit_bytes=vmem << 20),
    )


def shape(*dims, dtype=BF16):
    return jax.ShapeDtypeStruct(dims, dtype)


def swap(x, axes):
    return lax.all_to_all(x, axes, 0, 0, tiled=True)


def local(
    fine_input, merge_weight, conv_weight, pre_act, norm_gain, norm_bias, cotangent, counts, neighbours
):
    counts_scratch = pltpu.SMEM((SLABS * DEVS,), jnp.int32)
    grad, near, far, frames = call(
        prepare_kernel,
        (shape(B, 4, 16, C), shape(1, 4, 16, C), shape(1, 4, 16, C), shape(32, 16, 128)),
        [HBM] * 6,
        [
            counts_scratch,
            pltpu.VMEM((B, 16, 4 * C), BF16),
            pltpu.VMEM((B, 16, 4 * C), BF16),
            pltpu.VMEM((1, C), F32),
            pltpu.VMEM((1, C), F32),
            pltpu.VMEM((ROWS, C), BF16),
            pltpu.VMEM((SLABS, 16, 128), BF16),
            pltpu.SemaphoreType.DMA((6,)),
        ],
        vmem=60,
    )(counts, pre_act, cotangent, norm_gain.reshape(1, C), norm_bias.reshape(1, C), conv_weight)

    def shifted(x, axes, count, step):
        pairs = [(i, i + step) for i in range(count) if 0 <= i + step < count]
        return lax.ppermute(x, axes, pairs)

    def flipped(x):
        return lax.ppermute(x, "c", [(0, 1), (1, 0)])

    slab_low = shifted(grad, SLAB, SLABS, 1)
    slab_high = shifted(grad, SLAB, SLABS, -1)
    frames = swap(frames, ("zh", "y"))
    frames, slab_low, slab_high, near, far = lax.optimization_barrier(
        (frames, slab_low, slab_high, near, far)
    )
    dev_near = flipped(near)
    ups = [(i, i + 1) for i in range(1, DEVS - 1, 2)]
    dev_far = lax.ppermute(far, DEV, ups + [(j, i) for i, j in ups])
    frames = call(repeat_kernel, shape(SLABS, 32, 16, 128), [VMEM])(frames)
    frames = swap(frames, SLAB)

    fine_scratch = pltpu.VMEM((256, 768), BF16)
    weight_scratch = pltpu.VMEM((C, 768), BF16)
    merge_weight = merge_weight.T
    keep, send, taps = call(
        conv_kernel,
        (shape(SLABS, COLS, HALF), shape(SLABS, COLS, HALF), shape(3456, C)),
        [HBM] * 9,
        [
            counts_scratch,
            pltpu.SMEM((B, 27), jnp.int32),
            fine_scratch,
            weight_scratch,
            pltpu.SemaphoreType.DMA((12,)),
            pltpu.VMEM((15, 4, 16, C), BF16),
            pltpu.VMEM((6, 144, C), BF16),
            pltpu.VMEM((2, C, HALF), F32),
            pltpu.VMEM((3456, C), BF16),
            pltpu.VMEM((SLABS, COLS, HALF), BF16),
            pltpu.VMEM((SLABS, COLS, HALF), BF16),
        ],
        flops=6 * 10**9,
        out_spec=(HBM, HBM, HBM),
        vmem=60,
    )(
        counts, neighbours, fine_input, merge_weight, grad, slab_low, slab_high, dev_near, dev_far
    )

    frames, taps = lax.optimization_barrier((frames, taps))
    other = flipped(frames)
    fine_grad, term = call(
        back_kernel,
        (shape(256, 768), shape(DEVS, 24, 128)),
        [HBM] * 6,
        [
            counts_scratch,
            fine_scratch,
            weight_scratch,
            pltpu.VMEM((3456, C), BF16),
            pltpu.SemaphoreType.DMA((6,)),
            pltpu.VMEM((2, SLABS, 32, 16, 128), BF16),
            pltpu.VMEM((27 * C, C), BF16),
        ],
        flops=4 * 10**9,
        vmem=60,
    )(counts, fine_input, merge_weight, taps, frames, other)

    term, received = lax.optimization_barrier((term, flipped(send)))
    term = swap(term, DEV)
    term = call(spread_kernel, shape(SLABS, COLS, WIDE + 128), [VMEM] * 3)(term, keep, received)
    term = swap(term, SLAB)
    term = call(both_kernel, shape(32, 2, 24, 128), [VMEM])(term)
    term = swap(term, ("zh", "y"))
    term = lax.all_gather(term, "c", axis=0, tiled=False)
    merge_grad, conv_grad = call(
        last_kernel,
        (shape(C, 768, dtype=F32), shape(COLS, ROWS, dtype=F32)),
        [VMEM],
        [
            pltpu.VMEM((C, 768), F32),
            pltpu.VMEM((COLS, ROWS), F32),
            pltpu.SemaphoreType.DMA((2,)),
        ],
        out_spec=(HBM, HBM),
    )(term)
    return fine_grad, merge_grad.T, conv_grad.T


def solution(mesh):
    fine_mesh = Mesh(mesh.devices.reshape(SIZES), AXES)
    every = SLAB + DEV
    in_specs = (
        P(every, None),
        P(),
        P(DEV, None),
        P(every, None, None),
        P(),
        P(),
        P(every, None, None),
        P(),
        P(every, None),
    )
    out_specs = (P(every, None), P(), P(DEV, SLAB))
    return jax.shard_map(
        local, mesh=fine_mesh, in_specs=in_specs, out_specs=out_specs, check_vma=False
    )
```

```python
import jax
import jax.numpy as jnp
from jax import lax
from jax.experimental import pallas as pl
from jax.experimental.pallas import tpu as pltpu
from jax.sharding import Mesh, PartitionSpec as P

F32 = jnp.float32
BF16 = jnp.bfloat16

AXES = ("zl", "x", "zh", "y", "c")
SIZES = (2, 4, 4, 8, 2)
SLAB = ("zl", "x")
DEV = ("zh", "y", "c")
SLABS = 8
DEVS = 64
B = 4
C = 192
ROWS = 81
FRAME = 80
HALF = 32 * ROWS
COLS = C // SLABS
PIECES = 48
WIDE = 2688

VMEM = pl.BlockSpec(memory_space=pltpu.VMEM)
HBM = pl.BlockSpec(memory_space=pltpu.HBM)


def dot(a, b):
    return jnp.dot(a, b, preferred_element_type=F32)


def my_place():
    place = lax.axis_index(AXES[0])
    for axis, size in zip(AXES[1:], SIZES[1:]):
        place = place * size + lax.axis_index(axis)
    return place


def repeat_kernel(block, out):
    for i in range(out.shape[0]):
        out[i] = block[...]


def iota(rows, cols, dim):
    return lax.broadcasted_iota(jnp.int32, (rows, cols), dim)


def ones_where(condition):
    return jnp.where(condition, 1.0, 0.0).astype(BF16)


def place_in_nine(start, v):
    p = start + v
    brick = jnp.where(p == 0, 0, jnp.where(p == 5, 2, 1))
    return brick, jnp.where(p == 0, 3, jnp.where(p == 5, 0, p - 1))


def window_matrix():
    row, col = iota(144, 144, 0), iota(144, 144, 1)
    s = lax.shift_right_logical(row, 4)
    sx = jnp.where(s >= 6, 2, jnp.where(s >= 3, 1, 0))
    v = jnp.bitwise_and(row, 15)
    kx, x = place_in_nine(sx, lax.shift_right_logical(v, 2))
    ky, y = place_in_nine(s - 3 * sx, jnp.bitwise_and(v, 3))
    return ones_where(col == (kx * 3 + ky) * 16 + x * 4 + y)


def row_order(inverse):
    inner, outer = iota(256, 256, int(inverse)), iota(256, 256, int(not inverse))
    return ones_where(
        outer == jnp.bitwise_and(inner, 63) * 4 + lax.shift_right_logical(inner, 6)
    )


def fetch(sems, *pairs):
    copies = [pltpu.make_async_copy(src, dst, sems.at[i]) for i, (src, dst) in enumerate(pairs)]
    for copy in copies:
        copy.start()
    return copies


def tap_rows(tap):
    window = (2 - tap // 9) * 3 + 2 - tap // 3 % 3
    return (window * 6 + 2 - tap % 3) * 64


def prepare_kernel(
    counts_in, pre_in, cot_in, gain_in, bias_in, weight_in, grad, near, far, frames,
    counts, pre, cot, gain, bias, weight, tiles, sems,
):
    copies = fetch(
        sems, (counts_in, counts), (pre_in, pre), (cot_in, cot), (gain_in, gain), (bias_in, bias),
        (weight_in, weight),
    )
    place = my_place()
    copies[5].wait()
    shift = jnp.bitwise_and(place, 15)
    at = iota(FRAME, ROWS, 1) + shift
    turned = jnp.where(at >= FRAME, at - FRAME, at)
    spread = ones_where((iota(FRAME, ROWS, 0) == turned) & (iota(FRAME, ROWS, 1) < FRAME))
    turned = dot(spread, weight[...])
    for i in range(5):
        tiles[i] = turned[i * 16 : (i + 1) * 16, :128].astype(BF16)
    extra = dot(ones_where(iota(16, ROWS, 1) == ROWS - 1), weight[...])
    row = iota(16, 64, 0)
    extra = jnp.where(
        row == 0, extra[:, :64], jnp.where(row == 1, extra[:, 64:128], extra[:, 128:])
    )
    tails = [turned[i * 16 : (i + 1) * 16, 128:] for i in range(5)] + [extra]
    for i in range(3):
        pair = jnp.concatenate([tails[2 * i], tails[2 * i + 1]], axis=1)
        tiles[5 + i] = pair.astype(BF16)
    mine = tiles[lax.shift_right_logical(place, 6)]
    for i in range(32):
        frames[i] = mine
    for copy in copies[:5]:
        copy.wait()
    count = counts[place]
    g = gain[...]
    for b in range(B):
        p = pre[b].astype(F32)
        u = cot[b].astype(F32)
        for z in range(4):
            pz = p[:, z * C : (z + 1) * C]
            uz = u[:, z * C : (z + 1) * C]
            gate = (g * pz + bias[...] > 0) & (b < count)
            grad[b, z] = jnp.where(gate, uz * g, 0.0).astype(BF16)
    core = jnp.bitwise_and(place, 1)
    near[0] = grad[jnp.where(core == 0, count - 1, 0)]
    far[0] = grad[jnp.where(core == 0, 0, count - 1)]


def taps_kernel(
    near_in, grad, slab_low, slab_high, dev_near, dev_far, taps_out, near, sems, bricks, block, taps
):
    place = my_place()
    core = jnp.bitwise_and(place, 1)
    copies = fetch(
        sems, (near_in, near), (grad, bricks.at[0:4]), (slab_low, bricks.at[4:8]),
        (slab_high, bricks.at[8:12]), (dev_near, bricks.at[pl.ds(13 - core, 1)]),
        (dev_far, bricks.at[pl.ds(12 + core, 1)]),
    )
    bricks[14:15] = jnp.zeros((1, 4, 16, C), BF16)
    window = window_matrix()
    for copy in copies:
        copy.wait()
    for b in range(B):
        slots = []
        for k in range(27):
            brick = near[b, k]
            away = lax.shift_right_arithmetic(brick, 2) - place
            slot = jnp.bitwise_and(brick, 3)
            at = jnp.where(away == 0, slot, 14)
            at = jnp.where(away == -DEVS, 4 + slot, at)
            at = jnp.where(away == DEVS, 8 + slot, at)
            at = jnp.where(away == -1, 12, at)
            at = jnp.where(away == 1, 13, at)
            slots.append(jnp.where(brick < 0, 14, at))
        for plane in range(6):
            kz, z = ((0, 3), (1, 0), (1, 1), (1, 2), (1, 3), (2, 0))[plane]
            for q in range(9):
                block[plane, q * 16 : (q + 1) * 16] = bricks[slots[q * 3 + kz], z]
        for plane in range(6):
            moved = dot(window, block[plane]).astype(BF16)
            for s in range(9):
                row = ((s * 6 + plane) * B + b) * 16
                taps[row : row + 16] = moved[s * 16 : (s + 1) * 16]
    leave = pltpu.make_async_copy(taps, taps_out, sems.at[6])
    leave.start()
    leave.wait()


def conv_kernel(
    counts_in, fine_in, weight_in, taps_in, keep_out, send_out,
    counts, fine, weight, taps, sems, total, keep, send,
):
    place = my_place()
    core = jnp.bitwise_and(place, 1)
    copies = fetch(
        sems, (counts_in, counts), (fine_in, fine), (weight_in, weight), (taps_in, taps)
    )
    for copy in copies[:3]:
        copy.wait()
    count = counts[place]
    merged = lax.dot_general(
        fine[...], weight[...], (((1,), (1,)), ((), ())), preferred_element_type=F32
    )
    brick_of = lax.broadcasted_iota(jnp.int32, (256, C), 0) // 64
    merged = jnp.where(brick_of < count, merged, 0.0).astype(BF16)
    merged = jnp.transpose(dot(row_order(False), merged)).astype(BF16)
    copies[3].wait()
    for tap in range(27):
        row = tap_rows(tap)
        term = dot(merged, taps[row : row + 256])
        at = tap * C
        end = at + C
        while at < end:
            owner = at // ROWS
            stop = min(end, (owner + 1) * ROWS)
            to = (owner // 2) * ROWS + at % ROWS
            total[owner % 2, :, to : to + stop - at] = term[:, at - tap * C : stop - tap * C]
            at = stop
    leave = []
    for i, (held, out, half) in enumerate(((send, send_out, 1 - core), (keep, keep_out, core))):
        for slab in range(SLABS):
            held[slab] = total[half, slab * COLS : (slab + 1) * COLS].astype(BF16)
        leave.append(pltpu.make_async_copy(held, out, sems.at[4 + i]))
        leave[-1].start()
    for copy in leave:
        copy.wait()


def back_kernel(
    counts_in, fine_in, weight_in, taps_in, mine, other, fine_grad, term,
    counts, fine, weight, taps, sems, both, whole,
):
    place = my_place()
    core = jnp.bitwise_and(place, 1)
    copies = fetch(
        sems, (mine, both.at[core]), (other, both.at[1 - core]), (taps_in, taps),
        (fine_in, fine), (weight_in, weight), (counts_in, counts),
    )
    for copy in copies[:2]:
        copy.wait()
    row = iota(16, 128, 0)
    held = None
    for owner in range(DEVS):
        first = ROWS * owner // 16 * 16
        shift = owner % 16
        tiles = [both[owner % 2, i, owner // 2] for i in range(SLABS)]
        for i in range(1, 5):
            whole[first + i * 16 : first + (i + 1) * 16, :128] = tiles[i]
            half = i % 2 * 64
            whole[first + i * 16 : first + (i + 1) * 16, 128:] = tiles[5 + i // 2][
                :, half : half + 64
            ]
        main, tail = tiles[0].astype(F32), tiles[5][:, :64].astype(F32)
        extra = tiles[7][:, 64:].astype(F32)
        long = jnp.concatenate([extra[0:1], extra[1:2]], axis=1)
        ends = [jnp.where(row < shift, main, jnp.where(row == shift, long, 0.0))]
        short = row[:, :64]
        ends.append(jnp.where(short < shift, tail, jnp.where(short == shift, extra[2:3], 0.0)))
        if shift:
            main = jnp.where(row >= shift, main, held[0])
            tail = jnp.where(short >= shift, tail, held[1])
        whole[first : first + 16, :128] = main.astype(BF16)
        whole[first : first + 16, 128:] = tail.astype(BF16)
        if shift == 15:
            whole[first + 80 : first + 96, :128] = ends[0].astype(BF16)
            whole[first + 80 : first + 96, 128:] = ends[1].astype(BF16)
        held = ends
    for copy in copies[2:]:
        copy.wait()
    back = jnp.zeros((256, C), F32)
    for tap in range(27):
        row = tap_rows(tap)
        back = back + dot(taps[row : row + 256], whole[tap * C : (tap + 1) * C])
    brick_of = lax.broadcasted_iota(jnp.int32, (256, C), 0) // 16 % B
    count = counts[place]
    back = jnp.where(brick_of < count, back, 0.0).astype(BF16)
    back = dot(row_order(True), back)
    gm = back.astype(BF16)
    fine_grad[...] = dot(gm, weight[...]).astype(BF16)
    result = dot(jnp.transpose(back).astype(BF16), fine[...])
    for i in range(PIECES):
        piece = result[i % 8 * 24 : i % 8 * 24 + 24, i // 8 * 128 : i // 8 * 128 + 128]
        term[i // 24, i % 24] = piece.astype(BF16)


def join_kernel(parts, out):
    core = lax.axis_index("c")
    for i in range(24):
        out[i] = (parts[0, core, i].astype(F32) + parts[1, core, i].astype(F32)).astype(BF16)
    for i in range(24, 32):
        out[i] = jnp.zeros((24, 128), BF16)


def spread_kernel(parts, keep, received, out):
    merge = parts[0].astype(F32)
    for i in range(1, 32):
        merge = merge + parts[i].astype(F32)
    for i in range(SLABS):
        out[i, :, :HALF] = (keep[i].astype(F32) + received[i].astype(F32)).astype(BF16)
        out[i, :, HALF:WIDE] = jnp.zeros((COLS, WIDE - HALF), BF16)
        out[i, :, WIDE:] = merge.astype(BF16)


def both_kernel(parts, out):
    total = parts[0].astype(F32)
    for i in range(1, SLABS):
        total = total + parts[i].astype(F32)
    merge = total[:, WIDE:].astype(BF16)
    pad = jnp.zeros((COLS, 128 - ROWS), BF16)
    for i in range(32):
        piece = total[:, i * ROWS : (i + 1) * ROWS].astype(BF16)
        out[i, 0] = jnp.concatenate([piece, pad], axis=1)
        out[i, 1] = merge


def last_kernel(parts, merge_out, conv_out, merge, conv, sems):
    core = jnp.bitwise_and(my_place(), 1)
    for i in range(PIECES):
        row, col = i % 8 * 24, i // 8 * 128
        merge[row : row + 24, col : col + 128] = parts[i // 24, i % 24, 1].astype(F32)
    copies = fetch(sems, (merge, merge_out))
    total = parts[core, 0, 0].astype(F32)
    for i in range(1, 32):
        total = total + parts[core, i, 0].astype(F32)
    conv[...] = total[:, :ROWS]
    copies += fetch(sems.at[1:], (conv, conv_out))
    for copy in copies:
        copy.wait()


def call(kernel, outs, specs, scratch=(), flops=0, out_spec=None, vmem=20):
    return pl.pallas_call(
        kernel,
        out_shape=outs,
        in_specs=specs,
        out_specs=out_spec or jax.tree.map(lambda _: VMEM, outs),
        scratch_shapes=scratch,
        cost_estimate=pl.CostEstimate(flops=flops, bytes_accessed=0, transcendentals=0),
        compiler_params=pltpu.CompilerParams(vmem_limit_bytes=vmem << 20),
    )


def shape(*dims, dtype=BF16):
    return jax.ShapeDtypeStruct(dims, dtype)


def swap(x, axes):
    return lax.all_to_all(x, axes, 0, 0, tiled=True)


def local(
    fine_input, merge_weight, conv_weight, pre_act, norm_gain, norm_bias, cotangent, counts, neighbours
):
    counts_scratch = pltpu.SMEM((SLABS * DEVS,), jnp.int32)
    grad, near, far, frames = call(
        prepare_kernel,
        (shape(B, 4, 16, C), shape(1, 4, 16, C), shape(1, 4, 16, C), shape(32, 16, 128)),
        [HBM] * 6,
        [
            counts_scratch,
            pltpu.VMEM((B, 16, 4 * C), BF16),
            pltpu.VMEM((B, 16, 4 * C), BF16),
            pltpu.VMEM((1, C), F32),
            pltpu.VMEM((1, C), F32),
            pltpu.VMEM((ROWS, C), BF16),
            pltpu.VMEM((SLABS, 16, 128), BF16),
            pltpu.SemaphoreType.DMA((6,)),
        ],
        vmem=60,
    )(counts, pre_act, cotangent, norm_gain.reshape(1, C), norm_bias.reshape(1, C), conv_weight)

    def shifted(x, axes, count, step):
        pairs = [(i, i + step) for i in range(count) if 0 <= i + step < count]
        return lax.ppermute(x, axes, pairs)

    def flipped(x):
        return lax.ppermute(x, "c", [(0, 1), (1, 0)])

    slab_low = shifted(grad, SLAB, SLABS, 1)
    slab_high = shifted(grad, SLAB, SLABS, -1)
    frames = swap(frames, ("zh", "y"))
    frames, slab_low, slab_high, near, far = lax.optimization_barrier(
        (frames, slab_low, slab_high, near, far)
    )
    dev_near = flipped(near)
    ups = [(i, i + 1) for i in range(1, DEVS - 1, 2)]
    dev_far = lax.ppermute(far, DEV, ups + [(j, i) for i, j in ups])
    frames = call(repeat_kernel, shape(SLABS, 32, 16, 128), [VMEM])(frames)
    frames = swap(frames, SLAB)

    fine_scratch = pltpu.VMEM((256, 768), BF16)
    weight_scratch = pltpu.VMEM((C, 768), BF16)
    merge_weight = merge_weight.T
    taps_scratch = pltpu.VMEM((3456, C), BF16)
    half_scratch = pltpu.VMEM((SLABS, COLS, HALF), BF16)
    taps = call(
        taps_kernel,
        shape(3456, C),
        [HBM] * 6,
        [
            pltpu.SMEM((B, 27), jnp.int32),
            pltpu.SemaphoreType.DMA((7,)),
            pltpu.VMEM((15, 4, 16, C), BF16),
            pltpu.VMEM((6, 144, C), BF16),
            taps_scratch,
        ],
        flops=3 * 10**9,
        out_spec=HBM,
        vmem=60,
    )(neighbours, grad, slab_low, slab_high, dev_near, dev_far)
    frames, taps = lax.optimization_barrier((frames, taps))
    other = flipped(frames)
    keep, send = call(
        conv_kernel,
        (shape(SLABS, COLS, HALF), shape(SLABS, COLS, HALF)),
        [HBM] * 4,
        [
            counts_scratch,
            fine_scratch,
            weight_scratch,
            taps_scratch,
            pltpu.SemaphoreType.DMA((6,)),
            pltpu.VMEM((2, C, HALF), F32),
            half_scratch,
            half_scratch,
        ],
        flops=4 * 10**9,
        out_spec=(HBM, HBM),
        vmem=60,
    )(counts, fine_input, merge_weight, taps)
    fine_grad, term = call(
        back_kernel,
        (shape(256, 768), shape(2, 24, 24, 128)),
        [HBM] * 6,
        [
            counts_scratch,
            fine_scratch,
            weight_scratch,
            taps_scratch,
            pltpu.SemaphoreType.DMA((6,)),
            pltpu.VMEM((2, SLABS, 32, 16, 128), BF16),
            pltpu.VMEM((27 * C, C), BF16),
        ],
        flops=4 * 10**9,
        vmem=60,
    )(counts, fine_input, merge_weight, taps, frames, other)

    term = lax.all_gather(term, "c", axis=0, tiled=False)
    term, received = lax.optimization_barrier((term, flipped(send)))
    term = call(join_kernel, shape(32, 24, 128), [VMEM])(term)
    term = swap(term, ("zh", "y"))
    term = call(spread_kernel, shape(SLABS, COLS, WIDE + 128), [VMEM] * 3)(term, keep, received)
    term = swap(term, SLAB)
    term = call(both_kernel, shape(32, 2, 24, 128), [VMEM])(term)
    term = swap(term, ("zh", "y"))
    term = lax.all_gather(term, "c", axis=0, tiled=False)
    merge_grad, conv_grad = call(
        last_kernel,
        (shape(C, 768, dtype=F32), shape(COLS, ROWS, dtype=F32)),
        [VMEM],
        [
            pltpu.VMEM((C, 768), F32),
            pltpu.VMEM((COLS, ROWS), F32),
            pltpu.SemaphoreType.DMA((2,)),
        ],
        out_spec=(HBM, HBM),
    )(term)
    return fine_grad, merge_grad.T, conv_grad.T


def solution(mesh):
    fine_mesh = Mesh(mesh.devices.reshape(SIZES), AXES)
    every = SLAB + DEV
    in_specs = (
        P(every, None),
        P(),
        P(DEV, None),
        P(every, None, None),
        P(),
        P(),
        P(every, None, None),
        P(),
        P(every, None),
    )
    out_specs = (P(every, None), P(), P(DEV, SLAB))
    return jax.shard_map(
        local, mesh=fine_mesh, in_specs=in_specs, out_specs=out_specs, check_vma=False
    )
```

```python
import jax
import jax.numpy as jnp
from jax import lax
from jax.experimental import pallas as pl
from jax.experimental.pallas import tpu as pltpu
from jax.sharding import Mesh, PartitionSpec as P

F32 = jnp.float32
BF16 = jnp.bfloat16

AXES = ("zl", "x", "zh", "y", "c")
SIZES = (2, 4, 4, 8, 2)
SLAB = ("zl", "x")
DEV = ("zh", "y", "c")
SLABS = 8
DEVS = 64
B = 4
C = 192
ROWS = 81
FRAME = 80
HALF = 32 * ROWS
COLS = C // SLABS
PIECES = 48
WIDE = 2688

VMEM = pl.BlockSpec(memory_space=pltpu.VMEM)
HBM = pl.BlockSpec(memory_space=pltpu.HBM)


def dot(a, b):
    return jnp.dot(a, b, preferred_element_type=F32)


def my_place():
    place = lax.axis_index(AXES[0])
    for axis, size in zip(AXES[1:], SIZES[1:]):
        place = place * size + lax.axis_index(axis)
    return place


def repeat_kernel(block, out):
    for i in range(out.shape[0]):
        out[i] = block[...]


def iota(rows, cols, dim):
    return lax.broadcasted_iota(jnp.int32, (rows, cols), dim)


def ones_where(condition):
    return jnp.where(condition, 1.0, 0.0).astype(BF16)


def place_in_nine(start, v):
    p = start + v
    brick = jnp.where(p == 0, 0, jnp.where(p == 5, 2, 1))
    return brick, jnp.where(p == 0, 3, jnp.where(p == 5, 0, p - 1))


def window_matrix():
    row, col = iota(144, 144, 0), iota(144, 144, 1)
    s = lax.shift_right_logical(row, 4)
    sx = jnp.where(s >= 6, 2, jnp.where(s >= 3, 1, 0))
    v = jnp.bitwise_and(row, 15)
    kx, x = place_in_nine(sx, lax.shift_right_logical(v, 2))
    ky, y = place_in_nine(s - 3 * sx, jnp.bitwise_and(v, 3))
    return ones_where(col == (kx * 3 + ky) * 16 + x * 4 + y)


def row_order(inverse):
    inner, outer = iota(256, 256, int(inverse)), iota(256, 256, int(not inverse))
    return ones_where(
        outer == jnp.bitwise_and(inner, 63) * 4 + lax.shift_right_logical(inner, 6)
    )


def fetch(sems, *pairs):
    copies = [pltpu.make_async_copy(src, dst, sems.at[i]) for i, (src, dst) in enumerate(pairs)]
    for copy in copies:
        copy.start()
    return copies


def tap_rows(tap):
    window = (2 - tap // 9) * 3 + 2 - tap // 3 % 3
    return (window * 6 + 2 - tap % 3) * 64


def prepare_kernel(
    counts_in, pre_in, cot_in, gain_in, bias_in, weight_in, grad, near, far, frames,
    counts, pre, cot, gain, bias, weight, tiles, sems,
):
    copies = fetch(
        sems, (counts_in, counts), (pre_in, pre), (cot_in, cot), (gain_in, gain), (bias_in, bias),
        (weight_in, weight),
    )
    place = my_place()
    copies[5].wait()
    shift = jnp.bitwise_and(place, 15)
    at = iota(FRAME, ROWS, 1) + shift
    turned = jnp.where(at >= FRAME, at - FRAME, at)
    spread = ones_where((iota(FRAME, ROWS, 0) == turned) & (iota(FRAME, ROWS, 1) < FRAME))
    turned = dot(spread, weight[...])
    for i in range(5):
        tiles[i] = turned[i * 16 : (i + 1) * 16, :128].astype(BF16)
    extra = dot(ones_where(iota(16, ROWS, 1) == ROWS - 1), weight[...])
    row = iota(16, 64, 0)
    extra = jnp.where(
        row == 0, extra[:, :64], jnp.where(row == 1, extra[:, 64:128], extra[:, 128:])
    )
    tails = [turned[i * 16 : (i + 1) * 16, 128:] for i in range(5)] + [extra]
    for i in range(3):
        pair = jnp.concatenate([tails[2 * i], tails[2 * i + 1]], axis=1)
        tiles[5 + i] = pair.astype(BF16)
    mine = tiles[lax.shift_right_logical(place, 6)]
    for i in range(32):
        frames[i] = mine
    for copy in copies[:5]:
        copy.wait()
    count = counts[place]
    g = gain[...]
    for b in range(B):
        p = pre[b].astype(F32)
        u = cot[b].astype(F32)
        for z in range(4):
            pz = p[:, z * C : (z + 1) * C]
            uz = u[:, z * C : (z + 1) * C]
            gate = (g * pz + bias[...] > 0) & (b < count)
            grad[b, z] = jnp.where(gate, uz * g, 0.0).astype(BF16)
    core = jnp.bitwise_and(place, 1)
    near[0] = grad[jnp.where(core == 0, count - 1, 0)]
    far[0] = grad[jnp.where(core == 0, 0, count - 1)]


def conv_kernel(
    counts_in, near_in, fine_in, weight_in, grad, slab_low, slab_high, dev_near, dev_far,
    keep_out, send_out, taps_out, counts, near, fine, weight, sems, bricks, block, total, taps,
    keep, send,
):
    place = my_place()
    core = jnp.bitwise_and(place, 1)
    copies = fetch(
        sems, (near_in, near), (grad, bricks.at[0:4]), (slab_low, bricks.at[4:8]),
        (slab_high, bricks.at[8:12]), (dev_near, bricks.at[pl.ds(13 - core, 1)]),
        (dev_far, bricks.at[pl.ds(12 + core, 1)]),
        (counts_in, counts), (fine_in, fine), (weight_in, weight),
    )
    bricks[14:15] = jnp.zeros((1, 4, 16, C), BF16)
    window = window_matrix()
    for copy in copies[:6]:
        copy.wait()
    for b in range(B):
        slots = []
        for k in range(27):
            brick = near[b, k]
            away = lax.shift_right_arithmetic(brick, 2) - place
            slot = jnp.bitwise_and(brick, 3)
            at = jnp.where(away == 0, slot, 14)
            at = jnp.where(away == -DEVS, 4 + slot, at)
            at = jnp.where(away == DEVS, 8 + slot, at)
            at = jnp.where(away == -1, 12, at)
            at = jnp.where(away == 1, 13, at)
            slots.append(jnp.where(brick < 0, 14, at))
        for plane in range(6):
            kz, z = ((0, 3), (1, 0), (1, 1), (1, 2), (1, 3), (2, 0))[plane]
            for q in range(9):
                block[plane, q * 16 : (q + 1) * 16] = bricks[slots[q * 3 + kz], z]
        for plane in range(6):
            moved = dot(window, block[plane]).astype(BF16)
            for s in range(9):
                row = ((s * 6 + plane) * B + b) * 16
                taps[row : row + 16] = moved[s * 16 : (s + 1) * 16]
    leave = [pltpu.make_async_copy(taps, taps_out, sems.at[9])]
    leave[0].start()
    for copy in copies[6:]:
        copy.wait()
    count = counts[place]
    merged = lax.dot_general(
        fine[...], weight[...], (((1,), (1,)), ((), ())), preferred_element_type=F32
    )
    brick_of = lax.broadcasted_iota(jnp.int32, (256, C), 0) // 64
    merged = jnp.where(brick_of < count, merged, 0.0).astype(BF16)
    merged = jnp.transpose(dot(row_order(False), merged)).astype(BF16)
    for tap in range(27):
        row = tap_rows(tap)
        term = dot(merged, taps[row : row + 256])
        at = tap * C
        end = at + C
        while at < end:
            owner = at // ROWS
            stop = min(end, (owner + 1) * ROWS)
            to = (owner // 2) * ROWS + at % ROWS
            total[owner % 2, :, to : to + stop - at] = term[:, at - tap * C : stop - tap * C]
            at = stop
    for i, (held, out, half) in enumerate(((send, send_out, 1 - core), (keep, keep_out, core))):
        for slab in range(SLABS):
            held[slab] = total[half, slab * COLS : (slab + 1) * COLS].astype(BF16)
        leave.append(pltpu.make_async_copy(held, out, sems.at[10 + i]))
        leave[-1].start()
    for copy in leave:
        copy.wait()


def back_kernel(
    counts_in, fine_in, taps_in, mine, other, gm, term, counts, fine, taps, sems, both, whole,
):
    place = my_place()
    core = jnp.bitwise_and(place, 1)
    copies = fetch(
        sems, (mine, both.at[core]), (other, both.at[1 - core]), (taps_in, taps),
        (fine_in, fine), (counts_in, counts),
    )
    for copy in copies[:2]:
        copy.wait()
    row = iota(16, 128, 0)
    held = None
    for owner in range(DEVS):
        first = ROWS * owner // 16 * 16
        shift = owner % 16
        tiles = [both[owner % 2, i, owner // 2] for i in range(SLABS)]
        for i in range(1, 5):
            whole[first + i * 16 : first + (i + 1) * 16, :128] = tiles[i]
            half = i % 2 * 64
            whole[first + i * 16 : first + (i + 1) * 16, 128:] = tiles[5 + i // 2][
                :, half : half + 64
            ]
        main, tail = tiles[0].astype(F32), tiles[5][:, :64].astype(F32)
        extra = tiles[7][:, 64:].astype(F32)
        long = jnp.concatenate([extra[0:1], extra[1:2]], axis=1)
        ends = [jnp.where(row < shift, main, jnp.where(row == shift, long, 0.0))]
        short = row[:, :64]
        ends.append(jnp.where(short < shift, tail, jnp.where(short == shift, extra[2:3], 0.0)))
        if shift:
            main = jnp.where(row >= shift, main, held[0])
            tail = jnp.where(short >= shift, tail, held[1])
        whole[first : first + 16, :128] = main.astype(BF16)
        whole[first : first + 16, 128:] = tail.astype(BF16)
        if shift == 15:
            whole[first + 80 : first + 96, :128] = ends[0].astype(BF16)
            whole[first + 80 : first + 96, 128:] = ends[1].astype(BF16)
        held = ends
    for copy in copies[2:]:
        copy.wait()
    back = jnp.zeros((256, C), F32)
    for tap in range(27):
        row = tap_rows(tap)
        back = back + dot(taps[row : row + 256], whole[tap * C : (tap + 1) * C])
    brick_of = lax.broadcasted_iota(jnp.int32, (256, C), 0) // 16 % B
    count = counts[place]
    back = jnp.where(brick_of < count, back, 0.0).astype(BF16)
    back = dot(row_order(True), back)
    gm[...] = back.astype(BF16)
    result = dot(jnp.transpose(back).astype(BF16), fine[...])
    for i in range(PIECES):
        piece = result[i % 8 * 24 : i % 8 * 24 + 24, i // 8 * 128 : i // 8 * 128 + 128]
        term[i // 24, i % 24] = piece.astype(BF16)


def fine_kernel(gm_in, weight_in, fine_out, gm, weight, fine_grad, sems):
    for copy in fetch(sems, (gm_in, gm), (weight_in, weight)):
        copy.wait()
    fine_grad[...] = dot(gm[...], weight[...]).astype(BF16)
    for copy in fetch(sems.at[2:], (fine_grad, fine_out)):
        copy.wait()


def join_kernel(parts, out):
    core = lax.axis_index("c")
    for i in range(24):
        out[i] = (parts[0, core, i].astype(F32) + parts[1, core, i].astype(F32)).astype(BF16)
    for i in range(24, 32):
        out[i] = jnp.zeros((24, 128), BF16)


def spread_kernel(parts, keep, received, out):
    merge = parts[0].astype(F32)
    for i in range(1, 32):
        merge = merge + parts[i].astype(F32)
    for i in range(SLABS):
        out[i, :, :HALF] = (keep[i].astype(F32) + received[i].astype(F32)).astype(BF16)
        out[i, :, HALF:WIDE] = jnp.zeros((COLS, WIDE - HALF), BF16)
        out[i, :, WIDE:] = merge.astype(BF16)


def both_kernel(parts, out):
    total = parts[0].astype(F32)
    for i in range(1, SLABS):
        total = total + parts[i].astype(F32)
    merge = total[:, WIDE:].astype(BF16)
    pad = jnp.zeros((COLS, 128 - ROWS), BF16)
    for i in range(32):
        piece = total[:, i * ROWS : (i + 1) * ROWS].astype(BF16)
        out[i, 0] = jnp.concatenate([piece, pad], axis=1)
        out[i, 1] = merge


def last_kernel(parts, merge_out, conv_out, merge, conv, sems):
    core = jnp.bitwise_and(my_place(), 1)
    for i in range(PIECES):
        row, col = i % 8 * 24, i // 8 * 128
        merge[row : row + 24, col : col + 128] = parts[i // 24, i % 24, 1].astype(F32)
    copies = fetch(sems, (merge, merge_out))
    total = parts[core, 0, 0].astype(F32)
    for i in range(1, 32):
        total = total + parts[core, i, 0].astype(F32)
    conv[...] = total[:, :ROWS]
    copies += fetch(sems.at[1:], (conv, conv_out))
    for copy in copies:
        copy.wait()


def call(kernel, outs, specs, scratch=(), flops=0, out_spec=None, vmem=20):
    return pl.pallas_call(
        kernel,
        out_shape=outs,
        in_specs=specs,
        out_specs=out_spec or jax.tree.map(lambda _: VMEM, outs),
        scratch_shapes=scratch,
        cost_estimate=pl.CostEstimate(flops=flops, bytes_accessed=0, transcendentals=0),
        compiler_params=pltpu.CompilerParams(vmem_limit_bytes=vmem << 20),
    )


def shape(*dims, dtype=BF16):
    return jax.ShapeDtypeStruct(dims, dtype)


def swap(x, axes):
    return lax.all_to_all(x, axes, 0, 0, tiled=True)


def local(
    fine_input, merge_weight, conv_weight, pre_act, norm_gain, norm_bias, cotangent, counts, neighbours
):
    counts_scratch = pltpu.SMEM((SLABS * DEVS,), jnp.int32)
    grad, near, far, frames = call(
        prepare_kernel,
        (shape(B, 4, 16, C), shape(1, 4, 16, C), shape(1, 4, 16, C), shape(32, 16, 128)),
        [HBM] * 6,
        [
            counts_scratch,
            pltpu.VMEM((B, 16, 4 * C), BF16),
            pltpu.VMEM((B, 16, 4 * C), BF16),
            pltpu.VMEM((1, C), F32),
            pltpu.VMEM((1, C), F32),
            pltpu.VMEM((ROWS, C), BF16),
            pltpu.VMEM((SLABS, 16, 128), BF16),
            pltpu.SemaphoreType.DMA((6,)),
        ],
        vmem=60,
    )(counts, pre_act, cotangent, norm_gain.reshape(1, C), norm_bias.reshape(1, C), conv_weight)

    def shifted(x, axes, count, step):
        pairs = [(i, i + step) for i in range(count) if 0 <= i + step < count]
        return lax.ppermute(x, axes, pairs)

    def flipped(x):
        return lax.ppermute(x, "c", [(0, 1), (1, 0)])

    slab_low = shifted(grad, SLAB, SLABS, 1)
    slab_high = shifted(grad, SLAB, SLABS, -1)
    frames = swap(frames, ("zh", "y"))
    frames, slab_low, slab_high, near, far = lax.optimization_barrier(
        (frames, slab_low, slab_high, near, far)
    )
    dev_near = flipped(near)
    ups = [(i, i + 1) for i in range(1, DEVS - 1, 2)]
    dev_far = lax.ppermute(far, DEV, ups + [(j, i) for i, j in ups])
    frames = call(repeat_kernel, shape(SLABS, 32, 16, 128), [VMEM])(frames)
    frames = swap(frames, SLAB)

    fine_scratch = pltpu.VMEM((256, 768), BF16)
    weight_scratch = pltpu.VMEM((C, 768), BF16)
    merge_weight = merge_weight.T
    keep, send, taps = call(
        conv_kernel,
        (shape(SLABS, COLS, HALF), shape(SLABS, COLS, HALF), shape(3456, C)),
        [HBM] * 9,
        [
            counts_scratch,
            pltpu.SMEM((B, 27), jnp.int32),
            fine_scratch,
            weight_scratch,
            pltpu.SemaphoreType.DMA((12,)),
            pltpu.VMEM((15, 4, 16, C), BF16),
            pltpu.VMEM((6, 144, C), BF16),
            pltpu.VMEM((2, C, HALF), F32),
            pltpu.VMEM((3456, C), BF16),
            pltpu.VMEM((SLABS, COLS, HALF), BF16),
            pltpu.VMEM((SLABS, COLS, HALF), BF16),
        ],
        flops=6 * 10**9,
        out_spec=(HBM, HBM, HBM),
        vmem=60,
    )(
        counts, neighbours, fine_input, merge_weight, grad, slab_low, slab_high, dev_near, dev_far
    )

    frames, taps = lax.optimization_barrier((frames, taps))
    other = flipped(frames)
    gm, term = call(
        back_kernel,
        (shape(256, C), shape(2, 24, 24, 128)),
        [HBM] * 5,
        [
            counts_scratch,
            fine_scratch,
            pltpu.VMEM((3456, C), BF16),
            pltpu.SemaphoreType.DMA((5,)),
            pltpu.VMEM((2, SLABS, 32, 16, 128), BF16),
            pltpu.VMEM((27 * C, C), BF16),
        ],
        flops=4 * 10**9,
        vmem=60,
    )(counts, fine_input, taps, frames, other)
    fine_grad = call(
        fine_kernel,
        shape(256, 768),
        [HBM] * 2,
        [
            pltpu.VMEM((256, C), BF16),
            weight_scratch,
            fine_scratch,
            pltpu.SemaphoreType.DMA((3,)),
        ],
        flops=10**9,
        out_spec=HBM,
    )(gm, merge_weight)

    term = lax.all_gather(term, "c", axis=0, tiled=False)
    term = call(join_kernel, shape(32, 24, 128), [VMEM])(term)
    term = swap(term, ("zh", "y"))
    term = call(spread_kernel, shape(SLABS, COLS, WIDE + 128), [VMEM] * 3)(
        term, keep, flipped(send)
    )
    term = swap(term, SLAB)
    term = call(both_kernel, shape(32, 2, 24, 128), [VMEM])(term)
    term = swap(term, ("zh", "y"))
    term = lax.all_gather(term, "c", axis=0, tiled=False)
    merge_grad, conv_grad = call(
        last_kernel,
        (shape(C, 768, dtype=F32), shape(COLS, ROWS, dtype=F32)),
        [VMEM],
        [
            pltpu.VMEM((C, 768), F32),
            pltpu.VMEM((COLS, ROWS), F32),
            pltpu.SemaphoreType.DMA((2,)),
        ],
        out_spec=(HBM, HBM),
    )(term)
    return fine_grad, merge_grad.T, conv_grad.T


def solution(mesh):
    fine_mesh = Mesh(mesh.devices.reshape(SIZES), AXES)
    every = SLAB + DEV
    in_specs = (
        P(every, None),
        P(),
        P(DEV, None),
        P(every, None, None),
        P(),
        P(),
        P(every, None, None),
        P(),
        P(every, None),
    )
    out_specs = (P(every, None), P(), P(DEV, SLAB))
    return jax.shard_map(
        local, mesh=fine_mesh, in_specs=in_specs, out_specs=out_specs, check_vma=False
    )
```

```python
import jax
import jax.numpy as jnp
from jax import lax
from jax.experimental import pallas as pl
from jax.experimental.pallas import tpu as pltpu
from jax.sharding import Mesh, PartitionSpec as P

F32 = jnp.float32
BF16 = jnp.bfloat16

AXES = ("zl", "x", "zh", "y", "c")
SIZES = (2, 4, 4, 8, 2)
SLAB = ("zl", "x")
DEV = ("zh", "y", "c")
SLABS = 8
DEVS = 64
B = 4
C = 192
ROWS = 81
FRAME = 80
HALF = 32 * ROWS
COLS = C // SLABS
PIECES = 48

VMEM = pl.BlockSpec(memory_space=pltpu.VMEM)
HBM = pl.BlockSpec(memory_space=pltpu.HBM)


def dot(a, b):
    return jnp.dot(a, b, preferred_element_type=F32)


def my_place():
    place = lax.axis_index(AXES[0])
    for axis, size in zip(AXES[1:], SIZES[1:]):
        place = place * size + lax.axis_index(axis)
    return place


def repeat_kernel(block, out):
    for i in range(out.shape[0]):
        out[i] = block[...]


def iota(rows, cols, dim):
    return lax.broadcasted_iota(jnp.int32, (rows, cols), dim)


def ones_where(condition):
    return jnp.where(condition, 1.0, 0.0).astype(BF16)


def place_in_nine(start, v):
    p = start + v
    brick = jnp.where(p == 0, 0, jnp.where(p == 5, 2, 1))
    return brick, jnp.where(p == 0, 3, jnp.where(p == 5, 0, p - 1))


def window_matrix():
    row, col = iota(144, 144, 0), iota(144, 144, 1)
    s = lax.shift_right_logical(row, 4)
    sx = jnp.where(s >= 6, 2, jnp.where(s >= 3, 1, 0))
    v = jnp.bitwise_and(row, 15)
    kx, x = place_in_nine(sx, lax.shift_right_logical(v, 2))
    ky, y = place_in_nine(s - 3 * sx, jnp.bitwise_and(v, 3))
    return ones_where(col == (kx * 3 + ky) * 16 + x * 4 + y)


def row_order(inverse):
    inner, outer = iota(256, 256, int(inverse)), iota(256, 256, int(not inverse))
    return ones_where(
        outer == jnp.bitwise_and(inner, 63) * 4 + lax.shift_right_logical(inner, 6)
    )


def fetch(sems, *pairs):
    copies = [pltpu.make_async_copy(src, dst, sems.at[i]) for i, (src, dst) in enumerate(pairs)]
    for copy in copies:
        copy.start()
    return copies


def tap_rows(tap):
    window = (2 - tap // 9) * 3 + 2 - tap // 3 % 3
    return (window * 6 + 2 - tap % 3) * 64


def prepare_kernel(
    counts_in, pre_in, cot_in, gain_in, bias_in, weight_in, grad, near, far, frames,
    counts, pre, cot, gain, bias, weight, tiles, sems,
):
    copies = fetch(
        sems, (counts_in, counts), (pre_in, pre), (cot_in, cot), (gain_in, gain), (bias_in, bias),
        (weight_in, weight),
    )
    place = my_place()
    copies[5].wait()
    shift = jnp.bitwise_and(place, 15)
    at = iota(FRAME, ROWS, 1) + shift
    turned = jnp.where(at >= FRAME, at - FRAME, at)
    spread = ones_where((iota(FRAME, ROWS, 0) == turned) & (iota(FRAME, ROWS, 1) < FRAME))
    turned = dot(spread, weight[...])
    for i in range(5):
        tiles[i] = turned[i * 16 : (i + 1) * 16, :128].astype(BF16)
    extra = dot(ones_where(iota(16, ROWS, 1) == ROWS - 1), weight[...])
    row = iota(16, 64, 0)
    extra = jnp.where(
        row == 0, extra[:, :64], jnp.where(row == 1, extra[:, 64:128], extra[:, 128:])
    )
    tails = [turned[i * 16 : (i + 1) * 16, 128:] for i in range(5)] + [extra]
    for i in range(3):
        pair = jnp.concatenate([tails[2 * i], tails[2 * i + 1]], axis=1)
        tiles[5 + i] = pair.astype(BF16)
    mine = tiles[lax.shift_right_logical(place, 6)]
    for i in range(32):
        frames[i] = mine
    for copy in copies[:5]:
        copy.wait()
    count = counts[place]
    g = gain[...]
    for b in range(B):
        p = pre[b].astype(F32)
        u = cot[b].astype(F32)
        for z in range(4):
            pz = p[:, z * C : (z + 1) * C]
            uz = u[:, z * C : (z + 1) * C]
            gate = (g * pz + bias[...] > 0) & (b < count)
            grad[b, z] = jnp.where(gate, uz * g, 0.0).astype(BF16)
    core = jnp.bitwise_and(place, 1)
    near[0] = grad[jnp.where(core == 0, count - 1, 0)]
    far[0] = grad[jnp.where(core == 0, 0, count - 1)]


def conv_kernel(
    counts_in, near_in, fine_in, weight_in, grad, slab_low, slab_high, dev_near, dev_far,
    keep_out, send_out, taps_out, counts, near, fine, weight, sems, bricks, block, total, taps,
    keep, send,
):
    place = my_place()
    core = jnp.bitwise_and(place, 1)
    copies = fetch(
        sems, (near_in, near), (grad, bricks.at[0:4]), (slab_low, bricks.at[4:8]),
        (slab_high, bricks.at[8:12]), (dev_near, bricks.at[pl.ds(13 - core, 1)]),
        (dev_far, bricks.at[pl.ds(12 + core, 1)]),
        (counts_in, counts), (fine_in, fine), (weight_in, weight),
    )
    bricks[14:15] = jnp.zeros((1, 4, 16, C), BF16)
    window = window_matrix()
    for copy in copies[:6]:
        copy.wait()
    for b in range(B):
        slots = []
        for k in range(27):
            brick = near[b, k]
            away = lax.shift_right_arithmetic(brick, 2) - place
            slot = jnp.bitwise_and(brick, 3)
            at = jnp.where(away == 0, slot, 14)
            at = jnp.where(away == -DEVS, 4 + slot, at)
            at = jnp.where(away == DEVS, 8 + slot, at)
            at = jnp.where(away == -1, 12, at)
            at = jnp.where(away == 1, 13, at)
            slots.append(jnp.where(brick < 0, 14, at))
        for plane in range(6):
            kz, z = ((0, 3), (1, 0), (1, 1), (1, 2), (1, 3), (2, 0))[plane]
            for q in range(9):
                block[plane, q * 16 : (q + 1) * 16] = bricks[slots[q * 3 + kz], z]
        for plane in range(6):
            moved = dot(window, block[plane]).astype(BF16)
            for s in range(9):
                row = ((s * 6 + plane) * B + b) * 16
                taps[row : row + 16] = moved[s * 16 : (s + 1) * 16]
    leave = [pltpu.make_async_copy(taps, taps_out, sems.at[9])]
    leave[0].start()
    for copy in copies[6:]:
        copy.wait()
    count = counts[place]
    merged = lax.dot_general(
        fine[...], weight[...], (((1,), (1,)), ((), ())), preferred_element_type=F32
    )
    brick_of = lax.broadcasted_iota(jnp.int32, (256, C), 0) // 64
    merged = jnp.where(brick_of < count, merged, 0.0).astype(BF16)
    merged = jnp.transpose(dot(row_order(False), merged)).astype(BF16)
    for tap in range(27):
        row = tap_rows(tap)
        term = dot(merged, taps[row : row + 256])
        at = tap * C
        end = at + C
        while at < end:
            owner = at // ROWS
            stop = min(end, (owner + 1) * ROWS)
            to = (owner // 2) * ROWS + at % ROWS
            total[owner % 2, :, to : to + stop - at] = term[:, at - tap * C : stop - tap * C]
            at = stop
    for i, (held, out, half) in enumerate(((send, send_out, 1 - core), (keep, keep_out, core))):
        for slab in range(SLABS):
            held[slab] = total[half, slab * COLS : (slab + 1) * COLS].astype(BF16)
        leave.append(pltpu.make_async_copy(held, out, sems.at[10 + i]))
        leave[-1].start()
    for copy in leave:
        copy.wait()


def back_kernel(
    counts_in, fine_in, taps_in, mine, other, gm, term, counts, fine, taps, sems, both, whole,
):
    place = my_place()
    core = jnp.bitwise_and(place, 1)
    copies = fetch(
        sems, (mine, both.at[core]), (other, both.at[1 - core]), (taps_in, taps),
        (fine_in, fine), (counts_in, counts),
    )
    for copy in copies[:2]:
        copy.wait()
    row = iota(16, 128, 0)
    held = None
    for owner in range(DEVS):
        first = ROWS * owner // 16 * 16
        shift = owner % 16
        tiles = [both[owner % 2, i, owner // 2] for i in range(SLABS)]
        for i in range(1, 5):
            whole[first + i * 16 : first + (i + 1) * 16, :128] = tiles[i]
            half = i % 2 * 64
            whole[first + i * 16 : first + (i + 1) * 16, 128:] = tiles[5 + i // 2][
                :, half : half + 64
            ]
        main, tail = tiles[0].astype(F32), tiles[5][:, :64].astype(F32)
        extra = tiles[7][:, 64:].astype(F32)
        long = jnp.concatenate([extra[0:1], extra[1:2]], axis=1)
        ends = [jnp.where(row < shift, main, jnp.where(row == shift, long, 0.0))]
        short = row[:, :64]
        ends.append(jnp.where(short < shift, tail, jnp.where(short == shift, extra[2:3], 0.0)))
        if shift:
            main = jnp.where(row >= shift, main, held[0])
            tail = jnp.where(short >= shift, tail, held[1])
        whole[first : first + 16, :128] = main.astype(BF16)
        whole[first : first + 16, 128:] = tail.astype(BF16)
        if shift == 15:
            whole[first + 80 : first + 96, :128] = ends[0].astype(BF16)
            whole[first + 80 : first + 96, 128:] = ends[1].astype(BF16)
        held = ends
    for copy in copies[2:]:
        copy.wait()
    back = jnp.zeros((256, C), F32)
    for tap in range(27):
        row = tap_rows(tap)
        back = back + dot(taps[row : row + 256], whole[tap * C : (tap + 1) * C])
    brick_of = lax.broadcasted_iota(jnp.int32, (256, C), 0) // 16 % B
    count = counts[place]
    back = jnp.where(brick_of < count, back, 0.0).astype(BF16)
    back = dot(row_order(True), back)
    gm[...] = back.astype(BF16)
    result = dot(jnp.transpose(back).astype(BF16), fine[...])
    for i in range(PIECES):
        piece = result[i % 8 * 24 : i % 8 * 24 + 24, i // 8 * 128 : i // 8 * 128 + 128]
        term[i // 24, i % 24] = piece.astype(BF16)


def fine_kernel(gm_in, weight_in, fine_out, gm, weight, fine_grad, sems):
    for copy in fetch(sems, (gm_in, gm), (weight_in, weight)):
        copy.wait()
    fine_grad[...] = dot(gm[...], weight[...]).astype(BF16)
    for copy in fetch(sems.at[2:], (fine_grad, fine_out)):
        copy.wait()


def join_kernel(parts, out):
    core = lax.axis_index("c")
    for i in range(24):
        out[i] = (parts[0, core, i].astype(F32) + parts[1, core, i].astype(F32)).astype(BF16)
    for i in range(24, 32):
        out[i] = jnp.zeros((24, 128), BF16)


def spread_kernel(parts, out):
    total = parts[0].astype(F32)
    for i in range(1, 32):
        total = total + parts[i].astype(F32)
    for i in range(SLABS):
        out[i] = total.astype(BF16)


def split_kernel(keep, received, *outs):
    x = lax.axis_index("x")
    for dx, out in enumerate(outs):
        for zl in range(2):
            slab = zl * 4 + jnp.bitwise_and(x + dx, 3)
            out[zl] = (keep[slab].astype(F32) + received[slab].astype(F32)).astype(BF16)


def halve_kernel(a, b, c, d, keep, send):
    zl = lax.axis_index("zl")
    for out, half in ((keep, zl), (send, 1 - zl)):
        total = a[half].astype(F32) + b[half].astype(F32) + c[half].astype(F32)
        out[...] = (total + d[half].astype(F32)).astype(BF16)


def both_kernel(parts, keep, received, out):
    merge = parts[0].astype(F32)
    for i in range(1, SLABS):
        merge = merge + parts[i].astype(F32)
    merge = merge.astype(BF16)
    conv = keep[...].astype(F32) + received[...].astype(F32)
    pad = jnp.zeros((COLS, 128 - ROWS), BF16)
    for i in range(32):
        piece = conv[:, i * ROWS : (i + 1) * ROWS].astype(BF16)
        out[i, 0] = jnp.concatenate([piece, pad], axis=1)
        out[i, 1] = merge


def last_kernel(parts, merge_out, conv_out, merge, conv, sems):
    core = jnp.bitwise_and(my_place(), 1)
    for i in range(PIECES):
        row, col = i % 8 * 24, i // 8 * 128
        merge[row : row + 24, col : col + 128] = parts[i // 24, i % 24, 1].astype(F32)
    copies = fetch(sems, (merge, merge_out))
    total = parts[core, 0, 0].astype(F32)
    for i in range(1, 32):
        total = total + parts[core, i, 0].astype(F32)
    conv[...] = total[:, :ROWS]
    copies += fetch(sems.at[1:], (conv, conv_out))
    for copy in copies:
        copy.wait()


def call(kernel, outs, specs, scratch=(), flops=0, out_spec=None, vmem=20):
    return pl.pallas_call(
        kernel,
        out_shape=outs,
        in_specs=specs,
        out_specs=out_spec or jax.tree.map(lambda _: VMEM, outs),
        scratch_shapes=scratch,
        cost_estimate=pl.CostEstimate(flops=flops, bytes_accessed=0, transcendentals=0),
        compiler_params=pltpu.CompilerParams(vmem_limit_bytes=vmem << 20),
    )


def shape(*dims, dtype=BF16):
    return jax.ShapeDtypeStruct(dims, dtype)


def swap(x, axes):
    return lax.all_to_all(x, axes, 0, 0, tiled=True)


def local(
    fine_input, merge_weight, conv_weight, pre_act, norm_gain, norm_bias, cotangent, counts, neighbours
):
    counts_scratch = pltpu.SMEM((SLABS * DEVS,), jnp.int32)
    grad, near, far, frames = call(
        prepare_kernel,
        (shape(B, 4, 16, C), shape(1, 4, 16, C), shape(1, 4, 16, C), shape(32, 16, 128)),
        [HBM] * 6,
        [
            counts_scratch,
            pltpu.VMEM((B, 16, 4 * C), BF16),
            pltpu.VMEM((B, 16, 4 * C), BF16),
            pltpu.VMEM((1, C), F32),
            pltpu.VMEM((1, C), F32),
            pltpu.VMEM((ROWS, C), BF16),
            pltpu.VMEM((SLABS, 16, 128), BF16),
            pltpu.SemaphoreType.DMA((6,)),
        ],
        vmem=60,
    )(counts, pre_act, cotangent, norm_gain.reshape(1, C), norm_bias.reshape(1, C), conv_weight)

    def shifted(x, axes, count, step):
        pairs = [(i, i + step) for i in range(count) if 0 <= i + step < count]
        return lax.ppermute(x, axes, pairs)

    def flipped(x):
        return lax.ppermute(x, "c", [(0, 1), (1, 0)])

    slab_low = shifted(grad, SLAB, SLABS, 1)
    slab_high = shifted(grad, SLAB, SLABS, -1)
    frames = swap(frames, ("zh", "y"))
    dev_near = flipped(near)
    frames, slab_low, slab_high, dev_near, far = lax.optimization_barrier(
        (frames, slab_low, slab_high, dev_near, far)
    )
    ups = [(i, i + 1) for i in range(1, DEVS - 1, 2)]
    dev_far = lax.ppermute(far, DEV, ups + [(j, i) for i, j in ups])
    frames = call(repeat_kernel, shape(SLABS, 32, 16, 128), [VMEM])(frames)
    frames = swap(frames, SLAB)

    fine_scratch = pltpu.VMEM((256, 768), BF16)
    weight_scratch = pltpu.VMEM((C, 768), BF16)
    merge_weight = merge_weight.T
    keep, send, taps = call(
        conv_kernel,
        (shape(SLABS, COLS, HALF), shape(SLABS, COLS, HALF), shape(3456, C)),
        [HBM] * 9,
        [
            counts_scratch,
            pltpu.SMEM((B, 27), jnp.int32),
            fine_scratch,
            weight_scratch,
            pltpu.SemaphoreType.DMA((12,)),
            pltpu.VMEM((15, 4, 16, C), BF16),
            pltpu.VMEM((6, 144, C), BF16),
            pltpu.VMEM((2, C, HALF), F32),
            pltpu.VMEM((3456, C), BF16),
            pltpu.VMEM((SLABS, COLS, HALF), BF16),
            pltpu.VMEM((SLABS, COLS, HALF), BF16),
        ],
        flops=6 * 10**9,
        out_spec=(HBM, HBM, HBM),
        vmem=60,
    )(
        counts, neighbours, fine_input, merge_weight, grad, slab_low, slab_high, dev_near, dev_far
    )

    frames, taps = lax.optimization_barrier((frames, taps))
    other = flipped(frames)
    gm, term = call(
        back_kernel,
        (shape(256, C), shape(2, 24, 24, 128)),
        [HBM] * 5,
        [
            counts_scratch,
            fine_scratch,
            pltpu.VMEM((3456, C), BF16),
            pltpu.SemaphoreType.DMA((5,)),
            pltpu.VMEM((2, SLABS, 32, 16, 128), BF16),
            pltpu.VMEM((27 * C, C), BF16),
        ],
        flops=4 * 10**9,
        vmem=60,
    )(counts, fine_input, taps, frames, other)
    fine_grad = call(
        fine_kernel,
        shape(256, 768),
        [HBM] * 2,
        [
            pltpu.VMEM((256, C), BF16),
            weight_scratch,
            fine_scratch,
            pltpu.SemaphoreType.DMA((3,)),
        ],
        flops=10**9,
        out_spec=HBM,
    )(gm, merge_weight)

    term = lax.all_gather(term, "c", axis=0, tiled=False)
    term = call(join_kernel, shape(32, 24, 128), [VMEM])(term)
    term = swap(term, ("zh", "y"))
    term = call(spread_kernel, shape(SLABS, 24, 128), [VMEM])(term)
    conv = call(split_kernel, (shape(2, COLS, HALF),) * 4, [VMEM] * 2)(keep, flipped(send))
    moved = [
        lax.ppermute(conv[dx], "x", [(i, (i + dx) % 4) for i in range(4)]) for dx in (1, 2, 3)
    ]
    term, moved = lax.optimization_barrier((term, moved))
    term = swap(term, SLAB)
    keep, send = call(halve_kernel, (shape(COLS, HALF),) * 2, [VMEM] * 4)(conv[0], *moved)
    received = lax.ppermute(send, "zl", [(0, 1), (1, 0)])
    term = call(both_kernel, shape(32, 2, 24, 128), [VMEM] * 3)(term, keep, received)
    term = swap(term, ("zh", "y"))
    term = lax.all_gather(term, "c", axis=0, tiled=False)
    merge_grad, conv_grad = call(
        last_kernel,
        (shape(C, 768, dtype=F32), shape(COLS, ROWS, dtype=F32)),
        [VMEM],
        [
            pltpu.VMEM((C, 768), F32),
            pltpu.VMEM((COLS, ROWS), F32),
            pltpu.SemaphoreType.DMA((2,)),
        ],
        out_spec=(HBM, HBM),
    )(term)
    return fine_grad, merge_grad.T, conv_grad.T


def solution(mesh):
    fine_mesh = Mesh(mesh.devices.reshape(SIZES), AXES)
    every = SLAB + DEV
    in_specs = (
        P(every, None),
        P(),
        P(DEV, None),
        P(every, None, None),
        P(),
        P(),
        P(every, None, None),
        P(),
        P(every, None),
    )
    out_specs = (P(every, None), P(), P(DEV, SLAB))
    return jax.shard_map(
        local, mesh=fine_mesh, in_specs=in_specs, out_specs=out_specs, check_vma=False
    )
```

```python
import jax
import jax.numpy as jnp
from jax import lax
from jax.experimental import pallas as pl
from jax.experimental.pallas import tpu as pltpu
from jax.sharding import Mesh, PartitionSpec as P

F32 = jnp.float32
BF16 = jnp.bfloat16

AXES = ("zl", "x", "zh", "y", "c")
SIZES = (2, 4, 4, 8, 2)
SLAB = ("zl", "x")
DEV = ("zh", "y", "c")
SLABS = 8
DEVS = 64
B = 4
C = 192
ROWS = 81
FRAME = 80
HALF = 32 * ROWS
COLS = C // SLABS
PIECES = 48
WIDE = 2688

VMEM = pl.BlockSpec(memory_space=pltpu.VMEM)
HBM = pl.BlockSpec(memory_space=pltpu.HBM)


def dot(a, b):
    return jnp.dot(a, b, preferred_element_type=F32)


def my_place():
    place = lax.axis_index(AXES[0])
    for axis, size in zip(AXES[1:], SIZES[1:]):
        place = place * size + lax.axis_index(axis)
    return place


def repeat_kernel(block, out):
    for i in range(out.shape[0]):
        out[i] = block[...]


def iota(rows, cols, dim):
    return lax.broadcasted_iota(jnp.int32, (rows, cols), dim)


def ones_where(condition):
    return jnp.where(condition, 1.0, 0.0).astype(BF16)


def place_in_nine(start, v):
    p = start + v
    brick = jnp.where(p == 0, 0, jnp.where(p == 5, 2, 1))
    return brick, jnp.where(p == 0, 3, jnp.where(p == 5, 0, p - 1))


def window_matrix():
    row, col = iota(144, 144, 0), iota(144, 144, 1)
    s = lax.shift_right_logical(row, 4)
    sx = jnp.where(s >= 6, 2, jnp.where(s >= 3, 1, 0))
    v = jnp.bitwise_and(row, 15)
    kx, x = place_in_nine(sx, lax.shift_right_logical(v, 2))
    ky, y = place_in_nine(s - 3 * sx, jnp.bitwise_and(v, 3))
    return ones_where(col == (kx * 3 + ky) * 16 + x * 4 + y)


def row_order(inverse):
    inner, outer = iota(256, 256, int(inverse)), iota(256, 256, int(not inverse))
    return ones_where(
        outer == jnp.bitwise_and(inner, 63) * 4 + lax.shift_right_logical(inner, 6)
    )


def fetch(sems, *pairs):
    copies = [pltpu.make_async_copy(src, dst, sems.at[i]) for i, (src, dst) in enumerate(pairs)]
    for copy in copies:
        copy.start()
    return copies


def tap_rows(tap):
    window = (2 - tap // 9) * 3 + 2 - tap // 3 % 3
    return (window * 6 + 2 - tap % 3) * 64


def prepare_kernel(
    counts_in, pre_in, cot_in, gain_in, bias_in, weight_in, grad, near, far, frames,
    counts, pre, cot, gain, bias, weight, tiles, sems,
):
    copies = fetch(
        sems, (counts_in, counts), (pre_in, pre), (cot_in, cot), (gain_in, gain), (bias_in, bias),
        (weight_in, weight),
    )
    place = my_place()
    copies[5].wait()
    shift = jnp.bitwise_and(place, 15)
    at = iota(FRAME, ROWS, 1) + shift
    turned = jnp.where(at >= FRAME, at - FRAME, at)
    spread = ones_where((iota(FRAME, ROWS, 0) == turned) & (iota(FRAME, ROWS, 1) < FRAME))
    turned = dot(spread, weight[...])
    for i in range(5):
        tiles[i] = turned[i * 16 : (i + 1) * 16, :128].astype(BF16)
    extra = dot(ones_where(iota(16, ROWS, 1) == ROWS - 1), weight[...])
    row = iota(16, 64, 0)
    extra = jnp.where(
        row == 0, extra[:, :64], jnp.where(row == 1, extra[:, 64:128], extra[:, 128:])
    )
    tails = [turned[i * 16 : (i + 1) * 16, 128:] for i in range(5)] + [extra]
    for i in range(3):
        pair = jnp.concatenate([tails[2 * i], tails[2 * i + 1]], axis=1)
        tiles[5 + i] = pair.astype(BF16)
    mine = tiles[lax.shift_right_logical(place, 6)]
    for i in range(32):
        frames[i] = mine
    for copy in copies[:5]:
        copy.wait()
    count = counts[place]
    g = gain[...]
    for b in range(B):
        p = pre[b].astype(F32)
        u = cot[b].astype(F32)
        for z in range(4):
            pz = p[:, z * C : (z + 1) * C]
            uz = u[:, z * C : (z + 1) * C]
            gate = (g * pz + bias[...] > 0) & (b < count)
            grad[b, z] = jnp.where(gate, uz * g, 0.0).astype(BF16)
    core = jnp.bitwise_and(place, 1)
    near[0] = grad[jnp.where(core == 0, count - 1, 0)]
    far[0] = grad[jnp.where(core == 0, 0, count - 1)]


def conv_kernel(
    counts_in, near_in, fine_in, weight_in, grad, slab_low, slab_high, dev_near, dev_far,
    keep_out, send_out, taps_out, counts, near, fine, weight, sems, bricks, block, total, taps,
    keep, send,
):
    place = my_place()
    core = jnp.bitwise_and(place, 1)
    copies = fetch(
        sems, (near_in, near), (grad, bricks.at[0:4]), (slab_low, bricks.at[4:8]),
        (slab_high, bricks.at[8:12]), (dev_near, bricks.at[pl.ds(13 - core, 1)]),
        (dev_far, bricks.at[pl.ds(12 + core, 1)]),
        (counts_in, counts), (fine_in, fine), (weight_in, weight),
    )
    bricks[14:15] = jnp.zeros((1, 4, 16, C), BF16)
    window = window_matrix()
    for copy in copies[:6]:
        copy.wait()
    for b in range(B):
        slots = []
        for k in range(27):
            brick = near[b, k]
            away = lax.shift_right_arithmetic(brick, 2) - place
            slot = jnp.bitwise_and(brick, 3)
            at = jnp.where(away == 0, slot, 14)
            at = jnp.where(away == -DEVS, 4 + slot, at)
            at = jnp.where(away == DEVS, 8 + slot, at)
            at = jnp.where(away == -1, 12, at)
            at = jnp.where(away == 1, 13, at)
            slots.append(jnp.where(brick < 0, 14, at))
        for plane in range(6):
            kz, z = ((0, 3), (1, 0), (1, 1), (1, 2), (1, 3), (2, 0))[plane]
            for q in range(9):
                block[plane, q * 16 : (q + 1) * 16] = bricks[slots[q * 3 + kz], z]
        for plane in range(6):
            moved = dot(window, block[plane]).astype(BF16)
            for s in range(9):
                row = ((s * 6 + plane) * B + b) * 16
                taps[row : row + 16] = moved[s * 16 : (s + 1) * 16]
    leave = [pltpu.make_async_copy(taps, taps_out, sems.at[9])]
    leave[0].start()
    for copy in copies[6:]:
        copy.wait()
    count = counts[place]
    merged = lax.dot_general(
        fine[...], weight[...], (((1,), (1,)), ((), ())), preferred_element_type=F32
    )
    brick_of = lax.broadcasted_iota(jnp.int32, (256, C), 0) // 64
    merged = jnp.where(brick_of < count, merged, 0.0).astype(BF16)
    merged = jnp.transpose(dot(row_order(False), merged)).astype(BF16)
    for tap in range(27):
        row = tap_rows(tap)
        term = dot(merged, taps[row : row + 256])
        at = tap * C
        end = at + C
        while at < end:
            owner = at // ROWS
            stop = min(end, (owner + 1) * ROWS)
            to = (owner // 2) * ROWS + at % ROWS
            total[owner % 2, :, to : to + stop - at] = term[:, at - tap * C : stop - tap * C]
            at = stop
    for i, (held, out, half) in enumerate(((send, send_out, 1 - core), (keep, keep_out, core))):
        for slab in range(SLABS):
            held[slab] = total[half, slab * COLS : (slab + 1) * COLS].astype(BF16)
        leave.append(pltpu.make_async_copy(held, out, sems.at[10 + i]))
        leave[-1].start()
    for copy in leave:
        copy.wait()


def back_kernel(
    counts_in, fine_in, taps_in, mine, other, gm, term, counts, fine, taps, sems, both, whole,
):
    place = my_place()
    core = jnp.bitwise_and(place, 1)
    copies = fetch(
        sems, (mine, both.at[core]), (other, both.at[1 - core]), (taps_in, taps),
        (fine_in, fine), (counts_in, counts),
    )
    for copy in copies[:2]:
        copy.wait()
    row = iota(16, 128, 0)
    held = None
    for owner in range(DEVS):
        first = ROWS * owner // 16 * 16
        shift = owner % 16
        tiles = [both[owner % 2, i, owner // 2] for i in range(SLABS)]
        for i in range(1, 5):
            whole[first + i * 16 : first + (i + 1) * 16, :128] = tiles[i]
            half = i % 2 * 64
            whole[first + i * 16 : first + (i + 1) * 16, 128:] = tiles[5 + i // 2][
                :, half : half + 64
            ]
        main, tail = tiles[0].astype(F32), tiles[5][:, :64].astype(F32)
        extra = tiles[7][:, 64:].astype(F32)
        long = jnp.concatenate([extra[0:1], extra[1:2]], axis=1)
        ends = [jnp.where(row < shift, main, jnp.where(row == shift, long, 0.0))]
        short = row[:, :64]
        ends.append(jnp.where(short < shift, tail, jnp.where(short == shift, extra[2:3], 0.0)))
        if shift:
            main = jnp.where(row >= shift, main, held[0])
            tail = jnp.where(short >= shift, tail, held[1])
        whole[first : first + 16, :128] = main.astype(BF16)
        whole[first : first + 16, 128:] = tail.astype(BF16)
        if shift == 15:
            whole[first + 80 : first + 96, :128] = ends[0].astype(BF16)
            whole[first + 80 : first + 96, 128:] = ends[1].astype(BF16)
        held = ends
    for copy in copies[2:]:
        copy.wait()
    back = jnp.zeros((256, C), F32)
    for tap in range(27):
        row = tap_rows(tap)
        back = back + dot(taps[row : row + 256], whole[tap * C : (tap + 1) * C])
    brick_of = lax.broadcasted_iota(jnp.int32, (256, C), 0) // 16 % B
    count = counts[place]
    back = jnp.where(brick_of < count, back, 0.0).astype(BF16)
    back = dot(row_order(True), back)
    gm[...] = back.astype(BF16)
    result = dot(jnp.transpose(back).astype(BF16), fine[...])
    for i in range(PIECES):
        piece = result[i % 8 * 24 : i % 8 * 24 + 24, i // 8 * 128 : i // 8 * 128 + 128]
        term[i // 24, i % 24] = piece.astype(BF16)


def fine_kernel(gm_in, weight_in, fine_out, gm, weight, fine_grad, sems):
    for copy in fetch(sems, (gm_in, gm), (weight_in, weight)):
        copy.wait()
    fine_grad[...] = dot(gm[...], weight[...]).astype(BF16)
    for copy in fetch(sems.at[2:], (fine_grad, fine_out)):
        copy.wait()


def join_kernel(parts, out):
    core = lax.axis_index("c")
    for i in range(24):
        out[i] = (parts[0, core, i].astype(F32) + parts[1, core, i].astype(F32)).astype(BF16)
    for i in range(24, 32):
        out[i] = jnp.zeros((24, 128), BF16)


def spread_kernel(parts, keep, received, out):
    merge = parts[0].astype(F32)
    for i in range(1, 32):
        merge = merge + parts[i].astype(F32)
    for i in range(SLABS):
        out[i, :, :HALF] = (keep[i].astype(F32) + received[i].astype(F32)).astype(BF16)
        out[i, :, HALF:WIDE] = jnp.zeros((COLS, WIDE - HALF), BF16)
        out[i, :, WIDE:] = merge.astype(BF16)


def both_kernel(parts, out):
    total = parts[0].astype(F32)
    for i in range(1, SLABS):
        total = total + parts[i].astype(F32)
    merge = total[:, WIDE:].astype(BF16)
    pad = jnp.zeros((COLS, 128 - ROWS), BF16)
    for i in range(32):
        piece = total[:, i * ROWS : (i + 1) * ROWS].astype(BF16)
        out[i, 0] = jnp.concatenate([piece, pad], axis=1)
        out[i, 1] = merge


def last_kernel(parts, merge_out, conv_out, merge, conv, sems):
    core = jnp.bitwise_and(my_place(), 1)
    for i in range(PIECES):
        row, col = i % 8 * 24, i // 8 * 128
        merge[row : row + 24, col : col + 128] = parts[i // 24, i % 24, 1].astype(F32)
    copies = fetch(sems, (merge, merge_out))
    total = parts[core, 0, 0].astype(F32)
    for i in range(1, 32):
        total = total + parts[core, i, 0].astype(F32)
    conv[...] = total[:, :ROWS]
    copies += fetch(sems.at[1:], (conv, conv_out))
    for copy in copies:
        copy.wait()


def call(kernel, outs, specs, scratch=(), flops=0, out_spec=None, vmem=20):
    return pl.pallas_call(
        kernel,
        out_shape=outs,
        in_specs=specs,
        out_specs=out_spec or jax.tree.map(lambda _: VMEM, outs),
        scratch_shapes=scratch,
        cost_estimate=pl.CostEstimate(flops=flops, bytes_accessed=0, transcendentals=0),
        compiler_params=pltpu.CompilerParams(vmem_limit_bytes=vmem << 20),
    )


def shape(*dims, dtype=BF16):
    return jax.ShapeDtypeStruct(dims, dtype)


def swap(x, axes):
    return lax.all_to_all(x, axes, 0, 0, tiled=True)


def local(
    fine_input, merge_weight, conv_weight, pre_act, norm_gain, norm_bias, cotangent, counts, neighbours
):
    counts_scratch = pltpu.SMEM((SLABS * DEVS,), jnp.int32)
    grad, near, far, frames = call(
        prepare_kernel,
        (shape(B, 4, 16, C), shape(1, 4, 16, C), shape(1, 4, 16, C), shape(32, 16, 128)),
        [HBM] * 6,
        [
            counts_scratch,
            pltpu.VMEM((B, 16, 4 * C), BF16),
            pltpu.VMEM((B, 16, 4 * C), BF16),
            pltpu.VMEM((1, C), F32),
            pltpu.VMEM((1, C), F32),
            pltpu.VMEM((ROWS, C), BF16),
            pltpu.VMEM((SLABS, 16, 128), BF16),
            pltpu.SemaphoreType.DMA((6,)),
        ],
        vmem=60,
    )(counts, pre_act, cotangent, norm_gain.reshape(1, C), norm_bias.reshape(1, C), conv_weight)

    def shifted(x, axes, count, step):
        pairs = [(i, i + step) for i in range(count) if 0 <= i + step < count]
        return lax.ppermute(x, axes, pairs)

    def flipped(x):
        return lax.ppermute(x, "c", [(0, 1), (1, 0)])

    slab_low = shifted(grad, SLAB, SLABS, 1)
    slab_high = shifted(grad, SLAB, SLABS, -1)
    frames = swap(frames, ("zh", "y"))
    dev_near = flipped(near)
    frames, slab_low, slab_high, dev_near, far = lax.optimization_barrier(
        (frames, slab_low, slab_high, dev_near, far)
    )
    ups = [(i, i + 1) for i in range(1, DEVS - 1, 2)]
    dev_far = lax.ppermute(far, DEV, ups + [(j, i) for i, j in ups])
    frames = call(repeat_kernel, shape(SLABS, 32, 16, 128), [VMEM])(frames)
    frames = swap(frames, SLAB)

    fine_scratch = pltpu.VMEM((256, 768), BF16)
    weight_scratch = pltpu.VMEM((C, 768), BF16)
    merge_weight = merge_weight.T
    keep, send, taps = call(
        conv_kernel,
        (shape(SLABS, COLS, HALF), shape(SLABS, COLS, HALF), shape(3456, C)),
        [HBM] * 9,
        [
            counts_scratch,
            pltpu.SMEM((B, 27), jnp.int32),
            fine_scratch,
            weight_scratch,
            pltpu.SemaphoreType.DMA((12,)),
            pltpu.VMEM((15, 4, 16, C), BF16),
            pltpu.VMEM((6, 144, C), BF16),
            pltpu.VMEM((2, C, HALF), F32),
            pltpu.VMEM((3456, C), BF16),
            pltpu.VMEM((SLABS, COLS, HALF), BF16),
            pltpu.VMEM((SLABS, COLS, HALF), BF16),
        ],
        flops=6 * 10**9,
        out_spec=(HBM, HBM, HBM),
        vmem=60,
    )(
        counts, neighbours, fine_input, merge_weight, grad, slab_low, slab_high, dev_near, dev_far
    )

    frames, taps = lax.optimization_barrier((frames, taps))
    other = flipped(frames)
    gm, term = call(
        back_kernel,
        (shape(256, C), shape(2, 24, 24, 128)),
        [HBM] * 5,
        [
            counts_scratch,
            fine_scratch,
            pltpu.VMEM((3456, C), BF16),
            pltpu.SemaphoreType.DMA((5,)),
            pltpu.VMEM((2, SLABS, 32, 16, 128), BF16),
            pltpu.VMEM((27 * C, C), BF16),
        ],
        flops=4 * 10**9,
        vmem=60,
    )(counts, fine_input, taps, frames, other)
    fine_grad = call(
        fine_kernel,
        shape(256, 768),
        [HBM] * 2,
        [
            pltpu.VMEM((256, C), BF16),
            weight_scratch,
            fine_scratch,
            pltpu.SemaphoreType.DMA((3,)),
        ],
        flops=10**9,
        out_spec=HBM,
    )(gm, merge_weight)

    term = lax.all_gather(term, "c", axis=0, tiled=False)
    term = call(join_kernel, shape(32, 24, 128), [VMEM])(term)
    term = swap(term, ("zh", "y"))
    term = call(spread_kernel, shape(SLABS, COLS, WIDE + 128), [VMEM] * 3)(
        term, keep, flipped(send)
    )
    term = swap(term, SLAB)
    term = call(both_kernel, shape(32, 2, 24, 128), [VMEM])(term)
    term = swap(term, ("zh", "y"))
    term = lax.all_gather(term, "c", axis=0, tiled=False)
    merge_grad, conv_grad = call(
        last_kernel,
        (shape(C, 768, dtype=F32), shape(COLS, ROWS, dtype=F32)),
        [VMEM],
        [
            pltpu.VMEM((C, 768), F32),
            pltpu.VMEM((COLS, ROWS), F32),
            pltpu.SemaphoreType.DMA((2,)),
        ],
        out_spec=(HBM, HBM),
    )(term)
    return fine_grad, merge_grad.T, conv_grad.T


def solution(mesh):
    fine_mesh = Mesh(mesh.devices.reshape(SIZES), AXES)
    every = SLAB + DEV
    in_specs = (
        P(every, None),
        P(),
        P(DEV, None),
        P(every, None, None),
        P(),
        P(),
        P(every, None, None),
        P(),
        P(every, None),
    )
    out_specs = (P(every, None), P(), P(DEV, SLAB))
    return jax.shard_map(
        local, mesh=fine_mesh, in_specs=in_specs, out_specs=out_specs, check_vma=False
    )
```

```python
import jax
import jax.numpy as jnp
from jax import lax
from jax.experimental import pallas as pl
from jax.experimental.pallas import tpu as pltpu
from jax.sharding import Mesh, PartitionSpec as P

F32 = jnp.float32
BF16 = jnp.bfloat16

AXES = ("zl", "x", "zh", "y", "c")
SIZES = (2, 4, 4, 8, 2)
SLAB = ("zl", "x")
DEV = ("zh", "y", "c")
SLABS = 8
DEVS = 64
B = 4
C = 192
ROWS = 81
FRAME = 80
HALF = 32 * ROWS
COLS = C // SLABS
PIECES = 48
WIDE = 2688

VMEM = pl.BlockSpec(memory_space=pltpu.VMEM)
HBM = pl.BlockSpec(memory_space=pltpu.HBM)


def dot(a, b):
    return jnp.dot(a, b, preferred_element_type=F32)


def my_place():
    place = lax.axis_index(AXES[0])
    for axis, size in zip(AXES[1:], SIZES[1:]):
        place = place * size + lax.axis_index(axis)
    return place


def repeat_kernel(block, out):
    for i in range(out.shape[0]):
        out[i] = block[...]


def iota(rows, cols, dim):
    return lax.broadcasted_iota(jnp.int32, (rows, cols), dim)


def ones_where(condition):
    return jnp.where(condition, 1.0, 0.0).astype(BF16)


def place_in_nine(start, v):
    p = start + v
    brick = jnp.where(p == 0, 0, jnp.where(p == 5, 2, 1))
    return brick, jnp.where(p == 0, 3, jnp.where(p == 5, 0, p - 1))


def window_matrix():
    row, col = iota(144, 144, 0), iota(144, 144, 1)
    s = lax.shift_right_logical(row, 4)
    sx = jnp.where(s >= 6, 2, jnp.where(s >= 3, 1, 0))
    v = jnp.bitwise_and(row, 15)
    kx, x = place_in_nine(sx, lax.shift_right_logical(v, 2))
    ky, y = place_in_nine(s - 3 * sx, jnp.bitwise_and(v, 3))
    return ones_where(col == (kx * 3 + ky) * 16 + x * 4 + y)


def row_order(inverse):
    inner, outer = iota(256, 256, int(inverse)), iota(256, 256, int(not inverse))
    return ones_where(
        outer == jnp.bitwise_and(inner, 63) * 4 + lax.shift_right_logical(inner, 6)
    )


def fetch(sems, *pairs):
    copies = [pltpu.make_async_copy(src, dst, sems.at[i]) for i, (src, dst) in enumerate(pairs)]
    for copy in copies:
        copy.start()
    return copies


def tap_rows(tap):
    window = (2 - tap // 9) * 3 + 2 - tap // 3 % 3
    return (window * 6 + 2 - tap % 3) * 64


def prepare_kernel(
    counts_in, pre_in, cot_in, gain_in, bias_in, weight_in, grad, near, far, frames,
    counts, pre, cot, gain, bias, weight, tiles, sems,
):
    copies = fetch(
        sems, (counts_in, counts), (pre_in, pre), (cot_in, cot), (gain_in, gain), (bias_in, bias),
        (weight_in, weight),
    )
    place = my_place()
    copies[5].wait()
    shift = jnp.bitwise_and(place, 15)
    at = iota(FRAME, ROWS, 1) + shift
    turned = jnp.where(at >= FRAME, at - FRAME, at)
    spread = ones_where((iota(FRAME, ROWS, 0) == turned) & (iota(FRAME, ROWS, 1) < FRAME))
    turned = dot(spread, weight[...])
    for i in range(5):
        tiles[i] = turned[i * 16 : (i + 1) * 16, :128].astype(BF16)
    extra = dot(ones_where(iota(16, ROWS, 1) == ROWS - 1), weight[...])
    row = iota(16, 64, 0)
    extra = jnp.where(
        row == 0, extra[:, :64], jnp.where(row == 1, extra[:, 64:128], extra[:, 128:])
    )
    tails = [turned[i * 16 : (i + 1) * 16, 128:] for i in range(5)] + [extra]
    for i in range(3):
        pair = jnp.concatenate([tails[2 * i], tails[2 * i + 1]], axis=1)
        tiles[5 + i] = pair.astype(BF16)
    mine = tiles[lax.shift_right_logical(place, 6)]
    for i in range(32):
        frames[i] = mine
    for copy in copies[:5]:
        copy.wait()
    count = counts[place]
    g = gain[...]
    for b in range(B):
        p = pre[b].astype(F32)
        u = cot[b].astype(F32)
        for z in range(4):
            pz = p[:, z * C : (z + 1) * C]
            uz = u[:, z * C : (z + 1) * C]
            gate = (g * pz + bias[...] > 0) & (b < count)
            grad[b, z] = jnp.where(gate, uz * g, 0.0).astype(BF16)
    core = jnp.bitwise_and(place, 1)
    near[0] = grad[jnp.where(core == 0, count - 1, 0)]
    far[0] = grad[jnp.where(core == 0, 0, count - 1)]


def conv_kernel(
    counts_in, near_in, fine_in, weight_in, grad, slab_low, slab_high, dev_near, dev_far,
    keep_out, send_out, taps_out, counts, near, fine, weight, sems, bricks, block, total, taps,
    keep, send,
):
    place = my_place()
    core = jnp.bitwise_and(place, 1)
    copies = fetch(
        sems, (near_in, near), (grad, bricks.at[0:4]), (slab_low, bricks.at[4:8]),
        (slab_high, bricks.at[8:12]), (dev_near, bricks.at[pl.ds(13 - core, 1)]),
        (dev_far, bricks.at[pl.ds(12 + core, 1)]),
        (counts_in, counts), (fine_in, fine), (weight_in, weight),
    )
    bricks[14:15] = jnp.zeros((1, 4, 16, C), BF16)
    window = window_matrix()
    for copy in copies[:6]:
        copy.wait()
    for b in range(B):
        slots = []
        for k in range(27):
            brick = near[b, k]
            away = lax.shift_right_arithmetic(brick, 2) - place
            slot = jnp.bitwise_and(brick, 3)
            at = jnp.where(away == 0, slot, 14)
            at = jnp.where(away == -DEVS, 4 + slot, at)
            at = jnp.where(away == DEVS, 8 + slot, at)
            at = jnp.where(away == -1, 12, at)
            at = jnp.where(away == 1, 13, at)
            slots.append(jnp.where(brick < 0, 14, at))
        for plane in range(6):
            kz, z = ((0, 3), (1, 0), (1, 1), (1, 2), (1, 3), (2, 0))[plane]
            for q in range(9):
                block[plane, q * 16 : (q + 1) * 16] = bricks[slots[q * 3 + kz], z]
        for plane in range(6):
            moved = dot(window, block[plane]).astype(BF16)
            for s in range(9):
                row = ((s * 6 + plane) * B + b) * 16
                taps[row : row + 16] = moved[s * 16 : (s + 1) * 16]
    leave = [pltpu.make_async_copy(taps, taps_out, sems.at[9])]
    leave[0].start()
    for copy in copies[6:]:
        copy.wait()
    count = counts[place]
    merged = lax.dot_general(
        fine[...], weight[...], (((1,), (1,)), ((), ())), preferred_element_type=F32
    )
    brick_of = lax.broadcasted_iota(jnp.int32, (256, C), 0) // 64
    merged = jnp.where(brick_of < count, merged, 0.0).astype(BF16)
    merged = jnp.transpose(dot(row_order(False), merged)).astype(BF16)
    for tap in range(27):
        row = tap_rows(tap)
        term = dot(merged, taps[row : row + 256])
        at = tap * C
        end = at + C
        while at < end:
            owner = at // ROWS
            stop = min(end, (owner + 1) * ROWS)
            to = (owner // 2) * ROWS + at % ROWS
            total[owner % 2, :, to : to + stop - at] = term[:, at - tap * C : stop - tap * C]
            at = stop
    for i, (held, out, half) in enumerate(((send, send_out, 1 - core), (keep, keep_out, core))):
        for slab in range(SLABS):
            held[slab] = total[half, slab * COLS : (slab + 1) * COLS].astype(BF16)
        leave.append(pltpu.make_async_copy(held, out, sems.at[10 + i]))
        leave[-1].start()
    for copy in leave:
        copy.wait()


def back_kernel(
    counts_in, fine_in, taps_in, mine, other, gm, term, counts, fine, taps, sems, both, whole,
):
    place = my_place()
    core = jnp.bitwise_and(place, 1)
    copies = fetch(
        sems, (mine, both.at[core]), (other, both.at[1 - core]), (taps_in, taps),
        (fine_in, fine), (counts_in, counts),
    )
    for copy in copies[:2]:
        copy.wait()
    row = iota(16, 128, 0)
    held = None
    for owner in range(DEVS):
        first = ROWS * owner // 16 * 16
        shift = owner % 16
        tiles = [both[owner % 2, i, owner // 2] for i in range(SLABS)]
        for i in range(1, 5):
            whole[first + i * 16 : first + (i + 1) * 16, :128] = tiles[i]
            half = i % 2 * 64
            whole[first + i * 16 : first + (i + 1) * 16, 128:] = tiles[5 + i // 2][
                :, half : half + 64
            ]
        main, tail = tiles[0].astype(F32), tiles[5][:, :64].astype(F32)
        extra = tiles[7][:, 64:].astype(F32)
        long = jnp.concatenate([extra[0:1], extra[1:2]], axis=1)
        ends = [jnp.where(row < shift, main, jnp.where(row == shift, long, 0.0))]
        short = row[:, :64]
        ends.append(jnp.where(short < shift, tail, jnp.where(short == shift, extra[2:3], 0.0)))
        if shift:
            main = jnp.where(row >= shift, main, held[0])
            tail = jnp.where(short >= shift, tail, held[1])
        whole[first : first + 16, :128] = main.astype(BF16)
        whole[first : first + 16, 128:] = tail.astype(BF16)
        if shift == 15:
            whole[first + 80 : first + 96, :128] = ends[0].astype(BF16)
            whole[first + 80 : first + 96, 128:] = ends[1].astype(BF16)
        held = ends
    for copy in copies[2:]:
        copy.wait()
    back = jnp.zeros((256, C), F32)
    for tap in range(27):
        row = tap_rows(tap)
        back = back + dot(taps[row : row + 256], whole[tap * C : (tap + 1) * C])
    brick_of = lax.broadcasted_iota(jnp.int32, (256, C), 0) // 16 % B
    count = counts[place]
    back = jnp.where(brick_of < count, back, 0.0).astype(BF16)
    back = dot(row_order(True), back)
    gm[...] = back.astype(BF16)
    result = dot(jnp.transpose(back).astype(BF16), fine[...])
    for i in range(PIECES):
        piece = result[i % 8 * 24 : i % 8 * 24 + 24, i // 8 * 128 : i // 8 * 128 + 128]
        term[i // 24, i % 24] = piece.astype(BF16)


def fine_kernel(gm_in, weight_in, fine_out, gm, weight, fine_grad, sems):
    for copy in fetch(sems, (gm_in, gm), (weight_in, weight)):
        copy.wait()
    fine_grad[...] = dot(gm[...], weight[...]).astype(BF16)
    for copy in fetch(sems.at[2:], (fine_grad, fine_out)):
        copy.wait()


def join_kernel(parts, out):
    core = lax.axis_index("c")
    for i in range(24):
        out[i] = (parts[0, core, i].astype(F32) + parts[1, core, i].astype(F32)).astype(BF16)
    for i in range(24, 32):
        out[i] = jnp.zeros((24, 128), BF16)


def spread_kernel(parts, keep, received, out):
    merge = parts[0].astype(F32)
    for i in range(1, 32):
        merge = merge + parts[i].astype(F32)
    for i in range(SLABS):
        out[i, :, :HALF] = (keep[i].astype(F32) + received[i].astype(F32)).astype(BF16)
        out[i, :, HALF:WIDE] = jnp.zeros((COLS, WIDE - HALF), BF16)
        out[i, :, WIDE:] = merge.astype(BF16)


def both_kernel(parts, out):
    total = parts[0].astype(F32)
    for i in range(1, SLABS):
        total = total + parts[i].astype(F32)
    merge = total[:, WIDE:].astype(BF16)
    pad = jnp.zeros((COLS, 128 - ROWS), BF16)
    for i in range(32):
        piece = total[:, i * ROWS : (i + 1) * ROWS].astype(BF16)
        out[i, 0] = jnp.concatenate([piece, pad], axis=1)
        out[i, 1] = merge


def last_kernel(parts, merge_out, conv_out, merge, conv, sems):
    core = jnp.bitwise_and(my_place(), 1)
    for i in range(PIECES):
        row, col = i % 8 * 24, i // 8 * 128
        merge[row : row + 24, col : col + 128] = parts[i // 24, i % 24, 1].astype(F32)
    copies = fetch(sems, (merge, merge_out))
    total = parts[core, 0, 0].astype(F32)
    for i in range(1, 32):
        total = total + parts[core, i, 0].astype(F32)
    conv[...] = total[:, :ROWS]
    copies += fetch(sems.at[1:], (conv, conv_out))
    for copy in copies:
        copy.wait()


def call(kernel, outs, specs, scratch=(), flops=0, out_spec=None, vmem=20):
    return pl.pallas_call(
        kernel,
        out_shape=outs,
        in_specs=specs,
        out_specs=out_spec or jax.tree.map(lambda _: VMEM, outs),
        scratch_shapes=scratch,
        cost_estimate=pl.CostEstimate(flops=flops, bytes_accessed=0, transcendentals=0),
        compiler_params=pltpu.CompilerParams(vmem_limit_bytes=vmem << 20),
    )


def shape(*dims, dtype=BF16):
    return jax.ShapeDtypeStruct(dims, dtype)


def swap(x, axes):
    return lax.all_to_all(x, axes, 0, 0, tiled=True)


def local(
    fine_input, merge_weight, conv_weight, pre_act, norm_gain, norm_bias, cotangent, counts, neighbours
):
    counts_scratch = pltpu.SMEM((SLABS * DEVS,), jnp.int32)
    grad, near, far, frames = call(
        prepare_kernel,
        (shape(B, 4, 16, C), shape(1, 4, 16, C), shape(1, 4, 16, C), shape(32, 16, 128)),
        [HBM] * 6,
        [
            counts_scratch,
            pltpu.VMEM((B, 16, 4 * C), BF16),
            pltpu.VMEM((B, 16, 4 * C), BF16),
            pltpu.VMEM((1, C), F32),
            pltpu.VMEM((1, C), F32),
            pltpu.VMEM((ROWS, C), BF16),
            pltpu.VMEM((SLABS, 16, 128), BF16),
            pltpu.SemaphoreType.DMA((6,)),
        ],
        vmem=60,
    )(counts, pre_act, cotangent, norm_gain.reshape(1, C), norm_bias.reshape(1, C), conv_weight)

    def shifted(x, axes, count, step):
        pairs = [(i, i + step) for i in range(count) if 0 <= i + step < count]
        return lax.ppermute(x, axes, pairs)

    def flipped(x):
        return lax.ppermute(x, "c", [(0, 1), (1, 0)])

    slab_low = shifted(grad, SLAB, SLABS, 1)
    slab_high = shifted(grad, SLAB, SLABS, -1)
    frames = swap(frames, ("zh", "y"))
    dev_near = flipped(near)
    ups = [(i, i + 1) for i in range(1, DEVS - 1, 2)]
    dev_far = lax.ppermute(far, DEV, ups + [(j, i) for i, j in ups])
    frames, slab_low, slab_high, dev_near, dev_far = lax.optimization_barrier(
        (frames, slab_low, slab_high, dev_near, dev_far)
    )
    frames = call(repeat_kernel, shape(SLABS, 32, 16, 128), [VMEM])(frames)
    frames = swap(frames, SLAB)

    fine_scratch = pltpu.VMEM((256, 768), BF16)
    weight_scratch = pltpu.VMEM((C, 768), BF16)
    merge_weight = merge_weight.T
    keep, send, taps = call(
        conv_kernel,
        (shape(SLABS, COLS, HALF), shape(SLABS, COLS, HALF), shape(3456, C)),
        [HBM] * 9,
        [
            counts_scratch,
            pltpu.SMEM((B, 27), jnp.int32),
            fine_scratch,
            weight_scratch,
            pltpu.SemaphoreType.DMA((12,)),
            pltpu.VMEM((15, 4, 16, C), BF16),
            pltpu.VMEM((6, 144, C), BF16),
            pltpu.VMEM((2, C, HALF), F32),
            pltpu.VMEM((3456, C), BF16),
            pltpu.VMEM((SLABS, COLS, HALF), BF16),
            pltpu.VMEM((SLABS, COLS, HALF), BF16),
        ],
        flops=6 * 10**9,
        out_spec=(HBM, HBM, HBM),
        vmem=60,
    )(
        counts, neighbours, fine_input, merge_weight, grad, slab_low, slab_high, dev_near, dev_far
    )

    frames, taps = lax.optimization_barrier((frames, taps))
    other = flipped(frames)
    gm, term = call(
        back_kernel,
        (shape(256, C), shape(2, 24, 24, 128)),
        [HBM] * 5,
        [
            counts_scratch,
            fine_scratch,
            pltpu.VMEM((3456, C), BF16),
            pltpu.SemaphoreType.DMA((5,)),
            pltpu.VMEM((2, SLABS, 32, 16, 128), BF16),
            pltpu.VMEM((27 * C, C), BF16),
        ],
        flops=4 * 10**9,
        vmem=60,
    )(counts, fine_input, taps, frames, other)
    fine_grad = call(
        fine_kernel,
        shape(256, 768),
        [HBM] * 2,
        [
            pltpu.VMEM((256, C), BF16),
            weight_scratch,
            fine_scratch,
            pltpu.SemaphoreType.DMA((3,)),
        ],
        flops=10**9,
        out_spec=HBM,
    )(gm, merge_weight)

    term = lax.all_gather(term, "c", axis=0, tiled=False)
    term = call(join_kernel, shape(32, 24, 128), [VMEM])(term)
    term = swap(term, ("zh", "y"))
    term = call(spread_kernel, shape(SLABS, COLS, WIDE + 128), [VMEM] * 3)(
        term, keep, flipped(send)
    )
    term = swap(term, SLAB)
    term = call(both_kernel, shape(32, 2, 24, 128), [VMEM])(term)
    term = swap(term, ("zh", "y"))
    term = lax.all_gather(term, "c", axis=0, tiled=False)
    merge_grad, conv_grad = call(
        last_kernel,
        (shape(C, 768, dtype=F32), shape(COLS, ROWS, dtype=F32)),
        [VMEM],
        [
            pltpu.VMEM((C, 768), F32),
            pltpu.VMEM((COLS, ROWS), F32),
            pltpu.SemaphoreType.DMA((2,)),
        ],
        out_spec=(HBM, HBM),
    )(term)
    return fine_grad, merge_grad.T, conv_grad.T


def solution(mesh):
    fine_mesh = Mesh(mesh.devices.reshape(SIZES), AXES)
    every = SLAB + DEV
    in_specs = (
        P(every, None),
        P(),
        P(DEV, None),
        P(every, None, None),
        P(),
        P(),
        P(every, None, None),
        P(),
        P(every, None),
    )
    out_specs = (P(every, None), P(), P(DEV, SLAB))
    return jax.shard_map(
        local, mesh=fine_mesh, in_specs=in_specs, out_specs=out_specs, check_vma=False
    )
```

```python
import jax
import jax.numpy as jnp
from jax import lax
from jax.experimental import pallas as pl
from jax.experimental.pallas import tpu as pltpu
from jax.sharding import Mesh, PartitionSpec as P

F32 = jnp.float32
BF16 = jnp.bfloat16

AXES = ("zl", "x", "zh", "y", "c")
SIZES = (2, 4, 4, 8, 2)
SLAB = ("zl", "x")
DEV = ("zh", "y", "c")
SLABS = 8
DEVS = 64
B = 4
C = 192
ROWS = 81
FRAME = 80
HALF = 32 * ROWS
COLS = C // SLABS
PIECES = 48
WIDE = 2688

VMEM = pl.BlockSpec(memory_space=pltpu.VMEM)
HBM = pl.BlockSpec(memory_space=pltpu.HBM)


def dot(a, b):
    return jnp.dot(a, b, preferred_element_type=F32)


def my_place():
    place = lax.axis_index(AXES[0])
    for axis, size in zip(AXES[1:], SIZES[1:]):
        place = place * size + lax.axis_index(axis)
    return place


def repeat_kernel(block, out):
    for i in range(out.shape[0]):
        out[i] = block[...]


def iota(rows, cols, dim):
    return lax.broadcasted_iota(jnp.int32, (rows, cols), dim)


def ones_where(condition):
    return jnp.where(condition, 1.0, 0.0).astype(BF16)


def place_in_nine(start, v):
    p = start + v
    brick = jnp.where(p == 0, 0, jnp.where(p == 5, 2, 1))
    return brick, jnp.where(p == 0, 3, jnp.where(p == 5, 0, p - 1))


def window_matrix():
    row, col = iota(144, 144, 0), iota(144, 144, 1)
    s = lax.shift_right_logical(row, 4)
    sx = jnp.where(s >= 6, 2, jnp.where(s >= 3, 1, 0))
    v = jnp.bitwise_and(row, 15)
    kx, x = place_in_nine(sx, lax.shift_right_logical(v, 2))
    ky, y = place_in_nine(s - 3 * sx, jnp.bitwise_and(v, 3))
    return ones_where(col == (kx * 3 + ky) * 16 + x * 4 + y)


def row_order(inverse):
    inner, outer = iota(256, 256, int(inverse)), iota(256, 256, int(not inverse))
    return ones_where(
        outer == jnp.bitwise_and(inner, 63) * 4 + lax.shift_right_logical(inner, 6)
    )


def fetch(sems, *pairs):
    copies = [pltpu.make_async_copy(src, dst, sems.at[i]) for i, (src, dst) in enumerate(pairs)]
    for copy in copies:
        copy.start()
    return copies


def tap_rows(tap):
    window = (2 - tap // 9) * 3 + 2 - tap // 3 % 3
    return (window * 6 + 2 - tap % 3) * 64


def prepare_kernel(
    counts_in, pre_in, cot_in, gain_in, bias_in, weight_in, grad, near, far, frames,
    counts, pre, cot, gain, bias, weight, tiles, sems,
):
    copies = fetch(
        sems, (counts_in, counts), (pre_in, pre), (cot_in, cot), (gain_in, gain), (bias_in, bias),
        (weight_in, weight),
    )
    place = my_place()
    copies[5].wait()
    shift = jnp.bitwise_and(place, 15)
    at = iota(FRAME, ROWS, 1) + shift
    turned = jnp.where(at >= FRAME, at - FRAME, at)
    spread = ones_where((iota(FRAME, ROWS, 0) == turned) & (iota(FRAME, ROWS, 1) < FRAME))
    turned = dot(spread, weight[...])
    for i in range(5):
        tiles[i] = turned[i * 16 : (i + 1) * 16, :128].astype(BF16)
    extra = dot(ones_where(iota(16, ROWS, 1) == ROWS - 1), weight[...])
    row = iota(16, 64, 0)
    extra = jnp.where(
        row == 0, extra[:, :64], jnp.where(row == 1, extra[:, 64:128], extra[:, 128:])
    )
    tails = [turned[i * 16 : (i + 1) * 16, 128:] for i in range(5)] + [extra]
    for i in range(3):
        pair = jnp.concatenate([tails[2 * i], tails[2 * i + 1]], axis=1)
        tiles[5 + i] = pair.astype(BF16)
    mine = tiles[lax.shift_right_logical(place, 6)]
    for i in range(32):
        frames[i] = mine
    for copy in copies[:5]:
        copy.wait()
    count = counts[place]
    g = gain[...]
    for b in range(B):
        p = pre[b].astype(F32)
        u = cot[b].astype(F32)
        for z in range(4):
            pz = p[:, z * C : (z + 1) * C]
            uz = u[:, z * C : (z + 1) * C]
            gate = (g * pz + bias[...] > 0) & (b < count)
            grad[b, z] = jnp.where(gate, uz * g, 0.0).astype(BF16)
    core = jnp.bitwise_and(place, 1)
    near[0] = grad[jnp.where(core == 0, count - 1, 0)]
    far[0] = grad[jnp.where(core == 0, 0, count - 1)]


def merged_kernel(counts_in, fine_in, weight_in, out, counts, fine, weight, sems):
    copies = fetch(sems, (counts_in, counts), (fine_in, fine), (weight_in, weight))
    place = my_place()
    for copy in copies:
        copy.wait()
    count = counts[place]
    merged = lax.dot_general(
        fine[...], weight[...], (((1,), (1,)), ((), ())), preferred_element_type=F32
    )
    brick_of = lax.broadcasted_iota(jnp.int32, (256, C), 0) // 64
    merged = jnp.where(brick_of < count, merged, 0.0).astype(BF16)
    out[...] = jnp.transpose(dot(row_order(False), merged)).astype(BF16)


def conv_kernel(
    near_in, merged_in, grad, slab_low, slab_high, dev_near, dev_far,
    keep_out, send_out, taps_out, near, merged, sems, bricks, block, total, taps, keep, send,
):
    place = my_place()
    core = jnp.bitwise_and(place, 1)
    copies = fetch(
        sems, (near_in, near), (grad, bricks.at[0:4]), (slab_low, bricks.at[4:8]),
        (slab_high, bricks.at[8:12]), (dev_near, bricks.at[pl.ds(13 - core, 1)]),
        (dev_far, bricks.at[pl.ds(12 + core, 1)]),
        (merged_in, merged),
    )
    bricks[14:15] = jnp.zeros((1, 4, 16, C), BF16)
    window = window_matrix()
    for copy in copies[:6]:
        copy.wait()
    for b in range(B):
        slots = []
        for k in range(27):
            brick = near[b, k]
            away = lax.shift_right_arithmetic(brick, 2) - place
            slot = jnp.bitwise_and(brick, 3)
            at = jnp.where(away == 0, slot, 14)
            at = jnp.where(away == -DEVS, 4 + slot, at)
            at = jnp.where(away == DEVS, 8 + slot, at)
            at = jnp.where(away == -1, 12, at)
            at = jnp.where(away == 1, 13, at)
            slots.append(jnp.where(brick < 0, 14, at))
        for plane in range(6):
            kz, z = ((0, 3), (1, 0), (1, 1), (1, 2), (1, 3), (2, 0))[plane]
            for q in range(9):
                block[plane, q * 16 : (q + 1) * 16] = bricks[slots[q * 3 + kz], z]
        for plane in range(6):
            moved = dot(window, block[plane]).astype(BF16)
            for s in range(9):
                row = ((s * 6 + plane) * B + b) * 16
                taps[row : row + 16] = moved[s * 16 : (s + 1) * 16]
    leave = [pltpu.make_async_copy(taps, taps_out, sems.at[9])]
    leave[0].start()
    for copy in copies[6:]:
        copy.wait()
    for tap in range(27):
        row = tap_rows(tap)
        term = dot(merged[...], taps[row : row + 256])
        at = tap * C
        end = at + C
        while at < end:
            owner = at // ROWS
            stop = min(end, (owner + 1) * ROWS)
            to = (owner // 2) * ROWS + at % ROWS
            total[owner % 2, :, to : to + stop - at] = term[:, at - tap * C : stop - tap * C]
            at = stop
    for i, (held, out, half) in enumerate(((send, send_out, 1 - core), (keep, keep_out, core))):
        for slab in range(SLABS):
            held[slab] = total[half, slab * COLS : (slab + 1) * COLS].astype(BF16)
        leave.append(pltpu.make_async_copy(held, out, sems.at[10 + i]))
        leave[-1].start()
    for copy in leave:
        copy.wait()


def back_kernel(
    counts_in, fine_in, taps_in, mine, other, gm, term, counts, fine, taps, sems, both, whole,
):
    place = my_place()
    core = jnp.bitwise_and(place, 1)
    copies = fetch(
        sems, (mine, both.at[core]), (other, both.at[1 - core]), (taps_in, taps),
        (fine_in, fine), (counts_in, counts),
    )
    for copy in copies[:2]:
        copy.wait()
    row = iota(16, 128, 0)
    held = None
    for owner in range(DEVS):
        first = ROWS * owner // 16 * 16
        shift = owner % 16
        tiles = [both[owner % 2, i, owner // 2] for i in range(SLABS)]
        for i in range(1, 5):
            whole[first + i * 16 : first + (i + 1) * 16, :128] = tiles[i]
            half = i % 2 * 64
            whole[first + i * 16 : first + (i + 1) * 16, 128:] = tiles[5 + i // 2][
                :, half : half + 64
            ]
        main, tail = tiles[0].astype(F32), tiles[5][:, :64].astype(F32)
        extra = tiles[7][:, 64:].astype(F32)
        long = jnp.concatenate([extra[0:1], extra[1:2]], axis=1)
        ends = [jnp.where(row < shift, main, jnp.where(row == shift, long, 0.0))]
        short = row[:, :64]
        ends.append(jnp.where(short < shift, tail, jnp.where(short == shift, extra[2:3], 0.0)))
        if shift:
            main = jnp.where(row >= shift, main, held[0])
            tail = jnp.where(short >= shift, tail, held[1])
        whole[first : first + 16, :128] = main.astype(BF16)
        whole[first : first + 16, 128:] = tail.astype(BF16)
        if shift == 15:
            whole[first + 80 : first + 96, :128] = ends[0].astype(BF16)
            whole[first + 80 : first + 96, 128:] = ends[1].astype(BF16)
        held = ends
    for copy in copies[2:]:
        copy.wait()
    back = jnp.zeros((256, C), F32)
    for tap in range(27):
        row = tap_rows(tap)
        back = back + dot(taps[row : row + 256], whole[tap * C : (tap + 1) * C])
    brick_of = lax.broadcasted_iota(jnp.int32, (256, C), 0) // 16 % B
    count = counts[place]
    back = jnp.where(brick_of < count, back, 0.0).astype(BF16)
    back = dot(row_order(True), back)
    gm[...] = back.astype(BF16)
    result = dot(jnp.transpose(back).astype(BF16), fine[...])
    for i in range(PIECES):
        piece = result[i % 8 * 24 : i % 8 * 24 + 24, i // 8 * 128 : i // 8 * 128 + 128]
        term[i // 24, i % 24] = piece.astype(BF16)


def fine_kernel(gm_in, weight_in, fine_out, gm, weight, fine_grad, sems):
    for copy in fetch(sems, (gm_in, gm), (weight_in, weight)):
        copy.wait()
    fine_grad[...] = dot(gm[...], weight[...]).astype(BF16)
    for copy in fetch(sems.at[2:], (fine_grad, fine_out)):
        copy.wait()


def join_kernel(parts, out):
    core = lax.axis_index("c")
    for i in range(24):
        out[i] = (parts[0, core, i].astype(F32) + parts[1, core, i].astype(F32)).astype(BF16)
    for i in range(24, 32):
        out[i] = jnp.zeros((24, 128), BF16)


def spread_kernel(parts, keep, received, out):
    merge = parts[0].astype(F32)
    for i in range(1, 32):
        merge = merge + parts[i].astype(F32)
    for i in range(SLABS):
        out[i, :, :HALF] = (keep[i].astype(F32) + received[i].astype(F32)).astype(BF16)
        out[i, :, HALF:WIDE] = jnp.zeros((COLS, WIDE - HALF), BF16)
        out[i, :, WIDE:] = merge.astype(BF16)


def both_kernel(parts, out):
    total = parts[0].astype(F32)
    for i in range(1, SLABS):
        total = total + parts[i].astype(F32)
    merge = total[:, WIDE:].astype(BF16)
    pad = jnp.zeros((COLS, 128 - ROWS), BF16)
    for i in range(32):
        piece = total[:, i * ROWS : (i + 1) * ROWS].astype(BF16)
        out[i, 0] = jnp.concatenate([piece, pad], axis=1)
        out[i, 1] = merge


def last_kernel(parts, merge_out, conv_out, merge, conv, sems):
    core = jnp.bitwise_and(my_place(), 1)
    for i in range(PIECES):
        row, col = i % 8 * 24, i // 8 * 128
        merge[row : row + 24, col : col + 128] = parts[i // 24, i % 24, 1].astype(F32)
    copies = fetch(sems, (merge, merge_out))
    total = parts[core, 0, 0].astype(F32)
    for i in range(1, 32):
        total = total + parts[core, i, 0].astype(F32)
    conv[...] = total[:, :ROWS]
    copies += fetch(sems.at[1:], (conv, conv_out))
    for copy in copies:
        copy.wait()


def call(kernel, outs, specs, scratch=(), flops=0, out_spec=None, vmem=20):
    return pl.pallas_call(
        kernel,
        out_shape=outs,
        in_specs=specs,
        out_specs=out_spec or jax.tree.map(lambda _: VMEM, outs),
        scratch_shapes=scratch,
        cost_estimate=pl.CostEstimate(flops=flops, bytes_accessed=0, transcendentals=0),
        compiler_params=pltpu.CompilerParams(vmem_limit_bytes=vmem << 20),
    )


def shape(*dims, dtype=BF16):
    return jax.ShapeDtypeStruct(dims, dtype)


def swap(x, axes):
    return lax.all_to_all(x, axes, 0, 0, tiled=True)


def local(
    fine_input, merge_weight, conv_weight, pre_act, norm_gain, norm_bias, cotangent, counts, neighbours
):
    counts_scratch = pltpu.SMEM((SLABS * DEVS,), jnp.int32)
    grad, near, far, frames = call(
        prepare_kernel,
        (shape(B, 4, 16, C), shape(1, 4, 16, C), shape(1, 4, 16, C), shape(32, 16, 128)),
        [HBM] * 6,
        [
            counts_scratch,
            pltpu.VMEM((B, 16, 4 * C), BF16),
            pltpu.VMEM((B, 16, 4 * C), BF16),
            pltpu.VMEM((1, C), F32),
            pltpu.VMEM((1, C), F32),
            pltpu.VMEM((ROWS, C), BF16),
            pltpu.VMEM((SLABS, 16, 128), BF16),
            pltpu.SemaphoreType.DMA((6,)),
        ],
        vmem=60,
    )(counts, pre_act, cotangent, norm_gain.reshape(1, C), norm_bias.reshape(1, C), conv_weight)

    def shifted(x, axes, count, step):
        pairs = [(i, i + step) for i in range(count) if 0 <= i + step < count]
        return lax.ppermute(x, axes, pairs)

    def flipped(x):
        return lax.ppermute(x, "c", [(0, 1), (1, 0)])

    slab_low = shifted(grad, SLAB, SLABS, 1)
    slab_high = shifted(grad, SLAB, SLABS, -1)
    frames = swap(frames, ("zh", "y"))
    dev_near = flipped(near)
    frames, slab_low, slab_high, dev_near, far = lax.optimization_barrier(
        (frames, slab_low, slab_high, dev_near, far)
    )
    ups = [(i, i + 1) for i in range(1, DEVS - 1, 2)]
    dev_far = lax.ppermute(far, DEV, ups + [(j, i) for i, j in ups])
    frames = call(repeat_kernel, shape(SLABS, 32, 16, 128), [VMEM])(frames)
    frames = swap(frames, SLAB)

    fine_scratch = pltpu.VMEM((256, 768), BF16)
    weight_scratch = pltpu.VMEM((C, 768), BF16)
    merge_weight = merge_weight.T
    merged = call(
        merged_kernel,
        shape(C, 256),
        [HBM] * 3,
        [counts_scratch, fine_scratch, weight_scratch, pltpu.SemaphoreType.DMA((3,))],
        flops=10**9,
        vmem=60,
    )(counts, fine_input, merge_weight)
    keep, send, taps = call(
        conv_kernel,
        (shape(SLABS, COLS, HALF), shape(SLABS, COLS, HALF), shape(3456, C)),
        [HBM] * 7,
        [
            pltpu.SMEM((B, 27), jnp.int32),
            pltpu.VMEM((C, 256), BF16),
            pltpu.SemaphoreType.DMA((12,)),
            pltpu.VMEM((15, 4, 16, C), BF16),
            pltpu.VMEM((6, 144, C), BF16),
            pltpu.VMEM((2, C, HALF), F32),
            pltpu.VMEM((3456, C), BF16),
            pltpu.VMEM((SLABS, COLS, HALF), BF16),
            pltpu.VMEM((SLABS, COLS, HALF), BF16),
        ],
        flops=6 * 10**9,
        out_spec=(HBM, HBM, HBM),
        vmem=60,
    )(
        neighbours, merged, grad, slab_low, slab_high, dev_near, dev_far
    )

    frames, taps = lax.optimization_barrier((frames, taps))
    other = flipped(frames)
    gm, term = call(
        back_kernel,
        (shape(256, C), shape(2, 24, 24, 128)),
        [HBM] * 5,
        [
            counts_scratch,
            fine_scratch,
            pltpu.VMEM((3456, C), BF16),
            pltpu.SemaphoreType.DMA((5,)),
            pltpu.VMEM((2, SLABS, 32, 16, 128), BF16),
            pltpu.VMEM((27 * C, C), BF16),
        ],
        flops=4 * 10**9,
        vmem=60,
    )(counts, fine_input, taps, frames, other)
    fine_grad = call(
        fine_kernel,
        shape(256, 768),
        [HBM] * 2,
        [
            pltpu.VMEM((256, C), BF16),
            weight_scratch,
            fine_scratch,
            pltpu.SemaphoreType.DMA((3,)),
        ],
        flops=10**9,
        out_spec=HBM,
    )(gm, merge_weight)

    term = lax.all_gather(term, "c", axis=0, tiled=False)
    term = call(join_kernel, shape(32, 24, 128), [VMEM])(term)
    term = swap(term, ("zh", "y"))
    term = call(spread_kernel, shape(SLABS, COLS, WIDE + 128), [VMEM] * 3)(
        term, keep, flipped(send)
    )
    term = swap(term, SLAB)
    term = call(both_kernel, shape(32, 2, 24, 128), [VMEM])(term)
    term = swap(term, ("zh", "y"))
    term = lax.all_gather(term, "c", axis=0, tiled=False)
    merge_grad, conv_grad = call(
        last_kernel,
        (shape(C, 768, dtype=F32), shape(COLS, ROWS, dtype=F32)),
        [VMEM],
        [
            pltpu.VMEM((C, 768), F32),
            pltpu.VMEM((COLS, ROWS), F32),
            pltpu.SemaphoreType.DMA((2,)),
        ],
        out_spec=(HBM, HBM),
    )(term)
    return fine_grad, merge_grad.T, conv_grad.T


def solution(mesh):
    fine_mesh = Mesh(mesh.devices.reshape(SIZES), AXES)
    every = SLAB + DEV
    in_specs = (
        P(every, None),
        P(),
        P(DEV, None),
        P(every, None, None),
        P(),
        P(),
        P(every, None, None),
        P(),
        P(every, None),
    )
    out_specs = (P(every, None), P(), P(DEV, SLAB))
    return jax.shard_map(
        local, mesh=fine_mesh, in_specs=in_specs, out_specs=out_specs, check_vma=False
    )
```
